32 devices in a mesh: ctx: 4 (over x, core), ep: 8 (over z, y).
Axes of the slice: x: 2, y: 2, z: 4, core: 2. Of those that a mesh axis runs over, the one named last changes fastest.
Arguments:
- layer_input: bfloat16 [8, 1024, 2048], P('ep', 'ctx'), may hold values from -6 to 6
- attn_gain: float32 [2048], replicated, may hold values from 0.1 to 1.9
- q_weight: bfloat16 [2048, 4096], P('ep'), may hold values from -0.125 to 0.125
- key_matrix: bfloat16 [2048, 512], P('ep'), may hold values from -0.125 to 0.125
- value_matrix: bfloat16 [2048, 512], P('ep'), may hold values from -0.125 to 0.125
- o_weight: bfloat16 [4096, 2048], P('ep'), may hold values from -1 to 1
- q_gain: float32 [128], replicated, may hold values from 0.1 to 1.9
- key_norm_gain: float32 [128], replicated, may hold values from 0.1 to 1.9
- ffn_gain: float32 [2048], replicated, may hold values from 0.1 to 1.9
- router_weight: bfloat16 [2048, 32], P('ep'), may hold values from -0.0625 to 0.0625
- gate_weight: bfloat16 [32, 2048, 768], P(('ctx', 'ep')), may hold values from -0.125 to 0.125
- up_weight: bfloat16 [32, 2048, 768], P(('ctx', 'ep')), may hold values from -0.125 to 0.125
- down_weight: bfloat16 [32, 768, 2048], P(('ctx', 'ep')), may hold values from -0.875 to 0.875
- routes: int32 [8, 1024, 8], P('ep', 'ctx'), may hold values from 0 to 31, all different within a row; in each aligned block of 256 rows (0 to 255, 256 to 511, ..., all dimensions but the last counted through in order) at most 80 rows name the same one
- out_grad: bfloat16 [8, 1024, 2048], P('ep', 'ctx'), may hold values from -6 to 6
Outputs:
- layer_output: bfloat16 [8, 1024, 2048], P('ep', 'ctx')
- input_grad: float32 [8, 1024, 2048], P('ep', 'ctx')
- attn_gain_grad: float32 [2048], replicated
- q_weight_grad: float32 [2048, 4096], P(('ctx', 'ep'))
- k_weight_grad: float32 [2048, 512], P(('ctx', 'ep'))
- v_weight_grad: float32 [2048, 512], P(('ctx', 'ep'))
- o_weight_grad: float32 [4096, 2048], P(('ctx', 'ep'))
- q_gain_grad: float32 [128], replicated
- k_gain_grad: float32 [128], replicated
- ffn_gain_grad: float32 [2048], replicated
- router_weight_grad: float32 [2048, 32], P(('ctx', 'ep'))
- gate_weight_grad: float32 [32, 2048, 768], P(('ctx', 'ep'))
- up_weight_grad: float32 [32, 2048, 768], P(('ctx', 'ep'))
- down_weight_grad: float32 [32, 768, 2048], P(('ctx', 'ep'))
The draws below stay inside these ranges and needn't reach their ends.
Inputs may be any that keep to these rules, and one draw needn't show every extreme that they name: `routes`: each token names 8 different experts. Among the 256 tokens of one device (one block of 256 positions of one sequence) no expert is named more than 80 times, a bound that some block reaches in some such blocks.
All inputs are finite; a program needn't handle non-finite values.
Results may differ from the reference program's by a relative error of at most 0.02.
Values may be sent and summed in bfloat16 or wider, within the bound.
No kernel may reach another device: no remote copies, remote signals or barrier semaphores. Data moves between devices by JAX's collectives and lax.ppermute only.
A program may use at most 384 MiB of HBM per device.

```python
import math
import jax
import jax.numpy as jnp
import numpy as np
from jax import lax

MODEL_DIM = 2048
QUERY_HEADS = 32
KEY_VALUE_HEADS = 4
HEAD_DIM = 128
FF = 768
TOP = 8
STRETCH = 256
LENGTH = 1024
SEQUENCES = 8
EXPERTS = 32
CAP = 80
N_CTX = 4
N_EP = 8
DEVICES = 32


def block_scale(rng, extent, split, least, top_value):
    def one(dim, parts):
        heights = jax.random.uniform(jax.random.fold_in(jax.random.fold_in(rng, 6), dim), (parts,), jnp.float32, least / len(split), top_value / len(split))
        return jnp.repeat(jnp.exp(heights), extent[dim] // parts).reshape((-1,) + (1,) * (len(extent) - dim - 1))

    level = one(*split[0])
    for cut in split[1:]:
        level = level * one(*cut)
    return level


def shared_out(rng, own, number, rows, amount, top, bound, skew):
    ranking = jax.random.permutation(rng, amount)
    crowded, usual = load_shares(amount, rows * top, bound, skew, True), load_shares(amount, rows * top, bound, skew, False)
    places = jnp.arange(amount)

    def named(sizes, rotation):
        used = int((sizes > 0).sum())
        fixed = max(1, used // 4)
        moved = fixed + (places - fixed + rotation * (used - fixed)) % max(1, amount - fixed)
        return jnp.zeros((amount,), jnp.int32).at[ranking[jnp.where(places < fixed, places, moved)]].set(jnp.asarray(sizes, jnp.int32))

    sizes = jnp.where(number % 4 == 0, named(crowded, number // 4), named(usual, number - number // 4 - 1))
    mixed = jax.random.permutation(jax.random.fold_in(own, 3), amount)
    giver, receiver = mixed[0:amount // 2 * 2:2], mixed[1:amount // 2 * 2:2]
    slack = jnp.minimum(sizes[giver] - 1, bound - sizes[receiver]) // 2
    slack = jnp.where((giver == ranking[0]) | (receiver == ranking[0]) | (sizes[receiver] == 0), 0, jnp.maximum(slack, 0))
    moved = jax.random.randint(jax.random.fold_in(own, 4), (amount // 2,), 0, 1 << 20) % (slack + 1)
    sizes = sizes.at[giver].add(-moved).at[receiver].add(moved)
    labels = jnp.searchsorted(jnp.cumsum(sizes), jnp.arange(rows * top), side="right").astype(jnp.int32)
    table = labels.reshape(top, rows).T
    table = table[jax.random.permutation(jax.random.fold_in(own, 1), rows)]
    rotation = jax.random.randint(jax.random.fold_in(own, 2), (rows, 1), 0, top)
    return jnp.take_along_axis(table, (jnp.arange(top)[None, :] + rotation) % top, axis=1)


def load_shares(number_of, total, most, slope, full):
    portions = [(1 << 20) // math.isqrt(standing ** slope) + 1 for standing in range(1, number_of + 1)]
    largest = most if full else min(most, max(-(-total // number_of), total * portions[0] // sum(portions)))
    least = 1 if total - largest >= number_of - 1 else 0
    holding, spare = [largest] + [least] * (number_of - 1), total - largest - least * (number_of - 1)
    while spare > 0:
        movable = [i for i in range(1, number_of) if holding[i] < largest] or [i for i in range(1, number_of) if holding[i] < most]
        pool, budget = sum([portions[i] for i in movable]), spare
        for i in movable:
            addition = min(most - holding[i], max(1, budget * portions[i] // pool), spare)
            holding[i] = holding[i] + addition
            spare = spare - addition
    return np.array(holding)


def centred(key, shape, deviation, bound, split=(), held_as=jnp.bfloat16):
    factor_of = block_scale(key, shape, split, -0.22, 0.18) if split else 1.0
    entries = jax.random.normal(key, shape, jnp.float32) * deviation * factor_of
    return jnp.minimum(jnp.maximum(entries, -bound), bound).astype(held_as)


def setup_inputs(seed: int = 0) -> dict:
    splits = jax.random.split(jax.random.key(seed), 16)
    layer_input = centred(splits[0], (SEQUENCES, LENGTH, MODEL_DIM), 1.0, 6.0, ((0, 8), (1, 4)))
    attn_gain = jnp.clip(1.0 + 0.18 * jax.random.normal(splits[1], (MODEL_DIM,), jnp.float32), 0.1, 1.9)
    q_weight = centred(splits[2], (MODEL_DIM, QUERY_HEADS * HEAD_DIM), MODEL_DIM ** -0.5, 0.125, ((0, 8),))
    key_matrix = centred(splits[3], (MODEL_DIM, KEY_VALUE_HEADS * HEAD_DIM), MODEL_DIM ** -0.5, 0.125, ((0, 8),))
    value_matrix = centred(splits[4], (MODEL_DIM, KEY_VALUE_HEADS * HEAD_DIM), MODEL_DIM ** -0.5, 0.125, ((0, 8),))
    o_weight = centred(splits[5], (QUERY_HEADS * HEAD_DIM, MODEL_DIM), (QUERY_HEADS * HEAD_DIM // 128) ** -0.5, 1.0, ((0, 8),))
    q_gain = jnp.clip(1.0 + 0.18 * jax.random.normal(splits[6], (HEAD_DIM,), jnp.float32), 0.1, 1.9)
    key_norm_gain = jnp.clip(1.0 + 0.18 * jax.random.normal(splits[7], (HEAD_DIM,), jnp.float32), 0.1, 1.9)
    ffn_gain = jnp.clip(1.0 + 0.18 * jax.random.normal(splits[8], (MODEL_DIM,), jnp.float32), 0.1, 1.9)
    router_weight = centred(splits[9], (MODEL_DIM, EXPERTS), (4 * MODEL_DIM) ** -0.5, 0.0625, ((0, 8),))
    gate_weight = centred(splits[10], (EXPERTS, MODEL_DIM, FF), MODEL_DIM ** -0.5, 0.125, ((0, 32),))
    up_weight = centred(splits[11], (EXPERTS, MODEL_DIM, FF), MODEL_DIM ** -0.5, 0.125, ((0, 32),))
    down_weight = centred(splits[12], (EXPERTS, FF, MODEL_DIM), (FF // 16) ** -0.5, 0.875, ((0, 32),))
    routes_keys = jax.random.split(jax.random.fold_in(splits[13], 1), SEQUENCES * LENGTH // STRETCH)
    routes_turns = jax.random.permutation(jax.random.fold_in(splits[13], 3), SEQUENCES * LENGTH // STRETCH)
    routes = jax.vmap(lambda own, number: shared_out(jax.random.fold_in(splits[13], 2), own, number, STRETCH, EXPERTS, TOP, CAP, 1))(routes_keys, routes_turns).reshape((SEQUENCES, LENGTH, TOP))
    out_grad = centred(splits[14], (SEQUENCES, LENGTH, MODEL_DIM), 1.0, 6.0, ((0, 8), (1, 4)))
    return dict(layer_input=layer_input, attn_gain=attn_gain, q_weight=q_weight, key_matrix=key_matrix, value_matrix=value_matrix, o_weight=o_weight, q_gain=q_gain, key_norm_gain=key_norm_gain, ffn_gain=ffn_gain, router_weight=router_weight, gate_weight=gate_weight, up_weight=up_weight, down_weight=down_weight, routes=routes, out_grad=out_grad)


EPSILON = 1e-06
ROPE_BASE = 1000000.0
FULL_PRECISION = lax.Precision.HIGHEST

@jax.custom_vjp
def reduced_value(v):
    return lax.optimization_barrier(v.astype(jnp.bfloat16)).astype(jnp.float32)

@jax.custom_vjp
def reduced_backward(v):
    return v

def low_keep(v):
    return (reduced_value(v), None)

def low_pass(kept, grad):
    return (grad,)

def back_keep(v):
    return (v, None)

def back_low(kept, grad):
    return (reduced_value(grad),)
reduced_value.defvjp(low_keep, low_pass)
reduced_backward.defvjp(back_keep, back_low)

def norm_rows(value, gain):
    return value * lax.rsqrt(lax.optimization_barrier(jnp.mean(value * value, axis=-1, keepdims=True)) + EPSILON) * gain

def rotate(value, token_positions):
    half_width = value.shape[-1] // 2
    frequency = ROPE_BASE ** (-jnp.arange(half_width).astype(jnp.float32) * 2.0 / value.shape[-1])
    angles = token_positions[:, None] * frequency[None, :]
    cosine = jnp.cos(angles)[:, None, :]
    sine_part = jnp.sin(angles)[:, None, :]
    front_half = value[..., :half_width]
    back_half = value[..., half_width:]
    return jnp.concatenate([front_half * cosine - back_half * sine_part, back_half * cosine + front_half * sine_part], axis=-1)

def head_prepare(projected_rows, gain, token_positions, head_count):
    shaped = projected_rows.reshape(projected_rows.shape[0], head_count, -1)
    return rotate(norm_rows(shaped, gain), token_positions)

def soft_rows(value_rows):
    row_max = lax.optimization_barrier(jnp.max(value_rows, axis=-1, keepdims=True))
    shifted = jnp.exp(value_rows - row_max)
    return shifted / lax.optimization_barrier(jnp.sum(shifted, axis=-1, keepdims=True))

def route_gates(score_logits, picker):
    router = soft_rows(score_logits)
    picked = lax.optimization_barrier(jnp.sum(picker * router[..., None, :], axis=-1))
    return picked / lax.optimization_barrier(jnp.sum(picked, axis=-1, keepdims=True))

def reference(layer_input, attn_gain, q_weight, key_matrix, value_matrix, o_weight, q_gain, key_norm_gain, ffn_gain, router_weight, gate_weight, up_weight, down_weight, routes, out_grad):
    floats = [argument.astype(jnp.float32) for argument in (layer_input, attn_gain, q_weight, key_matrix, value_matrix, o_weight, q_gain, key_norm_gain, ffn_gain, router_weight, gate_weight, up_weight, down_weight)]
    seq_count = layer_input.shape[0]
    token_length = layer_input.shape[1]
    rows_per = DEVICES * CAP
    query_group_width = QUERY_HEADS // KEY_VALUE_HEADS
    score_scale = HEAD_DIM ** (-0.5)
    blocks = routes.reshape(seq_count, N_CTX, STRETCH * TOP)
    expert_hits = (blocks[..., None] == jnp.arange(EXPERTS, dtype=jnp.int32)).astype(jnp.int32)
    route_rank = lax.optimization_barrier(jnp.sum((jnp.cumsum(expert_hits, axis=2) - 1) * expert_hits, axis=-1)).astype(jnp.int32)
    source = jnp.arange(N_CTX, dtype=jnp.int32)[None, :, None] * N_EP + jnp.arange(seq_count, dtype=jnp.int32)[:, None, None]
    slot_of = (blocks * rows_per + source * CAP + route_rank).astype(jnp.int32).reshape(seq_count, token_length, TOP)
    token_of = jnp.broadcast_to(jnp.arange(seq_count * token_length, dtype=jnp.int32).reshape(seq_count, token_length, 1), (seq_count, token_length, TOP))
    sources = jnp.full((EXPERTS * rows_per,), seq_count * token_length, jnp.int32).at[slot_of.reshape(-1)].set(token_of.reshape(-1)).reshape(EXPERTS, rows_per)
    picker = (routes[..., None] == jnp.arange(EXPERTS, dtype=jnp.int32)).astype(jnp.float32)
    token_positions = jnp.arange(token_length).astype(jnp.float32)
    visible = jnp.arange(token_length)[None, :] <= jnp.arange(token_length)[:, None]

    def attend(seq_rows, query_full, key_full, value_full, output_full, query_gain_vector, key_gain_vector):
        query_projected = reduced_backward(jnp.dot(seq_rows, query_full, precision=FULL_PRECISION))
        key_projected = reduced_backward(jnp.dot(seq_rows, key_full, precision=FULL_PRECISION))
        value_projected = jnp.dot(seq_rows, value_full, precision=FULL_PRECISION)
        query_rows = reduced_value(head_prepare(query_projected, query_gain_vector, token_positions, QUERY_HEADS)).reshape(token_length, KEY_VALUE_HEADS, query_group_width, HEAD_DIM)
        key_rows = reduced_value(head_prepare(key_projected, key_gain_vector, token_positions, KEY_VALUE_HEADS))
        value_rows = reduced_value(reduced_backward(value_projected)).reshape(token_length, KEY_VALUE_HEADS, HEAD_DIM)
        raw_scores = reduced_backward(jnp.einsum('cngd,knd->ngck', query_rows, key_rows, precision=FULL_PRECISION) * score_scale)
        masked = jnp.where(visible, raw_scores, -1e+30)
        prob_low = reduced_value(soft_rows(masked))
        attn = reduced_value(reduced_backward(jnp.einsum('ngck,knd->cngd', prob_low, value_rows, precision=FULL_PRECISION))).reshape(token_length, QUERY_HEADS * HEAD_DIM)
        return reduced_backward(jnp.dot(attn, output_full, precision=FULL_PRECISION))

    def forward(input_full, attn_gain_row, query_full, key_full, value_full, output_full, query_gain_vector, key_gain_vector, ffn_gain_row, router_complete, gate_full, up_full, down_full):
        h_one = reduced_value(norm_rows(input_full, attn_gain_row))
        branch = lax.map(jax.checkpoint(lambda seq_rows: attend(seq_rows, query_full, key_full, value_full, output_full, query_gain_vector, key_gain_vector)), h_one)
        resid = input_full + branch
        hidden_second = reduced_value(norm_rows(resid, ffn_gain_row))
        score_logits = reduced_backward(jnp.einsum('ywt,tc->ywc', hidden_second, router_complete, precision=FULL_PRECISION))
        gates = route_gates(score_logits, picker)
        padded = jnp.concatenate([hidden_second.reshape(-1, MODEL_DIM), jnp.zeros((1, MODEL_DIM), jnp.float32)], axis=0)

        def expert(members):
            token_index, gate_mat, up_mat, down_mat = members
            expert_rows = reduced_backward(padded[token_index])
            gate_proj = reduced_backward(jnp.dot(expert_rows, gate_mat, precision=FULL_PRECISION))
            up_proj = reduced_backward(jnp.dot(expert_rows, up_mat, precision=FULL_PRECISION))
            hidden = reduced_value(gate_proj * jax.nn.sigmoid(gate_proj) * up_proj)
            return reduced_value(reduced_backward(jnp.dot(hidden, down_mat, precision=FULL_PRECISION)))
        produced = lax.map(jax.checkpoint(expert), (sources, gate_full, up_full, down_full)).reshape(-1, MODEL_DIM)
        mixed_out = resid
        for route_index in range(TOP):
            mixed_out = mixed_out + gates[..., route_index:route_index + 1] * produced[slot_of[..., route_index]]
        return mixed_out
    mixed_out, pullback = jax.vjp(forward, *floats)
    gradients = pullback(out_grad.astype(jnp.float32))
    return (mixed_out.astype(jnp.bfloat16), gradients[0], gradients[1], gradients[2], gradients[3], gradients[4], gradients[5], gradients[6], gradients[7], gradients[8], gradients[9], gradients[10], gradients[11], gradients[12])
```

```python
import math

import jax
import jax.numpy as jnp
from jax import lax
from jax.experimental import pallas as pl
from jax.experimental.pallas import tpu as pltpu
from jax.sharding import PartitionSpec as P

QUERY_HEADS = 32
KEY_VALUE_HEADS = 4
HEAD_DIM = 128
TOP = 8
BLOCK = 256

EPSILON = 1e-06
ROPE_BASE = 1000000.0
LOG2_E = 1.4426950408889634
F32 = jnp.float32
BF16 = jnp.bfloat16
AXES = ("ctx", "ep")
HIGHEST = lax.Precision.HIGHEST
WINDOW = {"x": 3, "y": 3, "z": 2}


def mm(a, b):
    return jnp.dot(a, b, preferred_element_type=F32)


def mm_t(a, b):
    return lax.dot_general(a, b, (((1,), (1,)), ((), ())), preferred_element_type=F32)


def t_mm(a, b):
    return lax.dot_general(a, b, (((0,), (0,)), ((), ())), preferred_element_type=F32)


def half_turn(v):
    return pltpu.roll(v, HEAD_DIM // 2, 1)


def head_norm(v, gain):
    scale = lax.rsqrt(jnp.mean(v * v, axis=-1, keepdims=True) + EPSILON)
    return v * scale * gain


def head_norm_back(v, gain, dy):
    scale = lax.rsqrt(jnp.mean(v * v, axis=-1, keepdims=True) + EPSILON)
    lifted = gain * dy
    inner = jnp.mean(v * lifted, axis=-1, keepdims=True)
    return (
        scale * lifted - v * (scale * scale * scale * inner),
        jnp.sum(v * scale * dy, axis=0, keepdims=True),
    )


def diagonal_mask():
    key_at = lax.broadcasted_iota(jnp.int32, (BLOCK, BLOCK), 0)
    query_at = lax.broadcasted_iota(jnp.int32, (BLOCK, BLOCK), 1)
    return key_at <= query_at


def attend_kernel(
    q_ref, k_ref, v_ref, cos_ref, sin_ref, qg_ref, kg_ref,
    out_ref, qr_ref, kr_ref, lse_ref, keys, values_t,
):
    blocks = q_ref.shape[0] // BLOCK
    coefficient = LOG2_E * HEAD_DIM ** (-0.5)

    @pl.when(pl.program_id(0) == 0)
    def _():
        normed = head_norm(k_ref[...], kg_ref[...])
        turned = (normed * cos_ref[...] + half_turn(normed) * sin_ref[...]).astype(BF16)
        keys[...] = turned
        kr_ref[...] = turned
        values_t[...] = v_ref[...].T.astype(BF16)

    normed = head_norm(q_ref[...], qg_ref[...])
    queries = (normed * cos_ref[...] + half_turn(normed) * sin_ref[...]).astype(BF16)
    qr_ref[...] = queries
    visible = diagonal_mask()
    for i in range(blocks):
        low, high = i * BLOCK, (i + 1) * BLOCK
        q_i = queries[low:high]
        s_in = jnp.where(visible, mm_t(keys[low:high, :], q_i) * coefficient, -1e30)
        top = jnp.max(s_in, axis=0, keepdims=True)
        if i:
            s_off = mm_t(keys[:low, :], q_i) * coefficient
            top = jnp.maximum(top, jnp.max(s_off, axis=0, keepdims=True))
        p_in = jnp.exp2(s_in - top)
        total = jnp.sum(p_in, axis=0, keepdims=True)
        mixed = mm(values_t[:, low:high], p_in.astype(BF16))
        if i:
            p_off = jnp.exp2(s_off - top)
            total = total + jnp.sum(p_off, axis=0, keepdims=True)
            mixed = mixed + mm(values_t[:, :low], p_off.astype(BF16))
        out_ref[low:high, :] = (mixed * (1.0 / total)).T.astype(BF16)
        lse_ref[0, :, low:high] = top + jnp.log2(total)


def attend_back_kernel(
    qr_ref, q_ref, do_ref, out_ref, lse_ref, kr_ref, k_ref, v_ref, cos_ref, sin_ref, qg_ref, kg_ref,
    grad_ref, qgain_ref, kgain_ref, keys_t, values, dk, dv, dq,
):
    step = pl.program_id(0)
    heads = pl.num_programs(0) - 2
    blocks = q_ref.shape[0] // BLOCK
    scale = HEAD_DIM ** (-0.5)
    coefficient = LOG2_E * scale

    @pl.when(step == 0)
    def _():
        keys_t[...] = kr_ref[...].astype(F32).T.astype(BF16)
        values[...] = v_ref[...].astype(BF16)
        dk[...] = jnp.zeros_like(dk)
        dv[...] = jnp.zeros_like(dv)
        qgain_ref[...] = jnp.zeros_like(qgain_ref)

    def turn_back(v):
        return v * cos_ref[...] - half_turn(v) * sin_ref[...]

    @pl.when(step < heads)
    def _():
        delta = jnp.sum((do_ref[...].astype(F32) * out_ref[...].astype(F32)).T, axis=0, keepdims=True)
        visible = diagonal_mask()
        for i in range(blocks):
            low, high = i * BLOCK, (i + 1) * BLOCK
            q_i = qr_ref[low:high, :]
            do_i = do_ref[low:high, :]
            lse_i = lse_ref[0, :, low:high]
            delta_i = delta[:, low:high]

            def part(first, last, masked):
                p = jnp.exp2(mm_t(kr_ref[first:last, :], q_i) * coefficient - lse_i)
                if masked:
                    p = jnp.where(visible, p, 0.0)
                dp = mm_t(values[first:last, :], do_i)
                dv[first:last, :] += mm(p.astype(BF16), do_i)
                ds = (p * (dp - delta_i)).astype(BF16)
                dk[first:last, :] += mm(ds, q_i)
                return mm(keys_t[:, first:last], ds)

            turned = part(low, high, True)
            if i:
                turned = turned + part(0, low, False)
            dq[low:high, :] = turned.T * scale
        back, gain_part = head_norm_back(q_ref[...], qg_ref[...], turn_back(dq[...]))
        grad_ref[...] = back.astype(BF16)
        qgain_ref[...] += gain_part

    @pl.when(step == heads)
    def _():
        back, gain_part = head_norm_back(k_ref[...], kg_ref[...], turn_back(dk[...] * scale))
        grad_ref[...] = back.astype(BF16)
        kgain_ref[...] = gain_part

    @pl.when(step == heads + 1)
    def _():
        grad_ref[...] = dv[...].astype(BF16)


def attend(qkv, cos, sin, q_gain, k_gain, heads):
    length = qkv.shape[0]
    column = lambda at: pl.BlockSpec((length, HEAD_DIM), lambda h: (0, at))
    moving = pl.BlockSpec((length, HEAD_DIM), lambda h: (0, h))
    fixed = pl.BlockSpec((length, HEAD_DIM), lambda h: (0, 0))
    row = pl.BlockSpec((1, HEAD_DIM), lambda h: (0, 0))
    pairs = heads * length * length
    return pl.pallas_call(
        attend_kernel,
        grid=(heads,),
        in_specs=[moving, column(heads), column(heads + 1), fixed, fixed, row, row],
        out_specs=[moving, moving, fixed, pl.BlockSpec((1, 1, length), lambda h: (h, 0, 0))],
        out_shape=[
            jax.ShapeDtypeStruct((length, heads * HEAD_DIM), BF16),
            jax.ShapeDtypeStruct((length, heads * HEAD_DIM), BF16),
            jax.ShapeDtypeStruct((length, HEAD_DIM), BF16),
            jax.ShapeDtypeStruct((heads, 1, length), F32),
        ],
        scratch_shapes=[pltpu.VMEM((length, HEAD_DIM), BF16), pltpu.VMEM((HEAD_DIM, length), BF16)],
        compiler_params=pltpu.CompilerParams(vmem_limit_bytes=40 * 1024 * 1024),
        cost_estimate=pl.CostEstimate(
            flops=2 * pairs * HEAD_DIM, bytes_accessed=10 * length * heads * HEAD_DIM, transcendentals=pairs // 2
        ),
        name="attend",
    )(qkv, qkv, qkv, cos, sin, q_gain, k_gain)


def attend_back(qkv, turned_q, turned_k, out, lse, grad_out, cos, sin, q_gain, k_gain, heads):
    length = qkv.shape[0]
    column = lambda at: pl.BlockSpec((length, HEAD_DIM), lambda h: (0, at))
    moving = pl.BlockSpec((length, HEAD_DIM), lambda h: (0, jnp.minimum(h, heads - 1)))
    fixed = pl.BlockSpec((length, HEAD_DIM), lambda h: (0, 0))
    row = pl.BlockSpec((1, HEAD_DIM), lambda h: (0, 0))
    pairs = heads * length * length
    return pl.pallas_call(
        attend_back_kernel,
        grid=(heads + 2,),
        in_specs=[
            moving, moving, moving, moving,
            pl.BlockSpec((1, 1, length), lambda h: (jnp.minimum(h, heads - 1), 0, 0)),
            fixed, column(heads), column(heads + 1), fixed, fixed, row, row,
        ],
        out_specs=[pl.BlockSpec((length, HEAD_DIM), lambda h: (0, h)), row, row],
        out_shape=[
            jax.ShapeDtypeStruct((length, (heads + 2) * HEAD_DIM), BF16),
            jax.ShapeDtypeStruct((1, HEAD_DIM), F32),
            jax.ShapeDtypeStruct((1, HEAD_DIM), F32),
        ],
        scratch_shapes=[
            pltpu.VMEM((HEAD_DIM, length), BF16),
            pltpu.VMEM((length, HEAD_DIM), BF16),
            pltpu.VMEM((length, HEAD_DIM), F32),
            pltpu.VMEM((length, HEAD_DIM), F32),
            pltpu.VMEM((length, HEAD_DIM), F32),
        ],
        compiler_params=pltpu.CompilerParams(vmem_limit_bytes=40 * 1024 * 1024),
        cost_estimate=pl.CostEstimate(
            flops=5 * pairs * HEAD_DIM, bytes_accessed=14 * length * heads * HEAD_DIM, transcendentals=pairs // 2
        ),
        name="attend_back",
    )(turned_q, qkv, grad_out, out, lse, turned_k, qkv, qkv, cos, sin, q_gain, k_gain)


def norm_back(v, scale, gain, dy):
    lifted = gain * dy
    inner = jnp.mean(v * lifted, axis=-1, keepdims=True)
    return scale * lifted - v * (scale * scale * scale * inner), jnp.sum(v * scale * dy, axis=0)


def layer(
    nctx, nep,
    layer_input, attn_gain, q_weight, key_matrix, value_matrix, o_weight, q_gain, key_norm_gain,
    ffn_gain, router_weight, gate_weight, up_weight, down_weight, routes, out_grad,
):
    rows, width = layer_input.shape[1:]
    devices = nctx * nep
    nz = nep // 2
    np_ = nctx * 2
    nb = nctx
    experts = devices
    capacity = rows * TOP * 5 // (4 * experts)
    length = rows * nctx
    heads = QUERY_HEADS // nctx
    q_cols = heads * HEAD_DIM
    at_ctx = lax.axis_index("ctx")
    at_ep = lax.axis_index("ep")

    lanes = {"x": [], "y": [], "z": [], "core": []}

    def after(v, *done):
        return lax.optimization_barrier((v, *done))[0]

    def swap(v, by_ctx, by_ep, window=True):
        if by_ctx == 0 and by_ep == 0:
            return v
        taken = [name for name, used in (("x", by_ctx >> 1), ("y", by_ep & 1), ("z", by_ep >> 1)) if used]
        if window:
            ahead = [lanes[name][-WINDOW[name]] for name in taken if len(lanes[name]) >= WINDOW[name]]
            if ahead:
                v = after(v, *ahead)
        pairs = [(i, ((i // nep) ^ by_ctx) * nep + ((i % nep) ^ by_ep)) for i in range(devices)]
        got = lax.ppermute(v, AXES, pairs)
        if window:
            for name in taken or ["core"]:
                lanes[name].append(got)
        return got

    def to_plane(v):
        n = v.shape[0] // nb
        half = n // 2
        got = [v[:n]] + [swap(v[b * n : (b + 1) * n], b & ~1, b & 1) for b in range(1, nb)]
        other = swap(jnp.concatenate([g[half:] for g in got], axis=0), 1, 0)
        return jnp.concatenate([g[:half] for g in got] + [other], axis=0)

    def from_plane(v):
        half = v.shape[0] // np_
        other = swap(v[nb * half :], 1, 0)
        sent = [jnp.concatenate([u[b * half : (b + 1) * half] for u in (v, other)], axis=0) for b in range(nb)]
        return jnp.concatenate([sent[0]] + [swap(sent[b], b & ~1, b & 1) for b in range(1, nb)], axis=0)

    def gather_z(piece, window=True):
        return [swap(piece, 0, 2 * j, window) for j in range(nz)]

    def gather_y(far, window=True):
        deep = far[0].shape[0]
        whole = jnp.zeros((nep * deep, far[0].shape[1]), far[0].dtype)
        for j in range(nz):
            for ry in range(2):
                part = swap(far[j], 0, ry, window)
                whole = lax.dynamic_update_slice(whole, part, ((at_ep ^ (2 * j + ry)) * deep, 0))
        return whole

    def sum_all(v):
        for by_ctx, by_ep in [(0, 1 << b) for b in range(nep.bit_length() - 1)] + [(1 << b, 0) for b in range(nctx.bit_length() - 1)]:
            v = v + swap(v, by_ctx, by_ep, False)
        return v

    def gather_ctx(piece):
        deep = piece.shape[0]
        whole = jnp.zeros((nctx * deep, piece.shape[1]), piece.dtype)
        for hi in range(0, nctx, 2):
            far = swap(piece, hi, 0)
            for lo in range(2):
                part = swap(far, lo, 0)
                whole = lax.dynamic_update_slice(whole, part, ((at_ctx ^ (hi + lo)) * deep, 0))
        return whole

    def scatter_ctx(block_of):
        held = {}
        for hi in reversed(range(0, nctx, 2)):
            arrived = swap(block_of(hi + 1).astype(BF16), 1, 0)
            held[hi] = block_of(hi) + arrived.astype(F32)
        total = held[0]
        for hi in range(2, nctx, 2):
            total = total + swap(held[hi].astype(BF16), hi, 0).astype(F32)
        return total

    def own_rows(v, m):
        return lax.dynamic_slice_in_dim(v, (at_ctx ^ m) * rows, rows, 0)

    x = layer_input[0].astype(F32)
    scale_one = lax.rsqrt(jnp.mean(x * x, axis=-1, keepdims=True) + EPSILON)
    h_one = (x * scale_one * attn_gain).astype(BF16)
    o_cols = width // nctx
    far_o = gather_z(lax.dynamic_slice_in_dim(o_weight, at_ctx * o_cols, o_cols, 1))
    qkv_piece = jnp.concatenate(
        [
            lax.dynamic_slice_in_dim(q_weight, at_ctx * q_cols, q_cols, 1),
            lax.dynamic_slice_in_dim(key_matrix, at_ctx * HEAD_DIM, HEAD_DIM, 1),
            lax.dynamic_slice_in_dim(value_matrix, at_ctx * HEAD_DIM, HEAD_DIM, 1),
        ],
        axis=1,
    )
    far_qkv = gather_z(qkv_piece)
    h_full = gather_ctx(h_one)
    o_all = gather_y(far_o)
    qkv_weight = gather_y(far_qkv)
    o_rows = jnp.zeros((q_cols, width), BF16)
    for m in range(nctx):
        there = at_ctx ^ m
        part = swap(lax.dynamic_slice_in_dim(o_all, there * q_cols, q_cols, 0), m, 0)
        o_rows = lax.dynamic_update_slice(o_rows, part, (0, there * o_cols))

    local_routes = after(routes[0], far_o[1])
    token = jnp.arange(rows, dtype=jnp.int32)
    upto = (token[:, None] <= token[None, :]).astype(BF16)
    slots = jnp.arange(capacity, dtype=jnp.int32).astype(F32)

    def slot_table(hits):
        rank = mm(hits.astype(BF16), upto) - 1.0
        return ((rank[:, None, :] == slots[None, :, None]) & (hits[:, None, :] > 0)).astype(BF16)

    plane_steps = jnp.arange(np_, dtype=jnp.int32)
    plane_chip, plane_core = plane_steps >> 1, plane_steps & 1
    plane_experts = (at_ctx ^ (plane_chip & ~1) ^ plane_core) * nep + (at_ep ^ (plane_chip & 1))
    routes_t = local_routes.T
    tables = []
    for j in range(nz):
        there = swap(routes_t, 0, 2 * j, False)
        hits = jnp.sum((there[None] == plane_experts[:, None, None]).astype(F32), axis=1)
        tables.append(slot_table(hits).reshape(np_ * capacity, rows))
    expert_ids = jnp.arange(experts, dtype=jnp.int32)
    picker_t = jnp.sum((routes_t[None] == expert_ids[:, None, None]).astype(F32), axis=1)
    picker = picker_t.T
    steps = jnp.arange(devices, dtype=jnp.int32)
    step_j, step_r = steps // np_, steps % np_
    step_chip, step_core = step_r % nb, step_r // nb
    step_source = (at_ctx ^ (step_chip & ~1) ^ step_core) * nep + (at_ep ^ (2 * step_j) ^ (step_chip & 1))
    reorder = (step_source[:, None] == steps[None, :]).astype(F32)

    def to_experts(v):
        arrived = lax.all_to_all(v, AXES, split_axis=0, concat_axis=0, tiled=True)
        return jnp.dot(reorder, arrived, precision=HIGHEST)

    def from_experts(v):
        ordered = jnp.dot(reorder.T, v, precision=HIGHEST)
        return lax.all_to_all(ordered, AXES, split_axis=0, concat_axis=0, tiled=True)

    expert_table = slot_table(to_experts(picker_t))

    def send(j, tokens):
        return to_plane(mm(tables[j], tokens).astype(BF16))

    def bring(j, made):
        total = t_mm(tables[j], from_plane(made))
        return swap(total.astype(BF16), 0, 2 * j).astype(F32) if j else total

    grad_out = out_grad[0]
    far_g = gather_z(grad_out)
    arrived_g = [send(0, far_g[0])]
    early_y, early_xy = lanes["y"][-2:]
    arrived_g.append(send(1, far_g[1]))
    router_full = gather_y(gather_z(after(router_weight, far_qkv[1]), False), False)
    qkv = mm(h_full, qkv_weight)

    frequency = ROPE_BASE ** (-jnp.arange(HEAD_DIM // 2).astype(F32) * 2.0 / HEAD_DIM)
    angles = jnp.arange(length).astype(F32)[:, None] * frequency[None, :]
    cosine, sine = jnp.cos(angles), jnp.sin(angles)
    cos_full = jnp.concatenate([cosine, cosine], axis=1)
    sin_full = jnp.concatenate([-sine, sine], axis=1)
    q_gain_row, k_gain_row = q_gain[None, :], key_norm_gain[None, :]
    attn, turned_q, turned_k, lse = attend(after(qkv, early_y), cos_full, sin_full, q_gain_row, k_gain_row, heads)
    attn = after(attn, early_xy)
    branch = scatter_ctx(lambda m: mm(own_rows(attn, m), o_rows))
    arrived_g += [send(j, far_g[j]) for j in range(2, nz)]

    resid = x + branch
    scale_two = lax.rsqrt(jnp.mean(resid * resid, axis=-1, keepdims=True) + EPSILON)
    h_two = (resid * scale_two * ffn_gain).astype(BF16)
    logits = mm(h_two, router_full)
    shifted = jnp.exp(logits - jnp.max(logits, axis=-1, keepdims=True))
    router = shifted / jnp.sum(shifted, axis=-1, keepdims=True)
    picked_total = jnp.sum(picker * router, axis=-1, keepdims=True)
    gates = picker * router / picked_total

    gate_up = jnp.concatenate([gate_weight[0], up_weight[0]], axis=1)
    down = down_weight[0]
    ff = down.shape[0]
    row_gates = jnp.sum(expert_table.astype(F32) * to_experts(gates.T)[:, None, :], axis=-1)
    row_gates = row_gates.reshape(nz, np_ * capacity, 1)
    far_h = gather_z(h_two)
    arrived_h, posted = [], []
    for j in range(nz):
        arrived_h.append(send(j, far_h[j]))
        posted.append(lanes["y"][-2])
    hidden_all, grad_gate_all, grad_up_all, grad_copies, dots = [], [], [], [], []

    def expert(j, *done):
        h_j = after(arrived_h[j], *done)
        grad_down = mm_t(arrived_g[j], down)
        both = mm(h_j, gate_up)
        gate_proj, up_proj = both[:, :ff], both[:, ff:]
        sigmoid = jax.nn.sigmoid(gate_proj)
        hidden = gate_proj * sigmoid * up_proj
        dots.append(jnp.sum(hidden * grad_down, axis=-1).reshape(np_, capacity))
        weighted = grad_down * row_gates[j]
        grad_up = (weighted * gate_proj * sigmoid).astype(BF16)
        grad_gate = (weighted * up_proj * sigmoid * (1.0 + gate_proj * (1.0 - sigmoid))).astype(BF16)
        grad_copies.append(mm_t(jnp.concatenate([grad_gate, grad_up], axis=1), gate_up).astype(BF16))
        hidden_all.append((hidden * row_gates[j]).astype(BF16))
        grad_gate_all.append(grad_gate)
        grad_up_all.append(grad_up)

    for j in range(nz - 1):
        expert(j, posted[j + 1])
    order = [*range(1, nz), 0]
    returned, marks = [], []
    for j in order:
        if j == nz - 1:
            expert(j, lanes["core"][-1])
        returned.append(bring(j, grad_copies[j]))
        marks.append(lanes["y"][-2])
    grad_two = sum(returned)
    joined_h = jnp.concatenate(arrived_h, axis=0)
    gate_part = t_mm(joined_h, after(jnp.concatenate(grad_gate_all, axis=0), marks[0]))
    up_part = t_mm(joined_h, after(jnp.concatenate(grad_up_all, axis=0), marks[1]))
    down_part = t_mm(after(jnp.concatenate(hidden_all, axis=0), marks[2]), jnp.concatenate(arrived_g, axis=0))
    outs = {j: mm(after(hidden_all[j], marks[2]), down).astype(BF16) for j in range(nz)}
    mixed = resid + bring(1, outs[1])

    slot_dots = jnp.concatenate(dots, axis=0)
    token_dots = jnp.sum(expert_table.astype(F32) * slot_dots[:, :, None], axis=1)
    grad_gates = from_experts(token_dots).T
    grad_pick = picker * (grad_gates - jnp.sum(grad_gates * gates, axis=-1, keepdims=True)) / picked_total
    grad_logits = router * (grad_pick - jnp.sum(router * grad_pick, axis=-1, keepdims=True))
    logit_low = grad_logits.astype(BF16)
    grad_two = grad_two + mm_t(logit_low, router_full)
    grad_resid, ffn_gain_part = norm_back(resid, scale_two, ffn_gain, grad_two)
    grad_resid = grad_resid + grad_out.astype(F32)
    router_part = t_mm(logit_low, h_two)
    branch_full = gather_ctx(grad_resid.astype(BF16))
    for j in range(2, nz):
        mixed = mixed + bring(j, outs[j])
    grad_attn = mm_t(branch_full, o_rows).astype(BF16)
    def scatter_ep(term):
        total, first = None, None
        for j in reversed(range(nz)):
            arrived = swap(term(j, 1).astype(BF16), 0, 1)
            first = arrived if first is None else first
            near = term(j, 0) + arrived.astype(F32)
            if j:
                near = swap(near.astype(BF16), 0, 2 * j).astype(F32)
            total = near if total is None else total + near
        return total, first

    o_own = q_cols // nep
    own_width = width // devices
    o_part = t_mm(attn, branch_full)
    router_part = t_mm(logit_low, h_two).reshape(experts, nctx, nep, own_width)
    router_rows = experts * nctx * own_width // width

    def o_term(j, ry):
        there = at_ep ^ (2 * j + ry)
        block = lax.dynamic_slice_in_dim(o_part, there * o_own, o_own, 0)
        router_block = lax.dynamic_slice_in_dim(router_part, there, 1, 2).reshape(router_rows, width)
        return jnp.concatenate([block, router_block], axis=0)

    o_sum, o_first = scatter_ep(o_term)
    o_grad = o_sum[:o_own]
    router_sum = o_sum[o_own:].reshape(experts, nctx, own_width).transpose(1, 2, 0)
    grad_qkv, q_gain_part, k_gain_part = attend_back(
        qkv, turned_q, turned_k, attn, lse, after(grad_attn, o_first), cos_full, sin_full, q_gain_row, k_gain_row, heads
    )
    qkv_part = t_mm(h_full, grad_qkv).reshape(nctx, nep, own_width, -1)

    def qkv_term(j, ry):
        return lax.dynamic_slice_in_dim(qkv_part, at_ep ^ (2 * j + ry), 1, 1)[:, 0]

    qkv_sum, qkv_first = scatter_ep(qkv_term)
    late_qkv = after(grad_qkv, qkv_first)
    grad_one = scatter_ctx(lambda m: mm_t(own_rows(late_qkv, m), qkv_weight))
    grad_input, attn_gain_part = norm_back(x, scale_one, attn_gain, grad_one)
    input_grad = grad_resid + grad_input
    late = sum_all(jnp.concatenate([attn_gain_part, ffn_gain_part, q_gain_part[0], k_gain_part[0]]))

    mixed = mixed + bring(0, outs[0])
    last = jnp.concatenate([qkv_sum, router_sum], axis=2).astype(BF16)
    last = lax.all_to_all(last, "ctx", split_axis=0, concat_axis=0, tiled=True).astype(F32)
    qkv_grad = last
    router_grad = jnp.sum(last[:, :, q_cols + 2 * HEAD_DIM :], axis=0)

    def columns(first, last):
        return jnp.concatenate([qkv_grad[c, :, first:last] for c in range(nctx)], axis=1)

    return (
        mixed.astype(BF16)[None],
        input_grad[None],
        late[:width],
        columns(0, q_cols),
        columns(q_cols, q_cols + HEAD_DIM),
        columns(q_cols + HEAD_DIM, q_cols + 2 * HEAD_DIM),
        o_grad,
        late[2 * width : 2 * width + HEAD_DIM],
        late[2 * width + HEAD_DIM :],
        late[width : 2 * width],
        router_grad,
        gate_part[None],
        up_part[None],
        down_part[None],
    )


def solution(mesh):
    nctx, nep = mesh.shape["ctx"], mesh.shape["ep"]
    tokens = P("ep", "ctx", None)
    own = P(("ctx", "ep"), None)
    expert = P(("ctx", "ep"), None, None)
    by_rows = P("ep", None)

    def on_device(*arrays):
        return layer(nctx, nep, *arrays)

    return jax.shard_map(
        on_device,
        mesh=mesh,
        in_specs=(
            tokens, P(), by_rows, by_rows, by_rows, by_rows, P(), P(), P(), by_rows,
            expert, expert, expert, tokens, tokens,
        ),
        out_specs=(
            tokens, tokens, P(), own, own, own, own, P(), P(), P(), own, expert, expert, expert,
        ),
        check_vma=False,
    )
```

```python
import math

import jax
import jax.numpy as jnp
from jax import lax
from jax.experimental import pallas as pl
from jax.experimental.pallas import tpu as pltpu
from jax.sharding import PartitionSpec as P

QUERY_HEADS = 32
KEY_VALUE_HEADS = 4
HEAD_DIM = 128
TOP = 8
BLOCK = 256

EPSILON = 1e-06
ROPE_BASE = 1000000.0
LOG2_E = 1.4426950408889634
F32 = jnp.float32
BF16 = jnp.bfloat16
AXES = ("ctx", "ep")
HIGHEST = lax.Precision.HIGHEST


def mm(a, b):
    return jnp.dot(a, b, preferred_element_type=F32)


def mm_t(a, b):
    return lax.dot_general(a, b, (((1,), (1,)), ((), ())), preferred_element_type=F32)


def t_mm(a, b):
    return lax.dot_general(a, b, (((0,), (0,)), ((), ())), preferred_element_type=F32)


LIGHT = pl.CostEstimate(flops=1, bytes_accessed=1, transcendentals=0)
VMEM_MOST = 56 * 1024 * 1024


def half_turn(v):
    return pltpu.roll(v, HEAD_DIM // 2, 1)


def head_norm(v, gain):
    scale = lax.rsqrt(jnp.mean(v * v, axis=-1, keepdims=True) + EPSILON)
    return v * scale * gain


def head_norm_back(v, gain, dy):
    scale = lax.rsqrt(jnp.mean(v * v, axis=-1, keepdims=True) + EPSILON)
    lifted = gain * dy
    inner = jnp.mean(v * lifted, axis=-1, keepdims=True)
    return (
        scale * lifted - v * (scale * scale * scale * inner),
        jnp.sum(v * scale * dy, axis=0, keepdims=True),
    )


def diagonal_mask():
    key_at = lax.broadcasted_iota(jnp.int32, (BLOCK, BLOCK), 0)
    query_at = lax.broadcasted_iota(jnp.int32, (BLOCK, BLOCK), 1)
    return key_at <= query_at


def attend_kernel(
    q_ref, k_ref, v_ref, cos_ref, sin_ref, qg_ref, kg_ref,
    out_ref, qr_ref, kr_ref, lse_ref, keys, values_t,
):
    blocks = q_ref.shape[0] // BLOCK
    coefficient = LOG2_E * HEAD_DIM ** (-0.5)

    @pl.when(pl.program_id(0) == 0)
    def _():
        normed = head_norm(k_ref[...], kg_ref[...])
        turned = (normed * cos_ref[...] + half_turn(normed) * sin_ref[...]).astype(BF16)
        keys[...] = turned
        kr_ref[...] = turned
        values_t[...] = v_ref[...].T.astype(BF16)

    normed = head_norm(q_ref[...], qg_ref[...])
    queries = (normed * cos_ref[...] + half_turn(normed) * sin_ref[...]).astype(BF16)
    qr_ref[...] = queries
    visible = diagonal_mask()
    for i in range(blocks):
        low, high = i * BLOCK, (i + 1) * BLOCK
        q_i = queries[low:high]
        s_in = jnp.where(visible, mm_t(keys[low:high, :], q_i) * coefficient, -1e30)
        top = jnp.max(s_in, axis=0, keepdims=True)
        if i:
            s_off = mm_t(keys[:low, :], q_i) * coefficient
            top = jnp.maximum(top, jnp.max(s_off, axis=0, keepdims=True))
        p_in = jnp.exp2(s_in - top)
        total = jnp.sum(p_in, axis=0, keepdims=True)
        mixed = mm(values_t[:, low:high], p_in.astype(BF16))
        if i:
            p_off = jnp.exp2(s_off - top)
            total = total + jnp.sum(p_off, axis=0, keepdims=True)
            mixed = mixed + mm(values_t[:, :low], p_off.astype(BF16))
        out_ref[low:high, :] = (mixed * (1.0 / total)).T.astype(BF16)
        lse_ref[0, :, low:high] = top + jnp.log2(total)


def attend_back_kernel(
    qr_ref, q_ref, do_ref, out_ref, lse_ref, kr_ref, k_ref, v_ref, cos_ref, sin_ref, qg_ref, kg_ref,
    grad_ref, qgain_ref, kgain_ref, keys_t, values, dk, dv, dq,
):
    step = pl.program_id(0)
    heads = pl.num_programs(0) - 2
    blocks = q_ref.shape[0] // BLOCK
    scale = HEAD_DIM ** (-0.5)
    coefficient = LOG2_E * scale

    @pl.when(step == 0)
    def _():
        keys_t[...] = kr_ref[...].astype(F32).T.astype(BF16)
        values[...] = v_ref[...].astype(BF16)
        dk[...] = jnp.zeros_like(dk)
        dv[...] = jnp.zeros_like(dv)
        qgain_ref[...] = jnp.zeros_like(qgain_ref)

    def turn_back(v):
        return v * cos_ref[...] - half_turn(v) * sin_ref[...]

    @pl.when(step < heads)
    def _():
        delta = jnp.sum((do_ref[...].astype(F32) * out_ref[...].astype(F32)).T, axis=0, keepdims=True)
        visible = diagonal_mask()
        for i in range(blocks):
            low, high = i * BLOCK, (i + 1) * BLOCK
            q_i = qr_ref[low:high, :]
            do_i = do_ref[low:high, :]
            lse_i = lse_ref[0, :, low:high]
            delta_i = delta[:, low:high]

            def part(first, last, masked):
                p = jnp.exp2(mm_t(kr_ref[first:last, :], q_i) * coefficient - lse_i)
                if masked:
                    p = jnp.where(visible, p, 0.0)
                dp = mm_t(values[first:last, :], do_i)
                dv[first:last, :] += mm(p.astype(BF16), do_i)
                ds = (p * (dp - delta_i)).astype(BF16)
                dk[first:last, :] += mm(ds, q_i)
                return mm(keys_t[:, first:last], ds)

            turned = part(low, high, True)
            if i:
                turned = turned + part(0, low, False)
            dq[low:high, :] = turned.T * scale
        back, gain_part = head_norm_back(q_ref[...], qg_ref[...], turn_back(dq[...]))
        grad_ref[...] = back.astype(BF16)
        qgain_ref[...] += gain_part

    @pl.when(step == heads)
    def _():
        back, gain_part = head_norm_back(k_ref[...], kg_ref[...], turn_back(dk[...] * scale))
        grad_ref[...] = back.astype(BF16)
        kgain_ref[...] = gain_part

    @pl.when(step == heads + 1)
    def _():
        grad_ref[...] = dv[...].astype(BF16)


def attend(qkv, cos, sin, q_gain, k_gain, heads):
    length = qkv.shape[0]
    column = lambda at: pl.BlockSpec((length, HEAD_DIM), lambda h: (0, at))
    moving = pl.BlockSpec((length, HEAD_DIM), lambda h: (0, h))
    fixed = pl.BlockSpec((length, HEAD_DIM), lambda h: (0, 0))
    row = pl.BlockSpec((1, HEAD_DIM), lambda h: (0, 0))
    return pl.pallas_call(
        attend_kernel,
        grid=(heads,),
        in_specs=[moving, column(heads), column(heads + 1), fixed, fixed, row, row],
        out_specs=[moving, moving, fixed, pl.BlockSpec((1, 1, length), lambda h: (h, 0, 0))],
        out_shape=[
            jax.ShapeDtypeStruct((length, heads * HEAD_DIM), BF16),
            jax.ShapeDtypeStruct((length, heads * HEAD_DIM), BF16),
            jax.ShapeDtypeStruct((length, HEAD_DIM), BF16),
            jax.ShapeDtypeStruct((heads, 1, length), F32),
        ],
        scratch_shapes=[pltpu.VMEM((length, HEAD_DIM), BF16), pltpu.VMEM((HEAD_DIM, length), BF16)],
        compiler_params=pltpu.CompilerParams(vmem_limit_bytes=40 * 1024 * 1024),
        cost_estimate=LIGHT,
        name="attend",
    )(qkv, qkv, qkv, cos, sin, q_gain, k_gain)


def attend_back(qkv, turned_q, turned_k, out, lse, grad_out, cos, sin, q_gain, k_gain, heads):
    length = qkv.shape[0]
    column = lambda at: pl.BlockSpec((length, HEAD_DIM), lambda h: (0, at))
    moving = pl.BlockSpec((length, HEAD_DIM), lambda h: (0, jnp.minimum(h, heads - 1)))
    fixed = pl.BlockSpec((length, HEAD_DIM), lambda h: (0, 0))
    row = pl.BlockSpec((1, HEAD_DIM), lambda h: (0, 0))
    return pl.pallas_call(
        attend_back_kernel,
        grid=(heads + 2,),
        in_specs=[
            moving, moving, moving, moving,
            pl.BlockSpec((1, 1, length), lambda h: (jnp.minimum(h, heads - 1), 0, 0)),
            fixed, column(heads), column(heads + 1), fixed, fixed, row, row,
        ],
        out_specs=[pl.BlockSpec((length, HEAD_DIM), lambda h: (0, h)), row, row],
        out_shape=[
            jax.ShapeDtypeStruct((length, (heads + 2) * HEAD_DIM), BF16),
            jax.ShapeDtypeStruct((1, HEAD_DIM), F32),
            jax.ShapeDtypeStruct((1, HEAD_DIM), F32),
        ],
        scratch_shapes=[
            pltpu.VMEM((HEAD_DIM, length), BF16),
            pltpu.VMEM((length, HEAD_DIM), BF16),
            pltpu.VMEM((length, HEAD_DIM), F32),
            pltpu.VMEM((length, HEAD_DIM), F32),
            pltpu.VMEM((length, HEAD_DIM), F32),
        ],
        compiler_params=pltpu.CompilerParams(vmem_limit_bytes=40 * 1024 * 1024),
        cost_estimate=LIGHT,
        name="attend_back",
    )(turned_q, qkv, grad_out, out, lse, turned_k, qkv, qkv, cos, sin, q_gain, k_gain)


def select_kernel(n_parts, table, *refs):
    parts, outs = refs[:n_parts], refs[n_parts:]
    deep = outs[0].shape[0]
    first = 0
    for part in parts:
        for at in range(0, part.shape[1], 1024):
            wide = min(1024, part.shape[1] - at)
            rows = mm(table[...], part[:, at : at + wide]).astype(BF16)
            for b, out in enumerate(outs):
                out[:, first : first + wide] = rows[b * deep : (b + 1) * deep]
            first += wide


def select(table, parts, chips):
    width, deep = sum(v.shape[1] for v in parts), table.shape[0] // chips
    return pl.pallas_call(
        lambda *refs: select_kernel(len(parts), *refs),
        out_shape=[jax.ShapeDtypeStruct((deep, width), BF16)] * chips,
        compiler_params=pltpu.CompilerParams(vmem_limit_bytes=VMEM_MOST),
        cost_estimate=LIGHT,
        name="select",
    )(table, *parts)


def combine_kernel(n_pieces, table, *refs):
    pieces, outs = refs[:n_pieces], refs[n_pieces:]
    deep, width = outs[0].shape
    for first in range(0, width, 512):
        at = slice(first, min(first + 512, width))
        rows = jnp.concatenate([p[:, at] for p in pieces], axis=0)
        total = t_mm(table[...], rows)
        for i, out in enumerate(outs):
            out[:, at] = total[i * deep : (i + 1) * deep].astype(out.dtype)


def combine(table, pieces, dtype, shares):
    shape = (table.shape[1] // shares, pieces[0].shape[1])
    return pl.pallas_call(
        lambda *refs: combine_kernel(len(pieces), *refs),
        out_shape=[jax.ShapeDtypeStruct(shape, dtype)] * shares,
        compiler_params=pltpu.CompilerParams(vmem_limit_bytes=VMEM_MOST),
        cost_estimate=LIGHT,
        name="combine",
    )(table, *pieces)


def pack_kernel(chips, near, other, *outs):
    deep = outs[0].shape[0] // 2
    first = 0
    for group in (outs[:chips], outs[chips:]):
        at = slice(first, first + group[0].shape[1])
        for b, out in enumerate(group):
            out[:deep, :] = near[b * deep : (b + 1) * deep, at]
            out[deep:, :] = other[b * deep : (b + 1) * deep, at]
        first = at.stop


def pack(near, other, chips, width):
    deep, first = 2 * near.shape[0] // chips, near.shape[1] - width
    got = pl.pallas_call(
        lambda *refs: pack_kernel(chips, *refs),
        out_shape=[jax.ShapeDtypeStruct((deep, n), BF16) for n in (first, width) for _ in range(chips)],
        compiler_params=pltpu.CompilerParams(vmem_limit_bytes=VMEM_MOST),
        cost_estimate=LIGHT,
        name="pack",
    )(near, other)
    return got[:chips], got[chips:]


def expert_kernel(chips, ff_tiles, n_in, *refs):
    h_in, g_in = refs[: chips + 1], refs[chips + 1 : 2 * chips + 2]
    gate_c, up_c, down_r, gate_r, up_r, down_c, router, picks, marks = refs[2 * chips + 2 : 2 * chips + 11]
    results = refs[n_in : n_in + 2]
    h_all, g_all, hid_all, gg_all, gu_all, scale, dots = refs[n_in + 2 :]
    step = pl.program_id(0)
    deep = h_in[0].shape[0] // 2
    half = chips * deep
    wide, out_wide = gate_c.shape[1], down_c.shape[1]
    width = h_in[0].shape[1]

    @pl.when(step == 0)
    def _():
        for arrived, joined in ((h_in, h_all), (g_in, g_all)):
            for b in range(chips):
                joined[b * deep : (b + 1) * deep, :] = arrived[b][:deep, :]
            joined[half:, :] = arrived[chips][...]
        dots[...] = jnp.zeros_like(dots)
        logits = mm(h_all[...], router[...])
        picked = picks[...] > 0
        top = jnp.max(jnp.where(picked, logits, -1e30), axis=-1, keepdims=True)
        weight = jnp.where(picked, jnp.exp(logits - top), 0.0)
        total = jnp.sum(weight, axis=-1, keepdims=True)
        own = jnp.sum(weight * marks[0:1, : logits.shape[1]], axis=-1, keepdims=True)
        scale[...] = own / jnp.where(total > 0, total, 1.0)

    @pl.when(step < ff_tiles)
    def _():
        gate_proj = mm(h_all[...], gate_c[...])
        up_proj = mm(h_all[...], up_c[...])
        grad_hidden = mm_t(g_all[...], down_r[...])
        at = pl.ds(pl.multiple_of(step * wide, wide), wide)
        sigmoid = jax.nn.sigmoid(gate_proj)
        turned = gate_proj * sigmoid
        hidden = turned * up_proj
        dots[...] += jnp.sum(hidden * grad_hidden, axis=-1, keepdims=True)
        weighted = grad_hidden * scale[...]
        hid_all[:, at] = (hidden * scale[...]).astype(BF16)
        gu_all[:, at] = (weighted * turned).astype(BF16)
        gg_all[:, at] = (weighted * up_proj * (sigmoid + turned * (1.0 - sigmoid))).astype(BF16)

    @pl.when(step >= ff_tiles)
    def _():
        back = (mm_t(gg_all[...], gate_r[...]) + mm_t(gu_all[...], up_r[...])).astype(BF16)
        made = mm(hid_all[...], down_c[...]).astype(BF16)
        at = pl.multiple_of((step - ff_tiles) * out_wide, out_wide)
        behind = pl.multiple_of(at + width + marks.shape[1], 128)
        for core in range(2):
            results[core][:, pl.ds(at, out_wide)] = back[core * half : (core + 1) * half]
            results[core][:, pl.ds(behind, out_wide)] = made[core * half : (core + 1) * half]

    @pl.when(step == ff_tiles)
    def _():
        high = dots[...].astype(BF16).astype(F32)
        tagged = (high * marks[1:2, :] + (dots[...] - high) * marks[2:3, :]).astype(BF16)
        for core in range(2):
            results[core][:, width : width + marks.shape[1]] = tagged[core * half : (core + 1) * half]


def expert_step(j, steps, h_in, g_in, gate, up, down, router, picks, marks, joined):
    chips, (deep, width), ff = len(h_in) - 1, h_in[0].shape, down.shape[0]
    rows, extra = chips * deep, marks.shape[1]
    half = rows // 2
    ff_tile, out_tile = min(256, ff), min(512, width)
    ff_tiles, out_tiles = ff // ff_tile, width // out_tile
    first = lambda i: jnp.minimum(i, ff_tiles - 1)
    second = lambda i: jnp.maximum(i - ff_tiles, 0)
    whole = lambda shape: pl.BlockSpec(shape, lambda i: (0, 0))
    here = lambda n: pl.BlockSpec((rows, n), lambda i: (j, 0))
    in_specs = ([whole((deep, width))] * chips + [whole((half, width))]) * 2 + [
        pl.BlockSpec((width, ff_tile), lambda i: (0, first(i))),
        pl.BlockSpec((width, ff_tile), lambda i: (0, first(i))),
        pl.BlockSpec((ff_tile, width), lambda i: (first(i), 0)),
        pl.BlockSpec((out_tile, ff), lambda i: (second(i), 0)),
        pl.BlockSpec((out_tile, ff), lambda i: (second(i), 0)),
        pl.BlockSpec((ff, out_tile), lambda i: (0, second(i))),
        whole(router.shape),
        pl.BlockSpec((rows, picks.shape[1]), lambda i: (j, 0)),
        whole(marks.shape),
    ]
    args = [*h_in, *g_in, gate, up, down, gate, up, down, router, picks, marks]
    aliases = {}
    if joined:
        aliases = {len(args) + i: 2 + i for i in range(len(joined))}
        args += joined
        in_specs += [pl.BlockSpec(memory_space=pl.ANY)] * len(joined)
    got = pl.pallas_call(
        lambda *refs: expert_kernel(chips, ff_tiles, len(args), *refs),
        grid=(ff_tiles + out_tiles,),
        in_specs=in_specs,
        out_specs=[whole((half, 2 * width + extra))] * 2
        + [here(width), here(width), here(ff), here(ff), here(ff)],
        out_shape=[jax.ShapeDtypeStruct((half, 2 * width + extra), BF16)] * 2
        + [jax.ShapeDtypeStruct((steps * rows, n), BF16) for n in (width, width, ff, ff, ff)],
        scratch_shapes=[pltpu.VMEM((rows, 1), F32), pltpu.VMEM((rows, 1), F32)],
        input_output_aliases=aliases,
        compiler_params=pltpu.CompilerParams(vmem_limit_bytes=VMEM_MOST),
        cost_estimate=LIGHT,
        name="expert",
    )(*args)
    return got[:2], list(got[2:])


def picks_kernel(capacity, own, routes, upto, out):
    top, sources, rows = routes.shape
    lanes = out.shape[1]
    hits = jnp.zeros((sources, rows), F32)
    for i in range(top):
        hits = hits + (routes[i] == own[0:1, 0:1]).astype(F32)
    rank = jnp.where(hits > 0, mm(hits.astype(BF16), upto[...]) - 1.0, -1.0)
    slot = lax.broadcasted_iota(jnp.int32, (capacity, rows), 0).astype(F32)
    lane = lax.broadcasted_iota(jnp.int32, (lanes, rows), 0)
    for source in range(sources):
        table = (rank[source : source + 1] == slot).astype(BF16)
        named = jnp.zeros((lanes, rows), F32)
        for i in range(top):
            named = named + (routes[i, source : source + 1, :] == lane).astype(F32)
        out[source * capacity : (source + 1) * capacity, :] = mm_t(table, named.astype(BF16)).astype(BF16)


def pick_rows(own, routes, upto, capacity, lanes):
    return pl.pallas_call(
        lambda *refs: picks_kernel(capacity, *refs),
        out_shape=jax.ShapeDtypeStruct((routes.shape[1] * capacity, lanes), BF16),
        compiler_params=pltpu.CompilerParams(vmem_limit_bytes=VMEM_MOST),
        cost_estimate=LIGHT,
        name="picks",
    )(own, routes, upto)


def product_kernel(kind, dtype, a, b, *rest):
    out = rest[-1]
    dims = {"nn": ((1,), (0,)), "nt": ((1,), (1,)), "tn": ((0,), (0,))}[kind]
    made = lax.dot_general(a[...], b[...], (dims, ((), ())), preferred_element_type=F32)
    if len(rest) == 2:
        made = made + rest[0][...].astype(F32)
    out[...] = made.astype(dtype)


def product(a, b, kind, dtype, tile, plus=None):
    m, n = a.shape[1 if kind == "tn" else 0], b.shape[0 if kind == "nt" else 1]
    tile = min(tile, m if kind == "tn" else n)
    whole = lambda v: pl.BlockSpec(v.shape, lambda i: (0, 0))
    if kind == "tn":
        specs = [pl.BlockSpec((a.shape[0], tile), lambda i: (0, i)), whole(b)]
        out_spec = pl.BlockSpec((tile, n), lambda i: (i, 0))
    else:
        b_spec = pl.BlockSpec((b.shape[0], tile), lambda i: (0, i))
        if kind == "nt":
            b_spec = pl.BlockSpec((tile, b.shape[1]), lambda i: (i, 0))
        specs = [whole(a), b_spec]
        out_spec = pl.BlockSpec((m, tile), lambda i: (0, i))
    args = [a, b] if plus is None else [a, b, plus]
    return pl.pallas_call(
        lambda *refs: product_kernel(kind, dtype, *refs),
        grid=((m if kind == "tn" else n) // tile,),
        in_specs=specs if plus is None else [*specs, out_spec],
        out_specs=out_spec,
        out_shape=jax.ShapeDtypeStruct((m, n), dtype),
        compiler_params=pltpu.CompilerParams(vmem_limit_bytes=VMEM_MOST),
        cost_estimate=LIGHT,
        name="product",
    )(*args)


def second_norm_kernel(held, arrived, x, gain, resid, normed, scale):
    total = x[...].astype(F32) + held[...] + arrived[...].astype(F32)
    factor = lax.rsqrt(jnp.mean(total * total, axis=-1, keepdims=True) + EPSILON)
    resid[...] = total
    normed[...] = (total * factor * gain[...]).astype(BF16)
    scale[...] = factor


def route_kernel(experts, h, router_weight, picker, router, gates, total):
    logits = mm(h[...], router_weight[...])
    real = lax.broadcasted_iota(jnp.int32, logits.shape, 1) < experts
    logits = jnp.where(real, logits, -1e30)
    shifted = jnp.where(real, jnp.exp(logits - jnp.max(logits, axis=-1, keepdims=True)), 0.0)
    probs = shifted / jnp.sum(shifted, axis=-1, keepdims=True)
    picked = picker[...] * probs
    picked_total = jnp.sum(picked, axis=-1, keepdims=True)
    router[...] = probs
    gates[...] = picked / picked_total
    total[...] = picked_total


def norm_back(v, scale, gain, dy):
    lifted = gain * dy
    inner = jnp.mean(v * lifted, axis=-1, keepdims=True)
    return scale * lifted - v * (scale * scale * scale * inner), jnp.sum(v * scale * dy, axis=0, keepdims=True)


def second_back_kernel(experts, n_homes, n_whole, *refs):
    homes = refs[:n_homes]
    gates, router, picker, total, router_weight, resid, scale, gain, grad_out = refs[n_homes : n_homes + 9]
    grad_resid, low, logit_low, gain_part = refs[n_homes + 9 :]
    width, lanes = resid.shape[1], router.shape[1]
    arrived = homes[0][...]
    for home in homes[1 : 1 + n_whole]:
        arrived = arrived + home[...].astype(F32)
    for upper, lower in zip(homes[1 + n_whole :: 2], homes[2 + n_whole :: 2]):
        arrived = arrived + jnp.where(pl.program_id(0) == 0, upper[...].astype(F32), lower[...].astype(F32))
    tags = arrived[:, width:]
    if tags.shape[1] == lanes:
        dots = tags + pltpu.roll(tags, lanes - experts, 1)
    else:
        dots = tags[:, :lanes] + tags[:, lanes : 2 * lanes]
    probs, chosen = router[...], picker[...]
    dots = jnp.where(chosen > 0, dots, 0.0)
    grad_pick = chosen * (dots - jnp.sum(dots * gates[...], axis=-1, keepdims=True)) / total[...]
    grad_logits = probs * (grad_pick - jnp.sum(probs * grad_pick, axis=-1, keepdims=True))
    logit_low[...] = grad_logits.astype(BF16)
    grad_two = arrived[:, :width] + mm_t(grad_logits.astype(BF16), router_weight[...])
    back, part = norm_back(resid[...], scale[...], gain[...], grad_two)
    back = back + grad_out[...].astype(F32)
    grad_resid[...] = back
    low[...] = back.astype(BF16)
    gain_part[...] = jnp.where(pl.program_id(0) == 0, 0.0, gain_part[...]) + part


def first_back_kernel(held, arrived, x, scale, gain, grad_resid, input_grad, gain_part):
    dy = held[...] + arrived[...].astype(F32)
    back, part = norm_back(x[...].astype(F32), scale[...], gain[...], dy)
    input_grad[...] = grad_resid[...] + back
    gain_part[...] = jnp.where(pl.program_id(0) == 0, 0.0, gain_part[...]) + part


def by_rows(kernel, args, outs, name, step=128):
    rows = args[0].shape[0]

    def spec(shape):
        if shape[0] == rows:
            return pl.BlockSpec((step, shape[1]), lambda i: (i, 0))
        return pl.BlockSpec(shape, lambda i: (0, 0))

    return pl.pallas_call(
        kernel,
        grid=(rows // step,),
        in_specs=[spec(v.shape) for v in args],
        out_specs=[spec(v.shape) for v in outs],
        out_shape=outs,
        compiler_params=pltpu.CompilerParams(vmem_limit_bytes=VMEM_MOST),
        cost_estimate=LIGHT,
        name=name,
    )(*args)


def layer(
    nctx, nep,
    layer_input, attn_gain, q_weight, key_matrix, value_matrix, o_weight, q_gain, key_norm_gain,
    ffn_gain, router_weight, gate_weight, up_weight, down_weight, routes, out_grad,
):
    rows, width = layer_input.shape[1:]
    devices = nctx * nep
    nz = nep // 2
    np_ = nctx * 2
    nb = nctx
    experts = devices
    capacity = -(-rows * TOP * 5 // (4 * experts) // 16) * 16
    length = rows * nctx
    heads = QUERY_HEADS // nctx
    q_cols = heads * HEAD_DIM
    at_ctx = lax.axis_index("ctx")
    at_ep = lax.axis_index("ep")

    due = {}
    clock = 0

    def after(v, *done):
        return lax.optimization_barrier((v, *done))[0] if done else v

    def now(v):
        return after(v, *due.get(clock, []))

    def tick():
        nonlocal clock
        clock += 1

    def swap(v, by_ctx, by_ep, rounds=1):
        if by_ctx == 0 and by_ep == 0:
            return v
        pairs = [(i, ((i // nep) ^ by_ctx) * nep + ((i % nep) ^ by_ep)) for i in range(devices)]
        got = lax.ppermute(now(v) if rounds else v, AXES, pairs)
        if rounds:
            due.setdefault(clock + rounds, []).append(got)
        return got

    def did(v):
        due.setdefault(clock + 1, []).append(v)
        return v

    def swap_z(v, j, rounds=1):
        return swap(v, 0, 2 * j, rounds)

    def sum_all(v):
        bits = [(1 << b, 0) for b in range(nctx.bit_length() - 1)] + [(0, 1 << b) for b in range(nep.bit_length() - 1)]
        for by_ctx, by_ep in bits:
            v = v + swap(v, by_ctx, by_ep, 0)
        return v

    def place(pieces, at, axis=0):
        size = pieces[0].shape[axis]
        shape = list(pieces[0].shape)
        shape[axis] = size * len(pieces)
        whole = after(jnp.zeros(shape, pieces[0].dtype), pieces[-1])
        for i, piece in enumerate(pieces):
            whole = lax.dynamic_update_slice_in_dim(whole, piece, at(i) * size, axis)
        return whole

    def place_ep(far, near):
        return place([v for j in range(nz) for v in (far[j], near[j])], lambda i: at_ep ^ i)

    def own_rows(v, m):
        return lax.dynamic_slice_in_dim(v, (at_ctx ^ m) * rows, rows, 0)

    z_first, z_second = range(1, nz // 2 + 1), range(nz // 2 + 1, nz)
    groups = [list(range(q * nz // 4, (q + 1) * nz // 4)) for q in range(4)]

    x = layer_input[0].astype(F32)
    scale_one = lax.rsqrt(jnp.mean(x * x, axis=-1, keepdims=True) + EPSILON)
    h_one = (x * scale_one * attn_gain).astype(BF16)
    o_cols = width // nctx
    o_piece = lax.dynamic_slice_in_dim(o_weight, at_ctx * o_cols, o_cols, 1)
    qkv_piece = jnp.concatenate(
        [
            lax.dynamic_slice_in_dim(q_weight, at_ctx * q_cols, q_cols, 1),
            lax.dynamic_slice_in_dim(key_matrix, at_ctx * HEAD_DIM, HEAD_DIM, 1),
            lax.dynamic_slice_in_dim(value_matrix, at_ctx * HEAD_DIM, HEAD_DIM, 1),
        ],
        axis=1,
    )
    router_deep = router_weight.size // o_cols
    o_deep = o_piece.shape[0]
    o_piece = jnp.concatenate([o_piece, router_weight.reshape(router_deep, o_cols)])
    far_o, near_o, far_w, near_w = {0: o_piece}, {}, {0: qkv_piece}, {}
    for j in z_first:
        far_o[j] = swap_z(o_piece, j)
    near_o[0] = swap(o_piece, 0, 1)
    near_w[0] = swap(qkv_piece, 0, 1)
    h_pieces = [h_one, None, swap(h_one, 2, 0, 3), None]
    routes_t = routes[0].T
    there = [routes_t] + [None] * (nz - 1)
    for j in groups[1]:
        there[j] = swap_z(routes_t, j)
    tick()

    for j in z_second:
        far_o[j] = swap_z(o_piece, j)
    for j in z_first:
        near_o[j] = swap(far_o[j], 0, 1)
    h_pieces[1] = swap(h_one, 1, 0)
    for j in groups[2]:
        there[j] = swap_z(routes_t, j)
    tick()

    for j in z_first:
        far_w[j] = swap_z(qkv_piece, j)
    for j in z_second:
        near_o[j] = swap(far_o[j], 0, 1)
    for j in groups[0][1:] + groups[3]:
        there[j] = swap_z(routes_t, j)
    tick()

    h_pieces[3] = swap(h_pieces[2], 1, 0)
    for j in z_second:
        far_w[j] = swap_z(qkv_piece, j)
    for j in z_first:
        near_w[j] = swap(far_w[j], 0, 1)
    o_all = now(place_ep(far_o, near_o)).reshape(nep, o_deep + router_deep, o_cols)
    o_part_of = nep // nctx

    def o_block(m):
        block = lax.dynamic_slice(o_all, ((at_ctx ^ m) * o_part_of, 0, 0), (o_part_of, o_deep, o_cols))
        return block.reshape(q_cols, o_cols)

    o_pieces = {0: o_block(0), 2: swap(o_block(2), 2, 0)}
    router_full = o_all[:, o_deep:].reshape(width, experts)
    token = jnp.arange(rows, dtype=jnp.int32)
    upto = (token[:, None] <= token[None, :]).astype(BF16)
    slots = jnp.arange(capacity, dtype=jnp.int32).astype(F32)

    def slot_table(hits):
        rank = mm(hits.astype(BF16), upto) - 1.0
        return ((rank[:, None, :] == slots[None, :, None]) & (hits[:, None, :] > 0)).astype(BF16)

    places = jnp.arange(np_, dtype=jnp.int32)
    plane_experts = (at_ctx ^ (places >> 1 & ~1) ^ (places & 1)) * nep + (at_ep ^ (places >> 1 & 1))
    tables = []
    for j in range(nz):
        hits = jnp.sum((now(there[j])[None] == plane_experts[:, None, None]).astype(F32), axis=1)
        tables.append(slot_table(hits).reshape(np_ * capacity, rows))
    lane_ids = jnp.arange(-(-experts // 128) * 128, dtype=jnp.int32)
    picker = jnp.sum((routes[0][:, :, None] == lane_ids).astype(F32), axis=1)

    def pick(far, q):
        return {j: [did(v) for v in select(tables[j], [now(v) for v in far[j]], nb)] for j in groups[q]}

    def fetch(v, far, q, *parts):
        half = width // 2
        for j in groups[q]:
            if j and len(parts) == 2:
                far[j] = [swap_z(v, j)]
            elif j:
                far.setdefault(j, []).append(swap_z(v[:, parts[0] * half : (parts[0] + 1) * half], j))

    def post(pieces, got, q, *bs, rounds=1):
        for j in groups[q]:
            for b in bs:
                got.setdefault(j, [pieces[j][0]] + [None] * (nb - 1))[b] = swap(pieces[j][b], b & ~1, b & 1, rounds)

    def share(got, q):
        half = np_ * capacity // 2 // nb
        for j in groups[q]:
            got[j].append(swap(jnp.concatenate([v[half:] for v in got[j]], axis=0), 1, 0))

    def share_back(made, q):
        for j in groups[q]:
            made[j] = [made[j][0], swap(made[j][1], 1, 0)]

    def packed(made, q):
        for j in groups[q]:
            copies[j], outs[j] = pack(now(made[j][0]), made[j][1], nb, width)
            did(copies[j][0])

    def gather(pieces, q, shares=2):
        total = {}
        for j in groups[q]:
            ready = [now(pieces[j][0]), *pieces[j][1:]]
            total[j] = combine(tables[j], ready, BF16, shares) if j else combine(tables[j], ready, F32, 1)
            for v in total[j]:
                did(v)
        return total

    def home(total, kept, part, rounds=1):
        for j, v in total.items():
            if j:
                kept.setdefault(j, [None] * len(v))[part] = swap_z(v[part], j, rounds)
            else:
                kept[j] = v

    grad_out = out_grad[0]
    far_g, got_g = {0: [grad_out]}, {}
    tick()

    for j in z_second:
        near_w[j] = swap(far_w[j], 0, 1)
    fetch(grad_out, far_g, 2, 0)
    fetch(grad_out, far_g, 0, 0, 1)
    picked_g0 = pick(far_g, 0)
    frequency = ROPE_BASE ** (-jnp.arange(HEAD_DIM // 2).astype(F32) * 2.0 / HEAD_DIM)
    angles = jnp.arange(length).astype(F32)[:, None] * frequency[None, :]
    cosine, sine = jnp.cos(angles), jnp.sin(angles)
    cos_full = jnp.concatenate([cosine, cosine], axis=1)
    sin_full = jnp.concatenate([-sine, sine], axis=1)
    q_gain_row, k_gain_row = q_gain[None, :], key_norm_gain[None, :]
    h_full = place(h_pieces, lambda i: at_ctx ^ i)
    flat_routes = now(jnp.concatenate(there))
    plane_routes = [flat_routes] + [swap(flat_routes, b & ~1, b & 1) for b in range(1, nb)]
    tick()

    o_pieces[3] = swap(o_block(3), 3, 0)
    o_pieces[1] = swap(o_block(1), 1, 0)
    post(picked_g0, got_g, 0, 1)
    fetch(grad_out, far_g, 2, 1)
    fetch(grad_out, far_g, 3, 0)
    qkv_weight = place_ep(far_w, near_w)
    qkv = mm(h_full, now(qkv_weight))
    attn, turned_q, turned_k, lse = attend(qkv, cos_full, sin_full, q_gain_row, k_gain_row, heads)
    did(attn)
    tick()

    router_wide = jnp.pad(router_full, ((0, 0), (0, lane_ids.shape[0] - experts)))
    fetch(grad_out, far_g, 3, 1)
    picked_g2 = pick(far_g, 2)
    o_rows = place([o_pieces[m] for m in range(nctx)], lambda i: at_ctx ^ i, 1)
    attn = now(attn)
    held = {}
    for hi in reversed(range(0, nctx, 2)):
        sent = swap(mm(own_rows(attn, hi + 1), o_rows).astype(BF16), 1, 0)
        held[hi] = did(mm(own_rows(attn, hi), o_rows) + sent.astype(F32))
    branch_far = swap(held[2].astype(BF16), 2, 0)
    tick()

    post(picked_g0, got_g, 0, 2, 3)
    post(picked_g2, got_g, 2, 1)
    shape = jax.ShapeDtypeStruct
    resid, h_two, scale_two = by_rows(
        second_norm_kernel,
        [held[0], now(branch_far), layer_input[0], ffn_gain[None]],
        [shape((rows, width), F32), shape((rows, width), BF16), shape((rows, 1), F32)],
        "second_norm",
    )
    far_h, got_h = {0: [h_two]}, {}
    fetch(h_two, far_h, 2, 0)
    fetch(h_two, far_h, 0, 0, 1)
    picked_h = pick(far_h, 0)
    tick()

    post(picked_h, got_h, 0, 1, 2, 3)
    share(got_g, 0)
    fetch(h_two, far_h, 2, 1)
    here_routes = now(jnp.stack(plane_routes))
    all_routes = jnp.stack([here_routes, swap(here_routes, 1, 0)])
    picked_g3 = pick(far_g, 3)
    gate, up, down = gate_weight[0], up_weight[0], down_weight[0]
    results, copies, outs, joined = {}, {}, {}, None

    def expert(q):
        nonlocal joined
        for j in groups[q]:
            h_in = [now(got_h[j][0]), *got_h[j][1:]]
            results[j], joined = expert_step(
                j, nz, h_in, got_g[j], gate, up, down, router_wide, picks, marks, joined
            )
            did(results[j][0])

    tick()

    post(picked_g2, got_g, 2, 2, 3)
    post(picked_g3, got_g, 3, 1)
    fetch(h_two, far_h, 3, 0)
    share(got_h, 0)
    picked_h2 = pick(far_h, 2)
    at_device = at_ctx * nep + at_ep
    all_routes = now(all_routes).reshape(2, nb, nz, TOP, rows).transpose(3, 2, 0, 1, 4)
    all_routes = all_routes.reshape(TOP, devices, rows)
    own_id = jnp.full((1, 128), at_device, jnp.int32)
    picks = did(pick_rows(own_id, all_routes, upto, capacity, lane_ids.shape[0]))
    extra = -(-2 * experts // 128) * 128
    extra_ids = jnp.arange(extra, dtype=jnp.int32)
    marks = jnp.stack([extra_ids == at_device, extra_ids == at_device, extra_ids == at_device + experts]).astype(F32)
    lanes = lane_ids.shape[0]
    router, gates, picked_total = by_rows(
        lambda *refs: route_kernel(experts, *refs),
        [now(h_two), router_wide, picker],
        [shape((rows, lanes), F32), shape((rows, lanes), F32), shape((rows, 1), F32)],
        "route",
    )
    did(gates)
    tick()
    post(picked_h2, got_h, 2, 1, 2, 3)
    share(got_g, 2)
    fetch(h_two, far_h, 3, 1)
    expert(0)
    tick()
    post(picked_g3, got_g, 3, 2, 3)
    fetch(grad_out, far_g, 1, 0, 1)
    picked_h3 = pick(far_h, 3)
    share(got_h, 2)
    share_back(results, 0)
    tick()
    post(picked_h3, got_h, 3, 1, 2, 3)
    share(got_g, 3)
    fetch(h_two, far_h, 1, 0, 1)
    picked_g1 = pick(far_g, 1)
    expert(2)
    tick()
    post(picked_g1, got_g, 1, 1, 2, 3)
    share(got_h, 3)
    share_back(results, 2)
    picked_h1 = pick(far_h, 1)
    packed(results, 0)
    tick()
    post(picked_h1, got_h, 1, 1, 2, 3)
    share(got_g, 1)
    expert(3)
    packed(results, 2)
    back, made = {}, {}
    tick()

    post(copies, back, 2, 1, 2, 3)
    share(got_h, 1)
    share_back(results, 3)
    packed(results, 3)
    tick()
    post(copies, back, 3, 1, 2, 3)
    total_2 = gather(back, 2)
    homes = {}
    home(total_2, homes, 0)
    for j in groups[1]:
        got_h[j][0] = after(got_h[j][0], *total_2[groups[2][-1]])
    expert(1)
    tick()
    post(copies, back, 0, 1, 2, 3)
    home(total_2, homes, 1)
    total_3 = gather(back, 3)
    share_back(results, 1)
    packed(results, 1)
    joined_h, joined_g, hidden_all, grad_gate_all, grad_up_all = joined
    gate_part = did(product(joined_h, now(grad_gate_all), "tn", F32, 512))
    tick()
    post(copies, back, 1, 1, 2, 3)
    home(total_3, homes, 0)
    total_0 = gather(back, 0, 1)
    up_part = did(product(joined_h, now(grad_up_all), "tn", F32, 512))
    tick()

    home(total_3, homes, 1)
    home(gather(back, 1, 1), homes, 0)
    home(total_0, homes, 0)
    post(outs, made, 3, 1, 2, 3)
    down_part = did(product(now(hidden_all), joined_g, "tn", F32, 256))
    tick()

    post(outs, made, 2, 1, 2, 3, rounds=2)
    whole = [homes[j][0] for j in sorted(homes) if j and len(homes[j]) == 1]
    homes = [now(homes[0][0]), *whole, *[v for j in sorted(homes) if len(homes[j]) == 2 for v in homes[j]]]
    grad_resid, low, logit_low, ffn_gain_part = by_rows(
        lambda *refs: second_back_kernel(experts, len(homes), len(whole), *refs),
        [*homes, gates, router, picker, picked_total, router_wide, resid, scale_two, ffn_gain[None], grad_out],
        [shape((rows, width), F32), shape((rows, width), BF16), shape((rows, lanes), BF16), shape((1, width), F32)],
        "second_back",
    )
    did(low)
    homes = {}
    total_3 = gather(made, 3)
    home(total_3, homes, 0)
    tick()
    low_pieces = [low, swap(low, 1, 0), swap(low, 2, 0), None]
    home(total_3, homes, 1)
    tick()
    low_pieces[3] = swap(low_pieces[2], 1, 0)
    total_2 = gather(made, 2)
    tick()

    post(outs, made, 1, 1, 2, 3)
    home(total_2, homes, 0)
    branch_full = now(place(low_pieces, lambda i: at_ctx ^ i))
    o_own = q_cols // nep
    own_width = width // devices
    o_part = product(attn, branch_full, "tn", F32, 256)
    router_part = t_mm(logit_low, h_two)[:experts].reshape(experts, nctx, nep, own_width)
    router_rows = experts * nctx * own_width // width

    def o_term(j, ry):
        place_of = at_ep ^ (2 * j + ry)
        block = lax.dynamic_slice_in_dim(o_part, place_of * o_own, o_own, 0)
        router_block = lax.dynamic_slice_in_dim(router_part, place_of, 1, 2).reshape(router_rows, width)
        return jnp.concatenate([block, router_block], axis=0)

    last_steps = list(reversed(range(nz)))
    o_sent = {j: did(o_term(j, 1).astype(BF16)) for j in last_steps}
    grad_attn = did(product(branch_full, o_rows, "nt", BF16, 512))
    tick()

    o_near = {j: swap(o_sent[j], 0, 1) for j in last_steps}
    home(total_2, homes, 1)
    total_1 = gather(made, 1, 1)
    grad_qkv, q_gain_part, k_gain_part = attend_back(
        qkv, turned_q, turned_k, attn, lse, now(grad_attn), cos_full, sin_full, q_gain_row, k_gain_row, heads
    )
    did(grad_qkv)
    tick()

    post(outs, made, 0, 1, 2, 3)
    o_far = {}
    o_mid = {j: (o_term(j, 0) + now(o_near[j]).astype(F32)).astype(BF16) for j in last_steps[:-1]}
    for j in last_steps[: nz // 4]:
        o_far[j] = swap_z(o_mid[j], j)
    qkv_part = product(h_full, now(grad_qkv), "tn", F32, 512).reshape(nctx, nep, own_width, -1)

    def qkv_term(j, ry):
        return lax.dynamic_slice_in_dim(qkv_part, at_ep ^ (2 * j + ry), 1, 1)[:, 0]

    qkv_sent = {j: did(qkv_term(j, 1).astype(BF16)) for j in last_steps}
    one_term = lambda m, plus, dtype: product(
        own_rows(grad_qkv, m), qkv_weight, "nt", dtype, 1024, plus
    )
    sent = [did(one_term(m, None, BF16)) for m in (3, 1)]
    tick()

    first_steps, other_steps = last_steps[::2], last_steps[1::2]
    qkv_near = {j: swap(qkv_sent[j], 0, 1) for j in first_steps}
    sent = [swap(v, 1, 0) for v in sent]
    for j in last_steps[nz // 4 : -1]:
        o_far[j] = swap_z(o_mid[j], j)
    held = [did(one_term(0, sent[1], F32)), did(one_term(2, sent[0], BF16))]
    tick()

    qkv_near.update({j: swap(qkv_sent[j], 0, 1) for j in other_steps})
    one_far = swap(held[1], 2, 0)
    qkv_mid = lambda j: (qkv_term(j, 0) + now(qkv_near[j]).astype(F32)).astype(BF16)
    qkv_far = {j: swap_z(qkv_mid(j), j) for j in last_steps[: nz // 4]}
    home(total_1, homes, 0)
    total_0 = gather(made, 0, 1)
    o_sum = o_term(0, 0) + o_near[0].astype(F32)
    for j in range(1, nz):
        o_sum = o_sum + now(o_far[j]).astype(F32)
    o_grad = did(o_sum[:o_own])
    router_sum = did(o_sum[o_own:].reshape(experts, nctx, own_width).transpose(1, 2, 0))
    tick()

    qkv_far.update({j: swap_z(qkv_mid(j), j) for j in last_steps[nz // 4 : -1]})
    home(total_0, homes, 0)
    input_grad, attn_gain_part = by_rows(
        first_back_kernel,
        [held[0], now(one_far), layer_input[0], scale_one, attn_gain[None], grad_resid],
        [shape((rows, width), F32), shape((1, width), F32)],
        "first_back",
    )
    did(input_grad)
    tick()

    qkv_sum = qkv_term(0, 0) + qkv_near[0].astype(F32)
    for j in range(1, nz):
        qkv_sum = qkv_sum + now(qkv_far[j]).astype(F32)
    last = jnp.concatenate([qkv_sum, router_sum], axis=2).astype(BF16)
    last_block = lambda m: lax.dynamic_index_in_dim(last, at_ctx ^ m, 0)
    last = place([swap(last_block(m), m, 0) for m in range(nctx)], lambda i: at_ctx ^ i).astype(F32)
    late = sum_all(jnp.concatenate([attn_gain_part[0], ffn_gain_part[0], q_gain_part[0], k_gain_part[0]]))
    qkv_grad = last
    router_grad = jnp.sum(last[:, :, q_cols + 2 * HEAD_DIM :], axis=0)
    mixed = resid
    for j in sorted(homes):
        mixed = mixed + jnp.concatenate(homes[j]).astype(F32)

    def columns(first, last):
        return jnp.concatenate([qkv_grad[c, :, first:last] for c in range(nctx)], axis=1)

    return (
        mixed.astype(BF16)[None],
        input_grad[None],
        late[:width],
        columns(0, q_cols),
        columns(q_cols, q_cols + HEAD_DIM),
        columns(q_cols + HEAD_DIM, q_cols + 2 * HEAD_DIM),
        o_grad,
        late[2 * width : 2 * width + HEAD_DIM],
        late[2 * width + HEAD_DIM :],
        late[width : 2 * width],
        router_grad,
        gate_part[None],
        up_part[None],
        down_part[None],
    )


def solution(mesh):
    nctx, nep = mesh.shape["ctx"], mesh.shape["ep"]
    tokens = P("ep", "ctx", None)
    own = P(("ctx", "ep"), None)
    expert = P(("ctx", "ep"), None, None)
    split_rows = P("ep", None)

    def on_device(*arrays):
        return layer(nctx, nep, *arrays)

    return jax.shard_map(
        on_device,
        mesh=mesh,
        in_specs=(
            tokens, P(), split_rows, split_rows, split_rows, split_rows, P(), P(), P(), split_rows,
            expert, expert, expert, tokens, tokens,
        ),
        out_specs=(
            tokens, tokens, P(), own, own, own, own, P(), P(), P(), own, expert, expert, expert,
        ),
        check_vma=False,
    )
```

```python
import math

import jax
import jax.numpy as jnp
from jax import lax
from jax.experimental import pallas as pl
from jax.experimental.pallas import tpu as pltpu
from jax.sharding import PartitionSpec as P

QUERY_HEADS = 32
KEY_VALUE_HEADS = 4
HEAD_DIM = 128
TOP = 8
BLOCK = 256

EPSILON = 1e-06
ROPE_BASE = 1000000.0
LOG2_E = 1.4426950408889634
F32 = jnp.float32
BF16 = jnp.bfloat16
AXES = ("ctx", "ep")
HIGHEST = lax.Precision.HIGHEST


def mm(a, b):
    return jnp.dot(a, b, preferred_element_type=F32)


def mm_t(a, b):
    return lax.dot_general(a, b, (((1,), (1,)), ((), ())), preferred_element_type=F32)


def t_mm(a, b):
    return lax.dot_general(a, b, (((0,), (0,)), ((), ())), preferred_element_type=F32)


LIGHT = pl.CostEstimate(flops=1, bytes_accessed=1, transcendentals=0)
VMEM_MOST = 56 * 1024 * 1024


def half_turn(v):
    return pltpu.roll(v, HEAD_DIM // 2, 1)


def head_norm(v, gain):
    scale = lax.rsqrt(jnp.mean(v * v, axis=-1, keepdims=True) + EPSILON)
    return v * scale * gain


def head_norm_back(v, gain, dy):
    scale = lax.rsqrt(jnp.mean(v * v, axis=-1, keepdims=True) + EPSILON)
    lifted = gain * dy
    inner = jnp.mean(v * lifted, axis=-1, keepdims=True)
    return (
        scale * lifted - v * (scale * scale * scale * inner),
        jnp.sum(v * scale * dy, axis=0, keepdims=True),
    )


def diagonal_mask():
    key_at = lax.broadcasted_iota(jnp.int32, (BLOCK, BLOCK), 0)
    query_at = lax.broadcasted_iota(jnp.int32, (BLOCK, BLOCK), 1)
    return key_at <= query_at


def attend_kernel(
    q_ref, k_ref, v_ref, cos_ref, sin_ref, qg_ref, kg_ref,
    out_ref, qr_ref, kr_ref, lse_ref, keys, values_t,
):
    blocks = q_ref.shape[0] // BLOCK
    coefficient = LOG2_E * HEAD_DIM ** (-0.5)

    @pl.when(pl.program_id(0) == 0)
    def _():
        normed = head_norm(k_ref[...], kg_ref[...])
        turned = (normed * cos_ref[...] + half_turn(normed) * sin_ref[...]).astype(BF16)
        keys[...] = turned
        kr_ref[...] = turned
        values_t[...] = v_ref[...].T.astype(BF16)

    normed = head_norm(q_ref[...], qg_ref[...])
    queries = (normed * cos_ref[...] + half_turn(normed) * sin_ref[...]).astype(BF16)
    qr_ref[...] = queries
    visible = diagonal_mask()
    for i in range(blocks):
        low, high = i * BLOCK, (i + 1) * BLOCK
        q_i = queries[low:high]
        s_in = jnp.where(visible, mm_t(keys[low:high, :], q_i) * coefficient, -1e30)
        top = jnp.max(s_in, axis=0, keepdims=True)
        if i:
            s_off = mm_t(keys[:low, :], q_i) * coefficient
            top = jnp.maximum(top, jnp.max(s_off, axis=0, keepdims=True))
        p_in = jnp.exp2(s_in - top)
        total = jnp.sum(p_in, axis=0, keepdims=True)
        mixed = mm(values_t[:, low:high], p_in.astype(BF16))
        if i:
            p_off = jnp.exp2(s_off - top)
            total = total + jnp.sum(p_off, axis=0, keepdims=True)
            mixed = mixed + mm(values_t[:, :low], p_off.astype(BF16))
        out_ref[low:high, :] = (mixed * (1.0 / total)).T.astype(BF16)
        lse_ref[0, :, low:high] = top + jnp.log2(total)


def attend_back_kernel(
    qr_ref, q_ref, do_ref, out_ref, lse_ref, kr_ref, k_ref, v_ref, cos_ref, sin_ref, qg_ref, kg_ref,
    grad_ref, qgain_ref, kgain_ref, keys_t, values, dk, dv, dq,
):
    step = pl.program_id(0)
    heads = pl.num_programs(0) - 2
    blocks = q_ref.shape[0] // BLOCK
    scale = HEAD_DIM ** (-0.5)
    coefficient = LOG2_E * scale

    @pl.when(step == 0)
    def _():
        keys_t[...] = kr_ref[...].astype(F32).T.astype(BF16)
        values[...] = v_ref[...].astype(BF16)
        dk[...] = jnp.zeros_like(dk)
        dv[...] = jnp.zeros_like(dv)
        qgain_ref[...] = jnp.zeros_like(qgain_ref)

    def turn_back(v):
        return v * cos_ref[...] - half_turn(v) * sin_ref[...]

    @pl.when(step < heads)
    def _():
        delta = jnp.sum((do_ref[...].astype(F32) * out_ref[...].astype(F32)).T, axis=0, keepdims=True)
        visible = diagonal_mask()
        for i in range(blocks):
            low, high = i * BLOCK, (i + 1) * BLOCK
            q_i = qr_ref[low:high, :]
            do_i = do_ref[low:high, :]
            lse_i = lse_ref[0, :, low:high]
            delta_i = delta[:, low:high]

            def part(first, last, masked):
                p = jnp.exp2(mm_t(kr_ref[first:last, :], q_i) * coefficient - lse_i)
                if masked:
                    p = jnp.where(visible, p, 0.0)
                dp = mm_t(values[first:last, :], do_i)
                dv[first:last, :] += mm(p.astype(BF16), do_i)
                ds = (p * (dp - delta_i)).astype(BF16)
                dk[first:last, :] += mm(ds, q_i)
                return mm(keys_t[:, first:last], ds)

            turned = part(low, high, True)
            if i:
                turned = turned + part(0, low, False)
            dq[low:high, :] = turned.T * scale
        back, gain_part = head_norm_back(q_ref[...], qg_ref[...], turn_back(dq[...]))
        grad_ref[...] = back.astype(BF16)
        qgain_ref[...] += gain_part

    @pl.when(step == heads)
    def _():
        back, gain_part = head_norm_back(k_ref[...], kg_ref[...], turn_back(dk[...] * scale))
        grad_ref[...] = back.astype(BF16)
        kgain_ref[...] = gain_part

    @pl.when(step == heads + 1)
    def _():
        grad_ref[...] = dv[...].astype(BF16)


def attend(qkv, cos, sin, q_gain, k_gain, heads):
    length = qkv.shape[0]
    column = lambda at: pl.BlockSpec((length, HEAD_DIM), lambda h: (0, at))
    moving = pl.BlockSpec((length, HEAD_DIM), lambda h: (0, h))
    fixed = pl.BlockSpec((length, HEAD_DIM), lambda h: (0, 0))
    row = pl.BlockSpec((1, HEAD_DIM), lambda h: (0, 0))
    return pl.pallas_call(
        attend_kernel,
        grid=(heads,),
        in_specs=[moving, column(heads), column(heads + 1), fixed, fixed, row, row],
        out_specs=[moving, moving, fixed, pl.BlockSpec((1, 1, length), lambda h: (h, 0, 0))],
        out_shape=[
            jax.ShapeDtypeStruct((length, heads * HEAD_DIM), BF16),
            jax.ShapeDtypeStruct((length, heads * HEAD_DIM), BF16),
            jax.ShapeDtypeStruct((length, HEAD_DIM), BF16),
            jax.ShapeDtypeStruct((heads, 1, length), F32),
        ],
        scratch_shapes=[pltpu.VMEM((length, HEAD_DIM), BF16), pltpu.VMEM((HEAD_DIM, length), BF16)],
        compiler_params=pltpu.CompilerParams(vmem_limit_bytes=40 * 1024 * 1024),
        cost_estimate=LIGHT,
        name="attend",
    )(qkv, qkv, qkv, cos, sin, q_gain, k_gain)


def attend_back(qkv, turned_q, turned_k, out, lse, grad_out, cos, sin, q_gain, k_gain, heads):
    length = qkv.shape[0]
    column = lambda at: pl.BlockSpec((length, HEAD_DIM), lambda h: (0, at))
    moving = pl.BlockSpec((length, HEAD_DIM), lambda h: (0, jnp.minimum(h, heads - 1)))
    fixed = pl.BlockSpec((length, HEAD_DIM), lambda h: (0, 0))
    row = pl.BlockSpec((1, HEAD_DIM), lambda h: (0, 0))
    return pl.pallas_call(
        attend_back_kernel,
        grid=(heads + 2,),
        in_specs=[
            moving, moving, moving, moving,
            pl.BlockSpec((1, 1, length), lambda h: (jnp.minimum(h, heads - 1), 0, 0)),
            fixed, column(heads), column(heads + 1), fixed, fixed, row, row,
        ],
        out_specs=[pl.BlockSpec((length, HEAD_DIM), lambda h: (0, h)), row, row],
        out_shape=[
            jax.ShapeDtypeStruct((length, (heads + 2) * HEAD_DIM), BF16),
            jax.ShapeDtypeStruct((1, HEAD_DIM), F32),
            jax.ShapeDtypeStruct((1, HEAD_DIM), F32),
        ],
        scratch_shapes=[
            pltpu.VMEM((HEAD_DIM, length), BF16),
            pltpu.VMEM((length, HEAD_DIM), BF16),
            pltpu.VMEM((length, HEAD_DIM), F32),
            pltpu.VMEM((length, HEAD_DIM), F32),
            pltpu.VMEM((length, HEAD_DIM), F32),
        ],
        compiler_params=pltpu.CompilerParams(vmem_limit_bytes=40 * 1024 * 1024),
        cost_estimate=LIGHT,
        name="attend_back",
    )(turned_q, qkv, grad_out, out, lse, turned_k, qkv, qkv, cos, sin, q_gain, k_gain)


def select_kernel(n_parts, table, *refs):
    parts, outs = refs[:n_parts], refs[n_parts:]
    deep = outs[0].shape[0]
    first = 0
    for part in parts:
        for at in range(0, part.shape[1], 1024):
            wide = min(1024, part.shape[1] - at)
            rows = mm(table[...], part[:, at : at + wide]).astype(BF16)
            for b, out in enumerate(outs):
                out[:, first : first + wide] = rows[b * deep : (b + 1) * deep]
            first += wide


def select(table, parts, chips):
    width, deep = sum(v.shape[1] for v in parts), table.shape[0] // chips
    return pl.pallas_call(
        lambda *refs: select_kernel(len(parts), *refs),
        out_shape=[jax.ShapeDtypeStruct((deep, width), BF16)] * chips,
        compiler_params=pltpu.CompilerParams(vmem_limit_bytes=VMEM_MOST),
        cost_estimate=LIGHT,
        name="select",
    )(table, *parts)


def combine_kernel(n_pieces, table, *refs):
    pieces, outs = refs[:n_pieces], refs[n_pieces:]
    deep, width = outs[0].shape
    for first in range(0, width, 512):
        at = slice(first, min(first + 512, width))
        rows = jnp.concatenate([p[:, at] for p in pieces], axis=0)
        total = t_mm(table[...], rows)
        for i, out in enumerate(outs):
            out[:, at] = total[i * deep : (i + 1) * deep].astype(out.dtype)


def combine(table, pieces, dtype, shares):
    shape = (table.shape[1] // shares, pieces[0].shape[1])
    return pl.pallas_call(
        lambda *refs: combine_kernel(len(pieces), *refs),
        out_shape=[jax.ShapeDtypeStruct(shape, dtype)] * shares,
        compiler_params=pltpu.CompilerParams(vmem_limit_bytes=VMEM_MOST),
        cost_estimate=LIGHT,
        name="combine",
    )(table, *pieces)


def pack_kernel(chips, near, other, *outs):
    deep = outs[0].shape[0] // 2
    first = 0
    for group in (outs[:chips], outs[chips:]):
        at = slice(first, first + group[0].shape[1])
        for b, out in enumerate(group):
            out[:deep, :] = near[b * deep : (b + 1) * deep, at]
            out[deep:, :] = other[b * deep : (b + 1) * deep, at]
        first = at.stop


def pack(near, other, chips, width):
    deep, first = 2 * near.shape[0] // chips, near.shape[1] - width
    got = pl.pallas_call(
        lambda *refs: pack_kernel(chips, *refs),
        out_shape=[jax.ShapeDtypeStruct((deep, n), BF16) for n in (first, width) for _ in range(chips)],
        compiler_params=pltpu.CompilerParams(vmem_limit_bytes=VMEM_MOST),
        cost_estimate=LIGHT,
        name="pack",
    )(near, other)
    return got[:chips], got[chips:]


def expert_kernel(chips, ff_tiles, n_in, *refs):
    h_in, g_in = refs[: chips + 1], refs[chips + 1 : 2 * chips + 2]
    gate_c, up_c, down_r, gate_r, up_r, down_c, router, picks, marks = refs[2 * chips + 2 : 2 * chips + 11]
    results = refs[n_in : n_in + 2]
    h_all, g_all, hid_all, gg_all, gu_all, scale, dots = refs[n_in + 2 :]
    step = pl.program_id(0)
    deep = h_in[0].shape[0] // 2
    half = chips * deep
    wide, out_wide = gate_c.shape[1], down_c.shape[1]
    width = h_in[0].shape[1]

    @pl.when(step == 0)
    def _():
        for arrived, joined in ((h_in, h_all), (g_in, g_all)):
            for b in range(chips):
                joined[b * deep : (b + 1) * deep, :] = arrived[b][:deep, :]
            joined[half:, :] = arrived[chips][...]
        dots[...] = jnp.zeros_like(dots)
        logits = mm(h_all[...], router[...])
        picked = picks[...] > 0
        top = jnp.max(jnp.where(picked, logits, -1e30), axis=-1, keepdims=True)
        weight = jnp.where(picked, jnp.exp(logits - top), 0.0)
        total = jnp.sum(weight, axis=-1, keepdims=True)
        own = jnp.sum(weight * marks[0:1, : logits.shape[1]], axis=-1, keepdims=True)
        scale[...] = own / jnp.where(total > 0, total, 1.0)

    @pl.when(step < ff_tiles)
    def _():
        gate_proj = mm(h_all[...], gate_c[...])
        up_proj = mm(h_all[...], up_c[...])
        grad_hidden = mm_t(g_all[...], down_r[...])
        at = pl.ds(pl.multiple_of(step * wide, wide), wide)
        sigmoid = jax.nn.sigmoid(gate_proj)
        turned = gate_proj * sigmoid
        hidden = turned * up_proj
        dots[...] += jnp.sum(hidden * grad_hidden, axis=-1, keepdims=True)
        weighted = grad_hidden * scale[...]
        hid_all[:, at] = (hidden * scale[...]).astype(BF16)
        gu_all[:, at] = (weighted * turned).astype(BF16)
        gg_all[:, at] = (weighted * up_proj * (sigmoid + turned * (1.0 - sigmoid))).astype(BF16)

    @pl.when(step >= ff_tiles)
    def _():
        back = (mm_t(gg_all[...], gate_r[...]) + mm_t(gu_all[...], up_r[...])).astype(BF16)
        made = mm(hid_all[...], down_c[...]).astype(BF16)
        at = pl.multiple_of((step - ff_tiles) * out_wide, out_wide)
        behind = pl.multiple_of(at + width + marks.shape[1], 128)
        for core in range(2):
            results[core][:, pl.ds(at, out_wide)] = back[core * half : (core + 1) * half]
            results[core][:, pl.ds(behind, out_wide)] = made[core * half : (core + 1) * half]

    @pl.when(step == ff_tiles)
    def _():
        high = dots[...].astype(BF16).astype(F32)
        tagged = (high * marks[1:2, :] + (dots[...] - high) * marks[2:3, :]).astype(BF16)
        for core in range(2):
            results[core][:, width : width + marks.shape[1]] = tagged[core * half : (core + 1) * half]


def expert_step(j, steps, h_in, g_in, gate, up, down, router, picks, marks, joined):
    chips, (deep, width), ff = len(h_in) - 1, h_in[0].shape, down.shape[0]
    rows, extra = chips * deep, marks.shape[1]
    half = rows // 2
    ff_tile, out_tile = min(256, ff), min(512, width)
    ff_tiles, out_tiles = ff // ff_tile, width // out_tile
    first = lambda i: jnp.minimum(i, ff_tiles - 1)
    second = lambda i: jnp.maximum(i - ff_tiles, 0)
    whole = lambda shape: pl.BlockSpec(shape, lambda i: (0, 0))
    here = lambda n: pl.BlockSpec((rows, n), lambda i: (j, 0))
    in_specs = ([whole((deep, width))] * chips + [whole((half, width))]) * 2 + [
        pl.BlockSpec((width, ff_tile), lambda i: (0, first(i))),
        pl.BlockSpec((width, ff_tile), lambda i: (0, first(i))),
        pl.BlockSpec((ff_tile, width), lambda i: (first(i), 0)),
        pl.BlockSpec((out_tile, ff), lambda i: (second(i), 0)),
        pl.BlockSpec((out_tile, ff), lambda i: (second(i), 0)),
        pl.BlockSpec((ff, out_tile), lambda i: (0, second(i))),
        whole(router.shape),
        pl.BlockSpec((rows, picks.shape[1]), lambda i: (j, 0)),
        whole(marks.shape),
    ]
    args = [*h_in, *g_in, gate, up, down, gate, up, down, router, picks, marks]
    aliases = {}
    if joined:
        aliases = {len(args) + i: 2 + i for i in range(len(joined))}
        args += joined
        in_specs += [pl.BlockSpec(memory_space=pl.ANY)] * len(joined)
    got = pl.pallas_call(
        lambda *refs: expert_kernel(chips, ff_tiles, len(args), *refs),
        grid=(ff_tiles + out_tiles,),
        in_specs=in_specs,
        out_specs=[whole((half, 2 * width + extra))] * 2
        + [here(width), here(width), here(ff), here(ff), here(ff)],
        out_shape=[jax.ShapeDtypeStruct((half, 2 * width + extra), BF16)] * 2
        + [jax.ShapeDtypeStruct((steps * rows, n), BF16) for n in (width, width, ff, ff, ff)],
        scratch_shapes=[pltpu.VMEM((rows, 1), F32), pltpu.VMEM((rows, 1), F32)],
        input_output_aliases=aliases,
        compiler_params=pltpu.CompilerParams(vmem_limit_bytes=VMEM_MOST),
        cost_estimate=LIGHT,
        name="expert",
    )(*args)
    return got[:2], list(got[2:])


def picks_kernel(capacity, own, routes, upto, out):
    top, sources, rows = routes.shape
    lanes = out.shape[1]
    hits = jnp.zeros((sources, rows), F32)
    for i in range(top):
        hits = hits + (routes[i] == own[0:1, 0:1]).astype(F32)
    rank = jnp.where(hits > 0, mm(hits.astype(BF16), upto[...]) - 1.0, -1.0)
    slot = lax.broadcasted_iota(jnp.int32, (capacity, rows), 0).astype(F32)
    lane = lax.broadcasted_iota(jnp.int32, (lanes, rows), 0)
    for source in range(sources):
        table = (rank[source : source + 1] == slot).astype(BF16)
        named = jnp.zeros((lanes, rows), F32)
        for i in range(top):
            named = named + (routes[i, source : source + 1, :] == lane).astype(F32)
        out[source * capacity : (source + 1) * capacity, :] = mm_t(table, named.astype(BF16)).astype(BF16)


def pick_rows(own, routes, upto, capacity, lanes):
    return pl.pallas_call(
        lambda *refs: picks_kernel(capacity, *refs),
        out_shape=jax.ShapeDtypeStruct((routes.shape[1] * capacity, lanes), BF16),
        compiler_params=pltpu.CompilerParams(vmem_limit_bytes=VMEM_MOST),
        cost_estimate=LIGHT,
        name="picks",
    )(own, routes, upto)


def product_kernel(kind, dtype, a, b, *rest):
    out = rest[-1]
    dims = {"nn": ((1,), (0,)), "nt": ((1,), (1,)), "tn": ((0,), (0,))}[kind]
    made = lax.dot_general(a[...], b[...], (dims, ((), ())), preferred_element_type=F32)
    if len(rest) == 2:
        made = made + rest[0][...].astype(F32)
    out[...] = made.astype(dtype)


def product(a, b, kind, dtype, tile, plus=None):
    m, n = a.shape[1 if kind == "tn" else 0], b.shape[0 if kind == "nt" else 1]
    tile = min(tile, m if kind == "tn" else n)
    whole = lambda v: pl.BlockSpec(v.shape, lambda i: (0, 0))
    if kind == "tn":
        specs = [pl.BlockSpec((a.shape[0], tile), lambda i: (0, i)), whole(b)]
        out_spec = pl.BlockSpec((tile, n), lambda i: (i, 0))
    else:
        b_spec = pl.BlockSpec((b.shape[0], tile), lambda i: (0, i))
        if kind == "nt":
            b_spec = pl.BlockSpec((tile, b.shape[1]), lambda i: (i, 0))
        specs = [whole(a), b_spec]
        out_spec = pl.BlockSpec((m, tile), lambda i: (0, i))
    args = [a, b] if plus is None else [a, b, plus]
    return pl.pallas_call(
        lambda *refs: product_kernel(kind, dtype, *refs),
        grid=((m if kind == "tn" else n) // tile,),
        in_specs=specs if plus is None else [*specs, out_spec],
        out_specs=out_spec,
        out_shape=jax.ShapeDtypeStruct((m, n), dtype),
        compiler_params=pltpu.CompilerParams(vmem_limit_bytes=VMEM_MOST),
        cost_estimate=LIGHT,
        name="product",
    )(*args)


def second_norm_kernel(held, arrived, x, gain, resid, normed, scale):
    total = x[...].astype(F32) + held[...] + arrived[...].astype(F32)
    factor = lax.rsqrt(jnp.mean(total * total, axis=-1, keepdims=True) + EPSILON)
    resid[...] = total
    normed[...] = (total * factor * gain[...]).astype(BF16)
    scale[...] = factor


def route_kernel(experts, h, router_weight, picker, router, gates, total):
    logits = mm(h[...], router_weight[...])
    real = lax.broadcasted_iota(jnp.int32, logits.shape, 1) < experts
    logits = jnp.where(real, logits, -1e30)
    shifted = jnp.where(real, jnp.exp(logits - jnp.max(logits, axis=-1, keepdims=True)), 0.0)
    probs = shifted / jnp.sum(shifted, axis=-1, keepdims=True)
    picked = picker[...] * probs
    picked_total = jnp.sum(picked, axis=-1, keepdims=True)
    router[...] = probs
    gates[...] = picked / picked_total
    total[...] = picked_total


def norm_back(v, scale, gain, dy):
    lifted = gain * dy
    inner = jnp.mean(v * lifted, axis=-1, keepdims=True)
    return scale * lifted - v * (scale * scale * scale * inner), jnp.sum(v * scale * dy, axis=0, keepdims=True)


def second_back_kernel(experts, n_homes, n_whole, *refs):
    homes = refs[:n_homes]
    gates, router, picker, total, router_weight, resid, scale, gain, grad_out = refs[n_homes : n_homes + 9]
    grad_resid, low, logit_low, gain_part = refs[n_homes + 9 :]
    width, lanes = resid.shape[1], router.shape[1]
    arrived = homes[0][...]
    for home in homes[1 : 1 + n_whole]:
        arrived = arrived + home[...].astype(F32)
    for upper, lower in zip(homes[1 + n_whole :: 2], homes[2 + n_whole :: 2]):
        arrived = arrived + jnp.where(pl.program_id(0) == 0, upper[...].astype(F32), lower[...].astype(F32))
    tags = arrived[:, width:]
    if tags.shape[1] == lanes:
        dots = tags + pltpu.roll(tags, lanes - experts, 1)
    else:
        dots = tags[:, :lanes] + tags[:, lanes : 2 * lanes]
    probs, chosen = router[...], picker[...]
    dots = jnp.where(chosen > 0, dots, 0.0)
    grad_pick = chosen * (dots - jnp.sum(dots * gates[...], axis=-1, keepdims=True)) / total[...]
    grad_logits = probs * (grad_pick - jnp.sum(probs * grad_pick, axis=-1, keepdims=True))
    logit_low[...] = grad_logits.astype(BF16)
    grad_two = arrived[:, :width] + mm_t(grad_logits.astype(BF16), router_weight[...])
    back, part = norm_back(resid[...], scale[...], gain[...], grad_two)
    back = back + grad_out[...].astype(F32)
    grad_resid[...] = back
    low[...] = back.astype(BF16)
    gain_part[...] = jnp.where(pl.program_id(0) == 0, 0.0, gain_part[...]) + part


def first_back_kernel(held, arrived, x, scale, gain, grad_resid, input_grad, gain_part):
    dy = held[...] + arrived[...].astype(F32)
    back, part = norm_back(x[...].astype(F32), scale[...], gain[...], dy)
    input_grad[...] = grad_resid[...] + back
    gain_part[...] = jnp.where(pl.program_id(0) == 0, 0.0, gain_part[...]) + part


def by_rows(kernel, args, outs, name, step=128):
    rows = args[0].shape[0]

    def spec(shape):
        if shape[0] == rows:
            return pl.BlockSpec((step, shape[1]), lambda i: (i, 0))
        return pl.BlockSpec(shape, lambda i: (0, 0))

    return pl.pallas_call(
        kernel,
        grid=(rows // step,),
        in_specs=[spec(v.shape) for v in args],
        out_specs=[spec(v.shape) for v in outs],
        out_shape=outs,
        compiler_params=pltpu.CompilerParams(vmem_limit_bytes=VMEM_MOST),
        cost_estimate=LIGHT,
        name=name,
    )(*args)


def layer(
    nctx, nep,
    layer_input, attn_gain, q_weight, key_matrix, value_matrix, o_weight, q_gain, key_norm_gain,
    ffn_gain, router_weight, gate_weight, up_weight, down_weight, routes, out_grad,
):
    rows, width = layer_input.shape[1:]
    devices = nctx * nep
    nz = nep // 2
    np_ = nctx * 2
    nb = nctx
    experts = devices
    capacity = -(-rows * TOP * 5 // (4 * experts) // 16) * 16
    length = rows * nctx
    heads = QUERY_HEADS // nctx
    q_cols = heads * HEAD_DIM
    at_ctx = lax.axis_index("ctx")
    at_ep = lax.axis_index("ep")

    due = {}
    clock = 0

    def after(v, *done):
        return lax.optimization_barrier((v, *done))[0] if done else v

    def now(v):
        return after(v, *due.get(clock, []))

    def tick():
        nonlocal clock
        clock += 1

    def swap(v, by_ctx, by_ep, rounds=1):
        if by_ctx == 0 and by_ep == 0:
            return v
        pairs = [(i, ((i // nep) ^ by_ctx) * nep + ((i % nep) ^ by_ep)) for i in range(devices)]
        got = lax.ppermute(now(v) if rounds else v, AXES, pairs)
        if rounds:
            due.setdefault(clock + rounds, []).append(got)
        return got

    def did(v):
        due.setdefault(clock + 1, []).append(v)
        return v

    def swap_z(v, j, rounds=1):
        return swap(v, 0, 2 * j, rounds)

    def sum_over(v, bits):
        for by_ctx, by_ep in bits:
            v = v + swap(v, by_ctx, by_ep, 0)
        return v

    def place(pieces, at, axis=0):
        size = pieces[0].shape[axis]
        shape = list(pieces[0].shape)
        shape[axis] = size * len(pieces)
        whole = after(jnp.zeros(shape, pieces[0].dtype), pieces[-1])
        for i, piece in enumerate(pieces):
            whole = lax.dynamic_update_slice_in_dim(whole, piece, at(i) * size, axis)
        return whole

    def place_ep(far, near):
        return place([v for j in range(nz) for v in (far[j], near[j])], lambda i: at_ep ^ i)

    def own_rows(v, m):
        return lax.dynamic_slice_in_dim(v, (at_ctx ^ m) * rows, rows, 0)

    z_first, z_second = range(1, nz // 2 + 1), range(nz // 2 + 1, nz)
    groups = [list(range(q * nz // 4, (q + 1) * nz // 4)) for q in range(4)]

    x = layer_input[0].astype(F32)
    scale_one = lax.rsqrt(jnp.mean(x * x, axis=-1, keepdims=True) + EPSILON)
    h_one = (x * scale_one * attn_gain).astype(BF16)
    o_cols = width // nctx
    o_piece = lax.dynamic_slice_in_dim(o_weight, at_ctx * o_cols, o_cols, 1)
    qkv_piece = jnp.concatenate(
        [
            lax.dynamic_slice_in_dim(q_weight, at_ctx * q_cols, q_cols, 1),
            lax.dynamic_slice_in_dim(key_matrix, at_ctx * HEAD_DIM, HEAD_DIM, 1),
            lax.dynamic_slice_in_dim(value_matrix, at_ctx * HEAD_DIM, HEAD_DIM, 1),
        ],
        axis=1,
    )
    router_deep = router_weight.size // o_cols
    o_deep = o_piece.shape[0]
    o_piece = jnp.concatenate([o_piece, router_weight.reshape(router_deep, o_cols)])
    far_o, near_o, far_w, near_w = {0: o_piece}, {}, {0: qkv_piece}, {}
    for j in z_first:
        far_o[j] = swap_z(o_piece, j)
    near_o[0] = swap(o_piece, 0, 1)
    near_w[0] = swap(qkv_piece, 0, 1)
    h_pieces = [h_one, None, swap(h_one, 2, 0, 3), None]
    routes_t = routes[0].T
    there = [routes_t] + [None] * (nz - 1)
    for j in groups[1]:
        there[j] = swap_z(routes_t, j)
    tick()

    for j in z_second:
        far_o[j] = swap_z(o_piece, j)
    for j in z_first:
        near_o[j] = swap(far_o[j], 0, 1)
    h_pieces[1] = swap(h_one, 1, 0)
    for j in groups[2]:
        there[j] = swap_z(routes_t, j)
    tick()

    for j in z_first:
        far_w[j] = swap_z(qkv_piece, j)
    for j in z_second:
        near_o[j] = swap(far_o[j], 0, 1)
    for j in groups[0][1:] + groups[3]:
        there[j] = swap_z(routes_t, j)
    tick()

    h_pieces[3] = swap(h_pieces[2], 1, 0)
    for j in z_second:
        far_w[j] = swap_z(qkv_piece, j)
    for j in z_first:
        near_w[j] = swap(far_w[j], 0, 1)
    o_all = now(place_ep(far_o, near_o)).reshape(nep, o_deep + router_deep, o_cols)
    o_part_of = nep // nctx

    def o_block(m):
        block = lax.dynamic_slice(o_all, ((at_ctx ^ m) * o_part_of, 0, 0), (o_part_of, o_deep, o_cols))
        return block.reshape(q_cols, o_cols)

    o_pieces = {0: o_block(0), 2: swap(o_block(2), 2, 0)}
    router_full = o_all[:, o_deep:].reshape(width, experts)
    token = jnp.arange(rows, dtype=jnp.int32)
    upto = (token[:, None] <= token[None, :]).astype(BF16)
    slots = jnp.arange(capacity, dtype=jnp.int32).astype(F32)

    def slot_table(hits):
        rank = mm(hits.astype(BF16), upto) - 1.0
        return ((rank[:, None, :] == slots[None, :, None]) & (hits[:, None, :] > 0)).astype(BF16)

    places = jnp.arange(np_, dtype=jnp.int32)
    plane_experts = (at_ctx ^ (places >> 1 & ~1) ^ (places & 1)) * nep + (at_ep ^ (places >> 1 & 1))
    tables = []
    for j in range(nz):
        hits = jnp.sum((now(there[j])[None] == plane_experts[:, None, None]).astype(F32), axis=1)
        tables.append(slot_table(hits).reshape(np_ * capacity, rows))
    lane_ids = jnp.arange(-(-experts // 128) * 128, dtype=jnp.int32)
    picker = jnp.sum((routes[0][:, :, None] == lane_ids).astype(F32), axis=1)

    def pick(far, q):
        return {j: [did(v) for v in select(tables[j], [now(v) for v in far[j]], nb)] for j in groups[q]}

    def fetch(v, far, q, *parts, rounds=1):
        half = width // 2
        for j in groups[q]:
            if j and len(parts) == 2:
                far[j] = [swap_z(v, j, rounds)]
            elif j:
                far.setdefault(j, []).append(swap_z(v[:, parts[0] * half : (parts[0] + 1) * half], j, rounds))

    def post(pieces, got, q, *bs, rounds=1):
        for j in groups[q]:
            for b in bs:
                got.setdefault(j, [pieces[j][0]] + [None] * (nb - 1))[b] = swap(pieces[j][b], b & ~1, b & 1, rounds)

    def share(got, q):
        half = np_ * capacity // 2 // nb
        for j in groups[q]:
            got[j].append(swap(jnp.concatenate([v[half:] for v in got[j]], axis=0), 1, 0))

    def share_back(made, q):
        for j in groups[q]:
            made[j] = [made[j][0], swap(made[j][1], 1, 0)]

    def packed(made, q):
        for j in groups[q]:
            copies[j], outs[j] = pack(now(made[j][0]), made[j][1], nb, width)
            did(copies[j][0])

    def gather(pieces, q, shares=2):
        total = {}
        for j in groups[q]:
            ready = [now(pieces[j][0]), *pieces[j][1:]]
            total[j] = combine(tables[j], ready, BF16, shares) if j else combine(tables[j], ready, F32, 1)
            for v in total[j]:
                did(v)
        return total

    def home(total, kept, part, rounds=1):
        for j, v in total.items():
            if j:
                kept.setdefault(j, [None] * len(v))[part] = swap_z(v[part], j, rounds)
            else:
                kept[j] = v

    grad_out = out_grad[0]
    far_g, got_g = {0: [grad_out]}, {}
    tick()

    for j in z_second:
        near_w[j] = swap(far_w[j], 0, 1)
    fetch(grad_out, far_g, 2, 0)
    fetch(grad_out, far_g, 0, 0, 1)
    picked_g0 = pick(far_g, 0)
    frequency = ROPE_BASE ** (-jnp.arange(HEAD_DIM // 2).astype(F32) * 2.0 / HEAD_DIM)
    angles = jnp.arange(length).astype(F32)[:, None] * frequency[None, :]
    cosine, sine = jnp.cos(angles), jnp.sin(angles)
    cos_full = jnp.concatenate([cosine, cosine], axis=1)
    sin_full = jnp.concatenate([-sine, sine], axis=1)
    q_gain_row, k_gain_row = q_gain[None, :], key_norm_gain[None, :]
    h_full = place(h_pieces, lambda i: at_ctx ^ i)
    flat_routes = now(jnp.concatenate(there))
    plane_routes = [flat_routes] + [swap(flat_routes, b & ~1, b & 1) for b in range(1, nb)]
    tick()

    o_pieces[3] = swap(o_block(3), 3, 0)
    o_pieces[1] = swap(o_block(1), 1, 0)
    post(picked_g0, got_g, 0, 1)
    fetch(grad_out, far_g, 2, 1)
    behind = after(grad_out, far_g[groups[2][-1]][-1])
    fetch(behind, far_g, 3, 0, rounds=2)
    qkv_weight = place_ep(far_w, near_w)
    qkv = mm(h_full, now(qkv_weight))
    attn, turned_q, turned_k, lse = attend(qkv, cos_full, sin_full, q_gain_row, k_gain_row, heads)
    did(attn)
    tick()

    router_wide = jnp.pad(router_full, ((0, 0), (0, lane_ids.shape[0] - experts)))
    fetch(grad_out, far_g, 3, 1, rounds=2)
    picked_g2 = pick(far_g, 2)
    o_rows = place([o_pieces[m] for m in range(nctx)], lambda i: at_ctx ^ i, 1)
    attn = now(attn)
    held = {}
    for hi in reversed(range(0, nctx, 2)):
        sent = swap(mm(own_rows(attn, hi + 1), o_rows).astype(BF16), 1, 0)
        held[hi] = did(mm(own_rows(attn, hi), o_rows) + sent.astype(F32))
    branch_far = swap(held[2].astype(BF16), 2, 0)
    tick()

    post(picked_g0, got_g, 0, 2, 3)
    post(picked_g2, got_g, 2, 1)
    shape = jax.ShapeDtypeStruct
    resid, h_two, scale_two = by_rows(
        second_norm_kernel,
        [held[0], now(branch_far), layer_input[0], ffn_gain[None]],
        [shape((rows, width), F32), shape((rows, width), BF16), shape((rows, 1), F32)],
        "second_norm",
    )
    far_h, got_h = {0: [h_two]}, {}
    fetch(h_two, far_h, 2, 0)
    fetch(h_two, far_h, 0, 0, 1)
    picked_h = pick(far_h, 0)
    tick()

    post(picked_h, got_h, 0, 1, 2, 3)
    share(got_g, 0)
    fetch(h_two, far_h, 2, 1)
    here_routes = now(jnp.stack(plane_routes))
    all_routes = jnp.stack([here_routes, swap(here_routes, 1, 0)])
    picked_g3 = pick(far_g, 3)
    gate, up, down = gate_weight[0], up_weight[0], down_weight[0]
    results, copies, outs, joined = {}, {}, {}, None

    def expert(q):
        nonlocal joined
        for j in groups[q]:
            h_in = [now(got_h[j][0]), *got_h[j][1:]]
            results[j], joined = expert_step(
                j, nz, h_in, got_g[j], gate, up, down, router_wide, picks, marks, joined
            )
            did(results[j][0])

    tick()

    post(picked_g2, got_g, 2, 2, 3)
    post(picked_g3, got_g, 3, 1)
    fetch(h_two, far_h, 3, 0)
    share(got_h, 0)
    picked_h2 = pick(far_h, 2)
    at_device = at_ctx * nep + at_ep
    all_routes = now(all_routes).reshape(2, nb, nz, TOP, rows).transpose(3, 2, 0, 1, 4)
    all_routes = all_routes.reshape(TOP, devices, rows)
    own_id = jnp.full((1, 128), at_device, jnp.int32)
    picks = did(pick_rows(own_id, all_routes, upto, capacity, lane_ids.shape[0]))
    extra = -(-2 * experts // 128) * 128
    extra_ids = jnp.arange(extra, dtype=jnp.int32)
    marks = jnp.stack([extra_ids == at_device, extra_ids == at_device, extra_ids == at_device + experts]).astype(F32)
    lanes = lane_ids.shape[0]
    router, gates, picked_total = by_rows(
        lambda *refs: route_kernel(experts, *refs),
        [now(h_two), router_wide, picker],
        [shape((rows, lanes), F32), shape((rows, lanes), F32), shape((rows, 1), F32)],
        "route",
    )
    did(gates)
    tick()
    post(picked_h2, got_h, 2, 1, 2, 3)
    share(got_g, 2)
    fetch(h_two, far_h, 3, 1)
    expert(0)
    tick()
    post(picked_g3, got_g, 3, 2, 3)
    fetch(grad_out, far_g, 1, 0, 1)
    picked_h3 = pick(far_h, 3)
    share(got_h, 2)
    share_back(results, 0)
    tick()
    post(picked_h3, got_h, 3, 1, 2, 3)
    share(got_g, 3)
    fetch(h_two, far_h, 1, 0, 1)
    picked_g1 = pick(far_g, 1)
    expert(2)
    tick()
    post(picked_g1, got_g, 1, 1, 2, 3)
    share(got_h, 3)
    share_back(results, 2)
    picked_h1 = pick(far_h, 1)
    packed(results, 0)
    tick()
    post(picked_h1, got_h, 1, 1, 2, 3)
    share(got_g, 1)
    expert(3)
    packed(results, 2)
    back, made = {}, {}
    tick()

    post(copies, back, 2, 1, 2, 3)
    share(got_h, 1)
    share_back(results, 3)
    packed(results, 3)
    tick()
    post(copies, back, 3, 1, 2, 3)
    total_2 = gather(back, 2)
    homes = {}
    home(total_2, homes, 0)
    for j in groups[1]:
        got_h[j][0] = after(got_h[j][0], *total_2[groups[2][-1]])
    expert(1)
    tick()
    post(copies, back, 0, 1, 2, 3)
    home(total_2, homes, 1)
    total_3 = gather(back, 3, 1)
    share_back(results, 1)
    packed(results, 1)
    joined_h, joined_g, hidden_all, grad_gate_all, grad_up_all = joined
    gate_part = did(product(joined_h, now(grad_gate_all), "tn", F32, 512))
    tick()
    post(copies, back, 1, 1, 2, 3)
    home(total_3, homes, 0, 2)
    total_0 = gather(back, 0, 1)
    up_part = did(product(joined_h, now(grad_up_all), "tn", F32, 512))
    tick()

    home(gather(back, 1, 1), homes, 0)
    home(total_0, homes, 0)
    post(outs, made, 3, 1, 2, 3)
    down_part = did(product(now(hidden_all), joined_g, "tn", F32, 256))
    tick()

    whole = [homes[j][0] for j in sorted(homes) if j and len(homes[j]) == 1]
    homes = [now(homes[0][0]), *whole, *[v for j in sorted(homes) if len(homes[j]) == 2 for v in homes[j]]]
    grad_resid, low, logit_low, ffn_gain_part = by_rows(
        lambda *refs: second_back_kernel(experts, len(homes), len(whole), *refs),
        [*homes, gates, router, picker, picked_total, router_wide, resid, scale_two, ffn_gain[None], grad_out],
        [shape((rows, width), F32), shape((rows, width), BF16), shape((rows, lanes), BF16), shape((1, width), F32)],
        "second_back",
    )
    did(low)
    homes = {}
    total_3 = gather(made, 3, 1)
    home(total_3, homes, 0, 2)
    tick()
    low_pieces = [low, swap(low, 1, 0), swap(low, 2, 0), None]
    post(outs, made, 2, 1)
    post(outs, made, 1, 1)
    tick()
    low_pieces[3] = swap(low_pieces[2], 1, 0)
    post(outs, made, 2, 2, 3, rounds=2)
    post(outs, made, 1, 2, rounds=2)
    post(outs, made, 0, 1, rounds=2)
    tick()

    branch_full = now(place(low_pieces, lambda i: at_ctx ^ i))
    o_own = q_cols // nep
    own_width = width // devices
    o_part = product(attn, branch_full, "tn", F32, 256)
    router_part = t_mm(logit_low, h_two)[:experts].reshape(experts, nctx, nep, own_width)
    router_rows = experts * nctx * own_width // width

    def o_term(j, ry):
        place_of = at_ep ^ (2 * j + ry)
        block = lax.dynamic_slice_in_dim(o_part, place_of * o_own, o_own, 0)
        router_block = lax.dynamic_slice_in_dim(router_part, place_of, 1, 2).reshape(router_rows, width)
        return jnp.concatenate([block, router_block], axis=0)

    last_steps = list(reversed(range(nz)))
    o_sent = {j: did(o_term(j, 1).astype(BF16)) for j in last_steps}
    grad_attn = did(product(branch_full, o_rows, "nt", BF16, 512))
    for j in groups[2]:
        made[j][0] = after(made[j][0], grad_attn)
    total_2 = gather(made, 2, 1)
    home(total_2, homes, 0, 2)
    tick()

    o_near = {j: swap(o_sent[j], 0, 1) for j in last_steps[:-1]}
    post(outs, made, 0, 2)
    grad_qkv, q_gain_part, k_gain_part = attend_back(
        qkv, turned_q, turned_k, attn, lse, now(grad_attn), cos_full, sin_full, q_gain_row, k_gain_row, heads
    )
    did(grad_qkv)
    tick()

    post(outs, made, 1, 3)
    post(outs, made, 0, 3)
    o_near[0] = swap(o_sent[0], 0, 1)
    o_far = {}
    o_mid = {j: (o_term(j, 0) + now(o_near[j]).astype(F32)).astype(BF16) for j in last_steps[:-1]}
    for j in last_steps[: nz // 4]:
        o_far[j] = swap_z(o_mid[j], j)
    qkv_part = product(h_full, now(grad_qkv), "tn", F32, 512).reshape(nctx, nep, own_width, -1)

    def qkv_term(j, ry):
        return lax.dynamic_slice_in_dim(qkv_part, at_ep ^ (2 * j + ry), 1, 1)[:, 0]

    qkv_sent = {j: did(qkv_term(j, 1).astype(BF16)) for j in last_steps}
    one_term = lambda m, plus, dtype: product(
        own_rows(grad_qkv, m), qkv_weight, "nt", dtype, 1024, plus
    )
    sent = [did(one_term(m, None, BF16)) for m in (3, 1)]
    tick()

    first_steps, other_steps = last_steps[::2], last_steps[1::2]
    qkv_near = {j: swap(qkv_sent[j], 0, 1) for j in first_steps}
    sent = [swap(v, 1, 0) for v in sent]
    for j in last_steps[nz // 4 : -1]:
        o_far[j] = swap_z(o_mid[j], j)
    total_1, total_0 = gather(made, 1, 1), gather(made, 0, 1)
    held = [did(one_term(0, sent[1], F32)), did(one_term(2, sent[0], BF16))]
    tick()

    qkv_near.update({j: swap(qkv_sent[j], 0, 1) for j in other_steps})
    one_far = swap(held[1], 2, 0)
    qkv_mid = lambda j: (qkv_term(j, 0) + now(qkv_near[j]).astype(F32)).astype(BF16)
    qkv_far = {j: swap_z(qkv_mid(j), j) for j in last_steps[: nz // 4]}
    home(total_1, homes, 0)
    o_sum = o_term(0, 0) + o_near[0].astype(F32)
    for j in range(1, nz):
        o_sum = o_sum + now(o_far[j]).astype(F32)
    o_grad = did(o_sum[:o_own])
    router_sum = did(o_sum[o_own:].reshape(experts, nctx, own_width).transpose(1, 2, 0))
    input_grad, attn_gain_part = by_rows(
        first_back_kernel,
        [held[0], one_far, layer_input[0], scale_one, attn_gain[None], grad_resid],
        [shape((rows, width), F32), shape((1, width), F32)],
        "first_back",
    )
    did(input_grad)
    tick()

    qkv_far.update({j: swap_z(qkv_mid(j), j) for j in last_steps[nz // 4 : -1]})
    home(total_0, homes, 0)
    late = jnp.concatenate([now(attn_gain_part)[0], ffn_gain_part[0], q_gain_part[0], k_gain_part[0]])
    late = did(sum_over(late, [(1 << b, 0) for b in range(nctx.bit_length() - 1)] + [(0, 1)]))
    tick()

    qkv_sum = qkv_term(0, 0) + qkv_near[0].astype(F32)
    for j in range(1, nz):
        qkv_sum = qkv_sum + now(qkv_far[j]).astype(F32)
    last = jnp.concatenate([qkv_sum, router_sum], axis=2).astype(BF16)
    last_block = lambda m: lax.dynamic_index_in_dim(last, at_ctx ^ m, 0)
    last = place([swap(last_block(m), m, 0) for m in range(nctx)], lambda i: at_ctx ^ i).astype(F32)
    late = sum_over(now(late), [(0, 2 << b) for b in range(nz.bit_length() - 1)])
    qkv_grad = last
    router_grad = jnp.sum(last[:, :, q_cols + 2 * HEAD_DIM :], axis=0)
    mixed = resid
    for j in sorted(homes):
        mixed = mixed + jnp.concatenate(homes[j]).astype(F32)

    def columns(first, last):
        return jnp.concatenate([qkv_grad[c, :, first:last] for c in range(nctx)], axis=1)

    return (
        mixed.astype(BF16)[None],
        input_grad[None],
        late[:width],
        columns(0, q_cols),
        columns(q_cols, q_cols + HEAD_DIM),
        columns(q_cols + HEAD_DIM, q_cols + 2 * HEAD_DIM),
        o_grad,
        late[2 * width : 2 * width + HEAD_DIM],
        late[2 * width + HEAD_DIM :],
        late[width : 2 * width],
        router_grad,
        gate_part[None],
        up_part[None],
        down_part[None],
    )


def solution(mesh):
    nctx, nep = mesh.shape["ctx"], mesh.shape["ep"]
    tokens = P("ep", "ctx", None)
    own = P(("ctx", "ep"), None)
    expert = P(("ctx", "ep"), None, None)
    split_rows = P("ep", None)

    def on_device(*arrays):
        return layer(nctx, nep, *arrays)

    return jax.shard_map(
        on_device,
        mesh=mesh,
        in_specs=(
            tokens, P(), split_rows, split_rows, split_rows, split_rows, P(), P(), P(), split_rows,
            expert, expert, expert, tokens, tokens,
        ),
        out_specs=(
            tokens, tokens, P(), own, own, own, own, P(), P(), P(), own, expert, expert, expert,
        ),
        check_vma=False,
    )
```

```python
import math

import jax
import jax.numpy as jnp
from jax import lax
from jax.experimental import pallas as pl
from jax.experimental.pallas import tpu as pltpu
from jax.sharding import PartitionSpec as P

QUERY_HEADS = 32
KEY_VALUE_HEADS = 4
HEAD_DIM = 128
TOP = 8
BLOCK = 256

EPSILON = 1e-06
ROPE_BASE = 1000000.0
LOG2_E = 1.4426950408889634
F32 = jnp.float32
BF16 = jnp.bfloat16
AXES = ("ctx", "ep")
HIGHEST = lax.Precision.HIGHEST


def mm(a, b):
    return jnp.dot(a, b, preferred_element_type=F32)


def mm_t(a, b):
    return lax.dot_general(a, b, (((1,), (1,)), ((), ())), preferred_element_type=F32)


def t_mm(a, b):
    return lax.dot_general(a, b, (((0,), (0,)), ((), ())), preferred_element_type=F32)


LIGHT = pl.CostEstimate(flops=1, bytes_accessed=1, transcendentals=0)
VMEM_MOST = 56 * 1024 * 1024


def half_turn(v):
    return pltpu.roll(v, HEAD_DIM // 2, 1)


def head_norm(v, gain):
    scale = lax.rsqrt(jnp.mean(v * v, axis=-1, keepdims=True) + EPSILON)
    return v * scale * gain


def head_norm_back(v, gain, dy):
    scale = lax.rsqrt(jnp.mean(v * v, axis=-1, keepdims=True) + EPSILON)
    lifted = gain * dy
    inner = jnp.mean(v * lifted, axis=-1, keepdims=True)
    return (
        scale * lifted - v * (scale * scale * scale * inner),
        jnp.sum(v * scale * dy, axis=0, keepdims=True),
    )


def diagonal_mask():
    key_at = lax.broadcasted_iota(jnp.int32, (BLOCK, BLOCK), 0)
    query_at = lax.broadcasted_iota(jnp.int32, (BLOCK, BLOCK), 1)
    return key_at <= query_at


def attend_kernel(
    q_ref, k_ref, v_ref, cos_ref, sin_ref, qg_ref, kg_ref,
    out_ref, qr_ref, kr_ref, lse_ref, keys, values_t,
):
    blocks = q_ref.shape[0] // BLOCK
    coefficient = LOG2_E * HEAD_DIM ** (-0.5)

    @pl.when(pl.program_id(0) == 0)
    def _():
        normed = head_norm(k_ref[...], kg_ref[...])
        turned = (normed * cos_ref[...] + half_turn(normed) * sin_ref[...]).astype(BF16)
        keys[...] = turned
        kr_ref[...] = turned
        values_t[...] = v_ref[...].T.astype(BF16)

    normed = head_norm(q_ref[...], qg_ref[...])
    queries = (normed * cos_ref[...] + half_turn(normed) * sin_ref[...]).astype(BF16)
    qr_ref[...] = queries
    visible = diagonal_mask()
    for i in range(blocks):
        low, high = i * BLOCK, (i + 1) * BLOCK
        q_i = queries[low:high]
        s_in = jnp.where(visible, mm_t(keys[low:high, :], q_i) * coefficient, -1e30)
        top = jnp.max(s_in, axis=0, keepdims=True)
        if i:
            s_off = mm_t(keys[:low, :], q_i) * coefficient
            top = jnp.maximum(top, jnp.max(s_off, axis=0, keepdims=True))
        p_in = jnp.exp2(s_in - top)
        total = jnp.sum(p_in, axis=0, keepdims=True)
        mixed = mm(values_t[:, low:high], p_in.astype(BF16))
        if i:
            p_off = jnp.exp2(s_off - top)
            total = total + jnp.sum(p_off, axis=0, keepdims=True)
            mixed = mixed + mm(values_t[:, :low], p_off.astype(BF16))
        out_ref[low:high, :] = (mixed * (1.0 / total)).T.astype(BF16)
        lse_ref[0, :, low:high] = top + jnp.log2(total)


def attend_back_kernel(
    qr_ref, q_ref, do_ref, out_ref, lse_ref, kr_ref, k_ref, v_ref, cos_ref, sin_ref, qg_ref, kg_ref,
    grad_ref, qgain_ref, kgain_ref, keys_t, values, dk, dv, dq,
):
    step = pl.program_id(0)
    heads = pl.num_programs(0) - 2
    blocks = q_ref.shape[0] // BLOCK
    scale = HEAD_DIM ** (-0.5)
    coefficient = LOG2_E * scale

    @pl.when(step == 0)
    def _():
        keys_t[...] = kr_ref[...].astype(F32).T.astype(BF16)
        values[...] = v_ref[...].astype(BF16)
        dk[...] = jnp.zeros_like(dk)
        dv[...] = jnp.zeros_like(dv)
        qgain_ref[...] = jnp.zeros_like(qgain_ref)

    def turn_back(v):
        return v * cos_ref[...] - half_turn(v) * sin_ref[...]

    @pl.when(step < heads)
    def _():
        delta = jnp.sum((do_ref[...].astype(F32) * out_ref[...].astype(F32)).T, axis=0, keepdims=True)
        visible = diagonal_mask()
        for i in range(blocks):
            low, high = i * BLOCK, (i + 1) * BLOCK
            q_i = qr_ref[low:high, :]
            do_i = do_ref[low:high, :]
            lse_i = lse_ref[0, :, low:high]
            delta_i = delta[:, low:high]

            def part(first, last, masked):
                p = jnp.exp2(mm_t(kr_ref[first:last, :], q_i) * coefficient - lse_i)
                if masked:
                    p = jnp.where(visible, p, 0.0)
                dp = mm_t(values[first:last, :], do_i)
                dv[first:last, :] += mm(p.astype(BF16), do_i)
                ds = (p * (dp - delta_i)).astype(BF16)
                dk[first:last, :] += mm(ds, q_i)
                return mm(keys_t[:, first:last], ds)

            turned = part(low, high, True)
            if i:
                turned = turned + part(0, low, False)
            dq[low:high, :] = turned.T * scale
        back, gain_part = head_norm_back(q_ref[...], qg_ref[...], turn_back(dq[...]))
        grad_ref[...] = back.astype(BF16)
        qgain_ref[...] += gain_part

    @pl.when(step == heads)
    def _():
        back, gain_part = head_norm_back(k_ref[...], kg_ref[...], turn_back(dk[...] * scale))
        grad_ref[...] = back.astype(BF16)
        kgain_ref[...] = gain_part

    @pl.when(step == heads + 1)
    def _():
        grad_ref[...] = dv[...].astype(BF16)


def attend(qkv, cos, sin, q_gain, k_gain, heads):
    length = qkv.shape[0]
    column = lambda at: pl.BlockSpec((length, HEAD_DIM), lambda h: (0, at))
    moving = pl.BlockSpec((length, HEAD_DIM), lambda h: (0, h))
    fixed = pl.BlockSpec((length, HEAD_DIM), lambda h: (0, 0))
    row = pl.BlockSpec((1, HEAD_DIM), lambda h: (0, 0))
    return pl.pallas_call(
        attend_kernel,
        grid=(heads,),
        in_specs=[moving, column(heads), column(heads + 1), fixed, fixed, row, row],
        out_specs=[moving, moving, fixed, pl.BlockSpec((1, 1, length), lambda h: (h, 0, 0))],
        out_shape=[
            jax.ShapeDtypeStruct((length, heads * HEAD_DIM), BF16),
            jax.ShapeDtypeStruct((length, heads * HEAD_DIM), BF16),
            jax.ShapeDtypeStruct((length, HEAD_DIM), BF16),
            jax.ShapeDtypeStruct((heads, 1, length), F32),
        ],
        scratch_shapes=[pltpu.VMEM((length, HEAD_DIM), BF16), pltpu.VMEM((HEAD_DIM, length), BF16)],
        compiler_params=pltpu.CompilerParams(vmem_limit_bytes=40 * 1024 * 1024),
        cost_estimate=LIGHT,
        name="attend",
    )(qkv, qkv, qkv, cos, sin, q_gain, k_gain)


def attend_back(qkv, turned_q, turned_k, out, lse, grad_out, cos, sin, q_gain, k_gain, heads):
    length = qkv.shape[0]
    column = lambda at: pl.BlockSpec((length, HEAD_DIM), lambda h: (0, at))
    moving = pl.BlockSpec((length, HEAD_DIM), lambda h: (0, jnp.minimum(h, heads - 1)))
    fixed = pl.BlockSpec((length, HEAD_DIM), lambda h: (0, 0))
    row = pl.BlockSpec((1, HEAD_DIM), lambda h: (0, 0))
    return pl.pallas_call(
        attend_back_kernel,
        grid=(heads + 2,),
        in_specs=[
            moving, moving, moving, moving,
            pl.BlockSpec((1, 1, length), lambda h: (jnp.minimum(h, heads - 1), 0, 0)),
            fixed, column(heads), column(heads + 1), fixed, fixed, row, row,
        ],
        out_specs=[pl.BlockSpec((length, HEAD_DIM), lambda h: (0, h)), row, row],
        out_shape=[
            jax.ShapeDtypeStruct((length, (heads + 2) * HEAD_DIM), BF16),
            jax.ShapeDtypeStruct((1, HEAD_DIM), F32),
            jax.ShapeDtypeStruct((1, HEAD_DIM), F32),
        ],
        scratch_shapes=[
            pltpu.VMEM((HEAD_DIM, length), BF16),
            pltpu.VMEM((length, HEAD_DIM), BF16),
            pltpu.VMEM((length, HEAD_DIM), F32),
            pltpu.VMEM((length, HEAD_DIM), F32),
            pltpu.VMEM((length, HEAD_DIM), F32),
        ],
        compiler_params=pltpu.CompilerParams(vmem_limit_bytes=40 * 1024 * 1024),
        cost_estimate=LIGHT,
        name="attend_back",
    )(turned_q, qkv, grad_out, out, lse, turned_k, qkv, qkv, cos, sin, q_gain, k_gain)


def select_kernel(n_parts, table, *refs):
    parts, outs = refs[:n_parts], refs[n_parts:]
    deep = outs[0].shape[0]
    first = 0
    for part in parts:
        for at in range(0, part.shape[1], 1024):
            wide = min(1024, part.shape[1] - at)
            rows = mm(table[...], part[:, at : at + wide]).astype(BF16)
            for b, out in enumerate(outs):
                out[:, first : first + wide] = rows[b * deep : (b + 1) * deep]
            first += wide


def select(table, parts, chips):
    width, deep = sum(v.shape[1] for v in parts), table.shape[0] // chips
    return pl.pallas_call(
        lambda *refs: select_kernel(len(parts), *refs),
        out_shape=[jax.ShapeDtypeStruct((deep, width), BF16)] * chips,
        compiler_params=pltpu.CompilerParams(vmem_limit_bytes=VMEM_MOST),
        cost_estimate=LIGHT,
        name="select",
    )(table, *parts)


def combine_kernel(n_pieces, table, *refs):
    pieces, outs = refs[:n_pieces], refs[n_pieces:]
    deep, width = outs[0].shape
    for first in range(0, width, 512):
        at = slice(first, min(first + 512, width))
        rows = jnp.concatenate([p[:, at] for p in pieces], axis=0)
        total = t_mm(table[...], rows)
        for i, out in enumerate(outs):
            out[:, at] = total[i * deep : (i + 1) * deep].astype(out.dtype)


def combine(table, pieces, dtype, shares):
    shape = (table.shape[1] // shares, pieces[0].shape[1])
    return pl.pallas_call(
        lambda *refs: combine_kernel(len(pieces), *refs),
        out_shape=[jax.ShapeDtypeStruct(shape, dtype)] * shares,
        compiler_params=pltpu.CompilerParams(vmem_limit_bytes=VMEM_MOST),
        cost_estimate=LIGHT,
        name="combine",
    )(table, *pieces)


def pack_kernel(chips, near, other, *outs):
    deep = outs[0].shape[0] // 2
    first = 0
    for group in (outs[:chips], outs[chips:]):
        at = slice(first, first + group[0].shape[1])
        for b, out in enumerate(group):
            out[:deep, :] = near[b * deep : (b + 1) * deep, at]
            out[deep:, :] = other[b * deep : (b + 1) * deep, at]
        first = at.stop


def pack(near, other, chips, width):
    deep, first = 2 * near.shape[0] // chips, near.shape[1] - width
    got = pl.pallas_call(
        lambda *refs: pack_kernel(chips, *refs),
        out_shape=[jax.ShapeDtypeStruct((deep, n), BF16) for n in (first, width) for _ in range(chips)],
        compiler_params=pltpu.CompilerParams(vmem_limit_bytes=VMEM_MOST),
        cost_estimate=LIGHT,
        name="pack",
    )(near, other)
    return got[:chips], got[chips:]


def expert_kernel(chips, ff_tiles, n_in, *refs):
    h_in, g_in = refs[: chips + 1], refs[chips + 1 : 2 * chips + 2]
    gate_c, up_c, down_r, gate_r, up_r, down_c, router, picks, marks = refs[2 * chips + 2 : 2 * chips + 11]
    results = refs[n_in : n_in + 2]
    h_all, g_all, hid_all, gg_all, gu_all, scale, dots = refs[n_in + 2 :]
    step = pl.program_id(0)
    deep = h_in[0].shape[0] // 2
    half = chips * deep
    wide, out_wide = gate_c.shape[1], down_c.shape[1]
    width = h_in[0].shape[1]

    @pl.when(step == 0)
    def _():
        for arrived, joined in ((h_in, h_all), (g_in, g_all)):
            for b in range(chips):
                joined[b * deep : (b + 1) * deep, :] = arrived[b][:deep, :]
            joined[half:, :] = arrived[chips][...]
        dots[...] = jnp.zeros_like(dots)
        logits = mm(h_all[...], router[...])
        picked = picks[...] > 0
        top = jnp.max(jnp.where(picked, logits, -1e30), axis=-1, keepdims=True)
        weight = jnp.where(picked, jnp.exp(logits - top), 0.0)
        total = jnp.sum(weight, axis=-1, keepdims=True)
        own = jnp.sum(weight * marks[0:1, : logits.shape[1]], axis=-1, keepdims=True)
        scale[...] = own / jnp.where(total > 0, total, 1.0)

    @pl.when(step < ff_tiles)
    def _():
        gate_proj = mm(h_all[...], gate_c[...])
        up_proj = mm(h_all[...], up_c[...])
        grad_hidden = mm_t(g_all[...], down_r[...])
        at = pl.ds(pl.multiple_of(step * wide, wide), wide)
        sigmoid = jax.nn.sigmoid(gate_proj)
        turned = gate_proj * sigmoid
        hidden = turned * up_proj
        dots[...] += jnp.sum(hidden * grad_hidden, axis=-1, keepdims=True)
        weighted = grad_hidden * scale[...]
        hid_all[:, at] = (hidden * scale[...]).astype(BF16)
        gu_all[:, at] = (weighted * turned).astype(BF16)
        gg_all[:, at] = (weighted * up_proj * (sigmoid + turned * (1.0 - sigmoid))).astype(BF16)

    @pl.when(step >= ff_tiles)
    def _():
        back = (mm_t(gg_all[...], gate_r[...]) + mm_t(gu_all[...], up_r[...])).astype(BF16)
        made = mm(hid_all[...], down_c[...]).astype(BF16)
        at = pl.multiple_of((step - ff_tiles) * out_wide, out_wide)
        behind = pl.multiple_of(at + width + marks.shape[1], 128)
        for core in range(2):
            results[core][:, pl.ds(at, out_wide)] = back[core * half : (core + 1) * half]
            results[core][:, pl.ds(behind, out_wide)] = made[core * half : (core + 1) * half]

    @pl.when(step == ff_tiles)
    def _():
        high = dots[...].astype(BF16).astype(F32)
        tagged = (high * marks[1:2, :] + (dots[...] - high) * marks[2:3, :]).astype(BF16)
        for core in range(2):
            results[core][:, width : width + marks.shape[1]] = tagged[core * half : (core + 1) * half]


def expert_step(j, steps, h_in, g_in, gate, up, down, router, picks, marks, joined):
    chips, (deep, width), ff = len(h_in) - 1, h_in[0].shape, down.shape[0]
    rows, extra = chips * deep, marks.shape[1]
    half = rows // 2
    ff_tile, out_tile = min(256, ff), min(512, width)
    ff_tiles, out_tiles = ff // ff_tile, width // out_tile
    first = lambda i: jnp.minimum(i, ff_tiles - 1)
    second = lambda i: jnp.maximum(i - ff_tiles, 0)
    whole = lambda shape: pl.BlockSpec(shape, lambda i: (0, 0))
    here = lambda n: pl.BlockSpec((rows, n), lambda i: (j, 0))
    in_specs = ([whole((deep, width))] * chips + [whole((half, width))]) * 2 + [
        pl.BlockSpec((width, ff_tile), lambda i: (0, first(i))),
        pl.BlockSpec((width, ff_tile), lambda i: (0, first(i))),
        pl.BlockSpec((ff_tile, width), lambda i: (first(i), 0)),
        pl.BlockSpec((out_tile, ff), lambda i: (second(i), 0)),
        pl.BlockSpec((out_tile, ff), lambda i: (second(i), 0)),
        pl.BlockSpec((ff, out_tile), lambda i: (0, second(i))),
        whole(router.shape),
        pl.BlockSpec((rows, picks.shape[1]), lambda i: (j, 0)),
        whole(marks.shape),
    ]
    args = [*h_in, *g_in, gate, up, down, gate, up, down, router, picks, marks]
    aliases = {}
    if joined:
        aliases = {len(args) + i: 2 + i for i in range(len(joined))}
        args += joined
        in_specs += [pl.BlockSpec(memory_space=pl.ANY)] * len(joined)
    got = pl.pallas_call(
        lambda *refs: expert_kernel(chips, ff_tiles, len(args), *refs),
        grid=(ff_tiles + out_tiles,),
        in_specs=in_specs,
        out_specs=[whole((half, 2 * width + extra))] * 2
        + [here(width), here(width), here(ff), here(ff), here(ff)],
        out_shape=[jax.ShapeDtypeStruct((half, 2 * width + extra), BF16)] * 2
        + [jax.ShapeDtypeStruct((steps * rows, n), BF16) for n in (width, width, ff, ff, ff)],
        scratch_shapes=[pltpu.VMEM((rows, 1), F32), pltpu.VMEM((rows, 1), F32)],
        input_output_aliases=aliases,
        compiler_params=pltpu.CompilerParams(vmem_limit_bytes=VMEM_MOST),
        cost_estimate=LIGHT,
        name="expert",
    )(*args)
    return got[:2], list(got[2:])


def picks_kernel(capacity, own, routes, upto, out):
    top, sources, rows = routes.shape
    lanes = out.shape[1]
    hits = jnp.zeros((sources, rows), F32)
    for i in range(top):
        hits = hits + (routes[i] == own[0:1, 0:1]).astype(F32)
    rank = jnp.where(hits > 0, mm(hits.astype(BF16), upto[...]) - 1.0, -1.0)
    slot = lax.broadcasted_iota(jnp.int32, (capacity, rows), 0).astype(F32)
    lane = lax.broadcasted_iota(jnp.int32, (lanes, rows), 0)
    for source in range(sources):
        table = (rank[source : source + 1] == slot).astype(BF16)
        named = jnp.zeros((lanes, rows), F32)
        for i in range(top):
            named = named + (routes[i, source : source + 1, :] == lane).astype(F32)
        out[source * capacity : (source + 1) * capacity, :] = mm_t(table, named.astype(BF16)).astype(BF16)


def pick_rows(own, routes, upto, capacity, lanes):
    return pl.pallas_call(
        lambda *refs: picks_kernel(capacity, *refs),
        out_shape=jax.ShapeDtypeStruct((routes.shape[1] * capacity, lanes), BF16),
        compiler_params=pltpu.CompilerParams(vmem_limit_bytes=VMEM_MOST),
        cost_estimate=LIGHT,
        name="picks",
    )(own, routes, upto)


def join_kernel(at, *refs):
    pieces, out = refs[:-1], refs[-1]
    for i, piece in enumerate(pieces):

        @pl.when((at[0] ^ pl.program_id(0)) == i)
        def _(piece=piece):
            out[...] = piece[...]


def join(pieces, at):
    deep, width = pieces[0].shape
    return pl.pallas_call(
        join_kernel,
        grid=(len(pieces),),
        in_specs=[pl.BlockSpec(memory_space=pltpu.SMEM)]
        + [pl.BlockSpec((deep, width), lambda i: (0, 0))] * len(pieces),
        out_specs=pl.BlockSpec((deep, width), lambda i: (i, 0)),
        out_shape=jax.ShapeDtypeStruct((len(pieces) * deep, width), pieces[0].dtype),
        compiler_params=pltpu.CompilerParams(vmem_limit_bytes=VMEM_MOST),
        cost_estimate=LIGHT,
        name="join",
    )(at, *pieces)


def product_kernel(kind, dtype, a, b, *rest):
    out = rest[-1]
    dims = {"nn": ((1,), (0,)), "nt": ((1,), (1,)), "tn": ((0,), (0,))}[kind]
    made = lax.dot_general(a[...], b[...], (dims, ((), ())), preferred_element_type=F32)
    if len(rest) == 2:
        made = made + rest[0][...].astype(F32)
    out[...] = made.astype(dtype)


def product(a, b, kind, dtype, tile, plus=None):
    m, n = a.shape[1 if kind == "tn" else 0], b.shape[0 if kind == "nt" else 1]
    tile = min(tile, m if kind == "tn" else n)
    whole = lambda v: pl.BlockSpec(v.shape, lambda i: (0, 0))
    if kind == "tn":
        specs = [pl.BlockSpec((a.shape[0], tile), lambda i: (0, i)), whole(b)]
        out_spec = pl.BlockSpec((tile, n), lambda i: (i, 0))
    else:
        b_spec = pl.BlockSpec((b.shape[0], tile), lambda i: (0, i))
        if kind == "nt":
            b_spec = pl.BlockSpec((tile, b.shape[1]), lambda i: (i, 0))
        specs = [whole(a), b_spec]
        out_spec = pl.BlockSpec((m, tile), lambda i: (0, i))
    args = [a, b] if plus is None else [a, b, plus]
    return pl.pallas_call(
        lambda *refs: product_kernel(kind, dtype, *refs),
        grid=((m if kind == "tn" else n) // tile,),
        in_specs=specs if plus is None else [*specs, out_spec],
        out_specs=out_spec,
        out_shape=jax.ShapeDtypeStruct((m, n), dtype),
        compiler_params=pltpu.CompilerParams(vmem_limit_bytes=VMEM_MOST),
        cost_estimate=LIGHT,
        name="product",
    )(*args)


def second_norm_kernel(held, arrived, x, gain, resid, normed, scale):
    total = x[...].astype(F32) + held[...] + arrived[...].astype(F32)
    factor = lax.rsqrt(jnp.mean(total * total, axis=-1, keepdims=True) + EPSILON)
    resid[...] = total
    normed[...] = (total * factor * gain[...]).astype(BF16)
    scale[...] = factor


def route_kernel(experts, h, router_weight, picker, router, gates, total):
    logits = mm(h[...], router_weight[...])
    real = lax.broadcasted_iota(jnp.int32, logits.shape, 1) < experts
    logits = jnp.where(real, logits, -1e30)
    shifted = jnp.where(real, jnp.exp(logits - jnp.max(logits, axis=-1, keepdims=True)), 0.0)
    probs = shifted / jnp.sum(shifted, axis=-1, keepdims=True)
    picked = picker[...] * probs
    picked_total = jnp.sum(picked, axis=-1, keepdims=True)
    router[...] = probs
    gates[...] = picked / picked_total
    total[...] = picked_total


def norm_back(v, scale, gain, dy):
    lifted = gain * dy
    inner = jnp.mean(v * lifted, axis=-1, keepdims=True)
    return scale * lifted - v * (scale * scale * scale * inner), jnp.sum(v * scale * dy, axis=0, keepdims=True)


def second_back_kernel(experts, n_homes, n_whole, *refs):
    homes = refs[:n_homes]
    gates, router, picker, total, router_weight, resid, scale, gain, grad_out = refs[n_homes : n_homes + 9]
    grad_resid, low, logit_low, gain_part = refs[n_homes + 9 :]
    width, lanes = resid.shape[1], router.shape[1]
    arrived = homes[0][...]
    for home in homes[1 : 1 + n_whole]:
        arrived = arrived + home[...].astype(F32)
    for upper, lower in zip(homes[1 + n_whole :: 2], homes[2 + n_whole :: 2]):
        arrived = arrived + jnp.where(pl.program_id(0) == 0, upper[...].astype(F32), lower[...].astype(F32))
    tags = arrived[:, width:]
    if tags.shape[1] == lanes:
        dots = tags + pltpu.roll(tags, lanes - experts, 1)
    else:
        dots = tags[:, :lanes] + tags[:, lanes : 2 * lanes]
    probs, chosen = router[...], picker[...]
    dots = jnp.where(chosen > 0, dots, 0.0)
    grad_pick = chosen * (dots - jnp.sum(dots * gates[...], axis=-1, keepdims=True)) / total[...]
    grad_logits = probs * (grad_pick - jnp.sum(probs * grad_pick, axis=-1, keepdims=True))
    logit_low[...] = grad_logits.astype(BF16)
    grad_two = arrived[:, :width] + mm_t(grad_logits.astype(BF16), router_weight[...])
    back, part = norm_back(resid[...], scale[...], gain[...], grad_two)
    back = back + grad_out[...].astype(F32)
    grad_resid[...] = back
    low[...] = back.astype(BF16)
    gain_part[...] = jnp.where(pl.program_id(0) == 0, 0.0, gain_part[...]) + part


def first_back_kernel(held, arrived, x, scale, gain, grad_resid, input_grad, gain_part):
    dy = held[...] + arrived[...].astype(F32)
    back, part = norm_back(x[...].astype(F32), scale[...], gain[...], dy)
    input_grad[...] = grad_resid[...] + back
    gain_part[...] = jnp.where(pl.program_id(0) == 0, 0.0, gain_part[...]) + part


def by_rows(kernel, args, outs, name, step=128):
    rows = args[0].shape[0]

    def spec(shape):
        if shape[0] == rows:
            return pl.BlockSpec((step, shape[1]), lambda i: (i, 0))
        return pl.BlockSpec(shape, lambda i: (0, 0))

    return pl.pallas_call(
        kernel,
        grid=(rows // step,),
        in_specs=[spec(v.shape) for v in args],
        out_specs=[spec(v.shape) for v in outs],
        out_shape=outs,
        compiler_params=pltpu.CompilerParams(vmem_limit_bytes=VMEM_MOST),
        cost_estimate=LIGHT,
        name=name,
    )(*args)


def layer(
    nctx, nep,
    layer_input, attn_gain, q_weight, key_matrix, value_matrix, o_weight, q_gain, key_norm_gain,
    ffn_gain, router_weight, gate_weight, up_weight, down_weight, routes, out_grad,
):
    rows, width = layer_input.shape[1:]
    devices = nctx * nep
    nz = nep // 2
    np_ = nctx * 2
    nb = nctx
    experts = devices
    capacity = -(-rows * TOP * 5 // (4 * experts) // 16) * 16
    length = rows * nctx
    heads = QUERY_HEADS // nctx
    q_cols = heads * HEAD_DIM
    at_ctx = lax.axis_index("ctx")
    at_ep = lax.axis_index("ep")

    due = {}
    clock = 0

    def after(v, *done):
        return lax.optimization_barrier((v, *done))[0] if done else v

    def now(v):
        return after(v, *due.get(clock, []))

    def tick():
        nonlocal clock
        clock += 1

    def swap(v, by_ctx, by_ep, rounds=1):
        if by_ctx == 0 and by_ep == 0:
            return v
        pairs = [(i, ((i // nep) ^ by_ctx) * nep + ((i % nep) ^ by_ep)) for i in range(devices)]
        got = lax.ppermute(now(v) if rounds else v, AXES, pairs)
        if rounds:
            due.setdefault(clock + rounds, []).append(got)
        return got

    def did(v):
        due.setdefault(clock + 1, []).append(v)
        return v

    def swap_z(v, j, rounds=1):
        return swap(v, 0, 2 * j, rounds)

    def sum_over(v, bits):
        for by_ctx, by_ep in bits:
            v = v + swap(v, by_ctx, by_ep, 0)
        return v

    def place(pieces, at, axis=0):
        size = pieces[0].shape[axis]
        shape = list(pieces[0].shape)
        shape[axis] = size * len(pieces)
        whole = after(jnp.zeros(shape, pieces[0].dtype), pieces[-1])
        for i, piece in enumerate(pieces):
            whole = lax.dynamic_update_slice_in_dim(whole, piece, at(i) * size, axis)
        return whole

    def place_ep(far, near):
        return place([v for j in range(nz) for v in (far[j], near[j])], lambda i: at_ep ^ i)

    def own_rows(v, m):
        return lax.dynamic_slice_in_dim(v, (at_ctx ^ m) * rows, rows, 0)

    z_first, z_second = range(1, nz // 2 + 1), range(nz // 2 + 1, nz)
    groups = [list(range(q * nz // 4, (q + 1) * nz // 4)) for q in range(4)]

    x = layer_input[0].astype(F32)
    scale_one = lax.rsqrt(jnp.mean(x * x, axis=-1, keepdims=True) + EPSILON)
    h_one = (x * scale_one * attn_gain).astype(BF16)
    o_cols = width // nctx
    o_piece = lax.dynamic_slice_in_dim(o_weight, at_ctx * o_cols, o_cols, 1)
    qkv_piece = jnp.concatenate(
        [
            lax.dynamic_slice_in_dim(q_weight, at_ctx * q_cols, q_cols, 1),
            lax.dynamic_slice_in_dim(key_matrix, at_ctx * HEAD_DIM, HEAD_DIM, 1),
            lax.dynamic_slice_in_dim(value_matrix, at_ctx * HEAD_DIM, HEAD_DIM, 1),
        ],
        axis=1,
    )
    router_deep = router_weight.size // o_cols
    o_deep = o_piece.shape[0]
    o_piece = jnp.concatenate([o_piece, router_weight.reshape(router_deep, o_cols)])
    far_o, near_o, far_w, near_w = {0: o_piece}, {}, {0: qkv_piece}, {}
    for j in z_first:
        far_o[j] = swap_z(o_piece, j)
    near_o[0] = swap(o_piece, 0, 1)
    near_w[0] = swap(qkv_piece, 0, 1)
    h_pieces = [h_one, None, swap(h_one, 2, 0, 3), None]
    routes_t = routes[0].T
    there = [routes_t] + [None] * (nz - 1)
    for j in groups[1]:
        there[j] = swap_z(routes_t, j)
    tick()

    for j in z_second:
        far_o[j] = swap_z(o_piece, j)
    for j in z_first:
        near_o[j] = swap(far_o[j], 0, 1)
    h_pieces[1] = swap(h_one, 1, 0)
    for j in groups[2]:
        there[j] = swap_z(routes_t, j)
    tick()

    for j in z_first:
        far_w[j] = swap_z(qkv_piece, j)
    for j in z_second:
        near_o[j] = swap(far_o[j], 0, 1)
    for j in groups[0][1:] + groups[3]:
        there[j] = swap_z(routes_t, j)
    tick()

    h_pieces[3] = swap(h_pieces[2], 1, 0)
    for j in z_second:
        far_w[j] = swap_z(qkv_piece, j)
    for j in z_first:
        near_w[j] = swap(far_w[j], 0, 1)
    o_all = now(place_ep(far_o, near_o)).reshape(nep, o_deep + router_deep, o_cols)
    o_part_of = nep // nctx

    def o_block(m):
        block = lax.dynamic_slice(o_all, ((at_ctx ^ m) * o_part_of, 0, 0), (o_part_of, o_deep, o_cols))
        return block.reshape(q_cols, o_cols)

    o_pieces = {0: o_block(0), 2: swap(o_block(2), 2, 0)}
    router_full = o_all[:, o_deep:].reshape(width, experts)
    token = jnp.arange(rows, dtype=jnp.int32)
    upto = (token[:, None] <= token[None, :]).astype(BF16)
    slots = jnp.arange(capacity, dtype=jnp.int32).astype(F32)

    def slot_table(hits):
        rank = mm(hits.astype(BF16), upto) - 1.0
        return ((rank[:, None, :] == slots[None, :, None]) & (hits[:, None, :] > 0)).astype(BF16)

    places = jnp.arange(np_, dtype=jnp.int32)
    plane_experts = (at_ctx ^ (places >> 1 & ~1) ^ (places & 1)) * nep + (at_ep ^ (places >> 1 & 1))
    tables = []
    for j in range(nz):
        hits = jnp.sum((now(there[j])[None] == plane_experts[:, None, None]).astype(F32), axis=1)
        tables.append(slot_table(hits).reshape(np_ * capacity, rows))
    lane_ids = jnp.arange(-(-experts // 128) * 128, dtype=jnp.int32)
    picker = jnp.sum((routes[0][:, :, None] == lane_ids).astype(F32), axis=1)

    def pick(far, q):
        return {j: [did(v) for v in select(tables[j], [now(v) for v in far[j]], nb)] for j in groups[q]}

    def fetch(v, far, q, *parts, rounds=1):
        half = width // 2
        for j in groups[q]:
            if j and len(parts) == 2:
                far[j] = [swap_z(v, j, rounds)]
            elif j:
                far.setdefault(j, []).append(swap_z(v[:, parts[0] * half : (parts[0] + 1) * half], j, rounds))

    def post(pieces, got, q, *bs, rounds=1):
        for j in groups[q]:
            for b in bs:
                got.setdefault(j, [pieces[j][0]] + [None] * (nb - 1))[b] = swap(pieces[j][b], b & ~1, b & 1, rounds)

    def share(got, q):
        half = np_ * capacity // 2 // nb
        for j in groups[q]:
            got[j].append(swap(jnp.concatenate([v[half:] for v in got[j]], axis=0), 1, 0))

    def share_back(made, q):
        for j in groups[q]:
            made[j] = [made[j][0], swap(made[j][1], 1, 0)]

    def packed(made, q):
        for j in groups[q]:
            copies[j], outs[j] = pack(now(made[j][0]), made[j][1], nb, width)
            did(copies[j][0])

    def gather(pieces, q, shares=2):
        total = {}
        for j in groups[q]:
            ready = [now(pieces[j][0]), *pieces[j][1:]]
            total[j] = combine(tables[j], ready, BF16, shares) if j else combine(tables[j], ready, F32, 1)
            for v in total[j]:
                did(v)
        return total

    def home(total, kept, part, rounds=1):
        for j, v in total.items():
            if j:
                kept.setdefault(j, [None] * len(v))[part] = swap_z(v[part], j, rounds)
            else:
                kept[j] = v

    grad_out = out_grad[0]
    far_g, got_g = {0: [grad_out]}, {}
    tick()

    for j in z_second:
        near_w[j] = swap(far_w[j], 0, 1)
    fetch(grad_out, far_g, 2, 0)
    fetch(grad_out, far_g, 0, 0, 1)
    picked_g0 = pick(far_g, 0)
    frequency = ROPE_BASE ** (-jnp.arange(HEAD_DIM // 2).astype(F32) * 2.0 / HEAD_DIM)
    angles = jnp.arange(length).astype(F32)[:, None] * frequency[None, :]
    cosine, sine = jnp.cos(angles), jnp.sin(angles)
    cos_full = jnp.concatenate([cosine, cosine], axis=1)
    sin_full = jnp.concatenate([-sine, sine], axis=1)
    q_gain_row, k_gain_row = q_gain[None, :], key_norm_gain[None, :]
    h_full = join(h_pieces, at_ctx[None])
    flat_routes = now(jnp.concatenate(there))
    plane_routes = [flat_routes] + [swap(flat_routes, b & ~1, b & 1) for b in range(1, nb)]
    tick()

    o_pieces[3] = swap(o_block(3), 3, 0)
    o_pieces[1] = swap(o_block(1), 1, 0)
    post(picked_g0, got_g, 0, 1)
    fetch(grad_out, far_g, 2, 1)
    behind = after(grad_out, far_g[groups[2][-1]][-1])
    fetch(behind, far_g, 3, 0, rounds=2)
    qkv_weight = place_ep(far_w, near_w)
    qkv = mm(h_full, now(qkv_weight))
    attn, turned_q, turned_k, lse = attend(qkv, cos_full, sin_full, q_gain_row, k_gain_row, heads)
    did(attn)
    tick()

    router_wide = jnp.pad(router_full, ((0, 0), (0, lane_ids.shape[0] - experts)))
    fetch(grad_out, far_g, 3, 1, rounds=2)
    picked_g2 = pick(far_g, 2)
    o_rows = place([o_pieces[m] for m in range(nctx)], lambda i: at_ctx ^ i, 1)
    attn = now(attn)
    held = {}
    for hi in reversed(range(0, nctx, 2)):
        sent = swap(mm(own_rows(attn, hi + 1), o_rows).astype(BF16), 1, 0)
        held[hi] = did(mm(own_rows(attn, hi), o_rows) + sent.astype(F32))
    branch_far = swap(held[2].astype(BF16), 2, 0)
    tick()

    post(picked_g0, got_g, 0, 2, 3)
    post(picked_g2, got_g, 2, 1)
    shape = jax.ShapeDtypeStruct
    resid, h_two, scale_two = by_rows(
        second_norm_kernel,
        [held[0], now(branch_far), layer_input[0], ffn_gain[None]],
        [shape((rows, width), F32), shape((rows, width), BF16), shape((rows, 1), F32)],
        "second_norm",
    )
    far_h, got_h = {0: [h_two]}, {}
    fetch(h_two, far_h, 2, 0)
    fetch(h_two, far_h, 0, 0, 1)
    picked_h = pick(far_h, 0)
    tick()

    post(picked_h, got_h, 0, 1, 2, 3)
    share(got_g, 0)
    fetch(h_two, far_h, 2, 1)
    here_routes = now(jnp.stack(plane_routes))
    all_routes = jnp.stack([here_routes, swap(here_routes, 1, 0)])
    picked_g3 = pick(far_g, 3)
    gate, up, down = gate_weight[0], up_weight[0], down_weight[0]
    results, copies, outs, joined = {}, {}, {}, None

    def expert(q):
        nonlocal joined
        for j in groups[q]:
            h_in = [now(got_h[j][0]), *got_h[j][1:]]
            results[j], joined = expert_step(
                j, nz, h_in, got_g[j], gate, up, down, router_wide, picks, marks, joined
            )
            did(results[j][0])

    tick()

    post(picked_g2, got_g, 2, 2, 3)
    post(picked_g3, got_g, 3, 1)
    fetch(h_two, far_h, 3, 0)
    share(got_h, 0)
    picked_h2 = pick(far_h, 2)
    at_device = at_ctx * nep + at_ep
    all_routes = now(all_routes).reshape(2, nb, nz, TOP, rows).transpose(3, 2, 0, 1, 4)
    all_routes = all_routes.reshape(TOP, devices, rows)
    own_id = jnp.full((1, 128), at_device, jnp.int32)
    picks = did(pick_rows(own_id, all_routes, upto, capacity, lane_ids.shape[0]))
    extra = -(-2 * experts // 128) * 128
    extra_ids = jnp.arange(extra, dtype=jnp.int32)
    marks = jnp.stack([extra_ids == at_device, extra_ids == at_device, extra_ids == at_device + experts]).astype(F32)
    lanes = lane_ids.shape[0]
    router, gates, picked_total = by_rows(
        lambda *refs: route_kernel(experts, *refs),
        [now(h_two), router_wide, picker],
        [shape((rows, lanes), F32), shape((rows, lanes), F32), shape((rows, 1), F32)],
        "route",
    )
    did(gates)
    tick()
    post(picked_h2, got_h, 2, 1, 2, 3)
    share(got_g, 2)
    fetch(h_two, far_h, 3, 1)
    expert(0)
    tick()
    post(picked_g3, got_g, 3, 2, 3)
    fetch(grad_out, far_g, 1, 0, 1)
    picked_h3 = pick(far_h, 3)
    share(got_h, 2)
    share_back(results, 0)
    tick()
    post(picked_h3, got_h, 3, 1, 2, 3)
    share(got_g, 3)
    fetch(h_two, far_h, 1, 0, 1)
    picked_g1 = pick(far_g, 1)
    expert(2)
    tick()
    post(picked_g1, got_g, 1, 1, 2, 3)
    share(got_h, 3)
    share_back(results, 2)
    picked_h1 = pick(far_h, 1)
    packed(results, 0)
    tick()
    post(picked_h1, got_h, 1, 1, 2, 3)
    share(got_g, 1)
    expert(3)
    packed(results, 2)
    back, made = {}, {}
    tick()

    post(copies, back, 2, 1, 2, 3)
    share(got_h, 1)
    share_back(results, 3)
    packed(results, 3)
    tick()
    post(copies, back, 3, 1, 2, 3)
    total_2 = gather(back, 2)
    homes = {}
    home(total_2, homes, 0)
    for j in groups[1]:
        got_h[j][0] = after(got_h[j][0], *total_2[groups[2][-1]])
    expert(1)
    tick()
    post(copies, back, 0, 1, 2, 3)
    home(total_2, homes, 1)
    total_3 = gather(back, 3, 1)
    share_back(results, 1)
    packed(results, 1)
    joined_h, joined_g, hidden_all, grad_gate_all, grad_up_all = joined
    gate_part = did(product(joined_h, now(grad_gate_all), "tn", F32, 512))
    tick()
    post(copies, back, 1, 1, 2, 3)
    home(total_3, homes, 0, 2)
    total_0 = gather(back, 0, 1)
    up_part = did(product(joined_h, now(grad_up_all), "tn", F32, 512))
    tick()

    home(gather(back, 1, 1), homes, 0)
    home(total_0, homes, 0)
    post(outs, made, 3, 1, 2, 3)
    down_part = did(product(now(hidden_all), joined_g, "tn", F32, 256))
    tick()

    whole = [homes[j][0] for j in sorted(homes) if j and len(homes[j]) == 1]
    homes = [now(homes[0][0]), *whole, *[v for j in sorted(homes) if len(homes[j]) == 2 for v in homes[j]]]
    grad_resid, low, logit_low, ffn_gain_part = by_rows(
        lambda *refs: second_back_kernel(experts, len(homes), len(whole), *refs),
        [*homes, gates, router, picker, picked_total, router_wide, resid, scale_two, ffn_gain[None], grad_out],
        [shape((rows, width), F32), shape((rows, width), BF16), shape((rows, lanes), BF16), shape((1, width), F32)],
        "second_back",
    )
    did(low)
    homes = {}
    total_3 = gather(made, 3, 1)
    home(total_3, homes, 0, 2)
    tick()
    low_pieces = [low, swap(low, 1, 0), swap(low, 2, 0), None]
    post(outs, made, 2, 1)
    post(outs, made, 1, 1)
    tick()
    low_pieces[3] = swap(low_pieces[2], 1, 0)
    post(outs, made, 2, 2, 3, rounds=2)
    post(outs, made, 1, 3, rounds=2)
    post(outs, made, 0, 1, rounds=2)
    tick()

    branch_full = now(join(low_pieces, at_ctx[None]))
    o_own = q_cols // nep
    own_width = width // devices
    o_part = product(attn, branch_full, "tn", F32, 256)
    router_part = t_mm(logit_low, h_two)[:experts].reshape(experts, nctx, nep, own_width)
    router_rows = experts * nctx * own_width // width

    def o_term(j, ry):
        place_of = at_ep ^ (2 * j + ry)
        block = lax.dynamic_slice_in_dim(o_part, place_of * o_own, o_own, 0)
        router_block = lax.dynamic_slice_in_dim(router_part, place_of, 1, 2).reshape(router_rows, width)
        return jnp.concatenate([block, router_block], axis=0)

    last_steps = list(reversed(range(nz)))
    o_sent = {j: did(o_term(j, 1).astype(BF16)) for j in last_steps}
    grad_attn = did(product(branch_full, o_rows, "nt", BF16, 512))
    for j in groups[2]:
        made[j][0] = after(made[j][0], grad_attn)
    total_2 = gather(made, 2, 1)
    home(total_2, homes, 0, 2)
    tick()

    o_near = {j: swap(o_sent[j], 0, 1) for j in last_steps[:-1]}
    post(outs, made, 1, 2)
    grad_qkv, q_gain_part, k_gain_part = attend_back(
        qkv, turned_q, turned_k, attn, lse, now(grad_attn), cos_full, sin_full, q_gain_row, k_gain_row, heads
    )
    did(grad_qkv)
    tick()

    post(outs, made, 0, 2, 3)
    o_near[0] = swap(o_sent[0], 0, 1)
    o_far = {}
    o_mid = {j: (o_term(j, 0) + now(o_near[j]).astype(F32)).astype(BF16) for j in last_steps[:-1]}
    for j in last_steps[: nz // 4]:
        o_far[j] = swap_z(o_mid[j], j)
    qkv_part = product(h_full, now(grad_qkv), "tn", F32, 512).reshape(nctx, nep, own_width, -1)

    def qkv_term(j, ry):
        return lax.dynamic_slice_in_dim(qkv_part, at_ep ^ (2 * j + ry), 1, 1)[:, 0]

    qkv_sent = {j: did(qkv_term(j, 1).astype(BF16)) for j in last_steps}
    one_term = lambda m, plus, dtype: product(
        own_rows(grad_qkv, m), qkv_weight, "nt", dtype, 1024, plus
    )
    sent = [did(one_term(m, None, BF16)) for m in (3, 1)]
    tick()

    first_steps, other_steps = last_steps[::2], last_steps[1::2]
    qkv_near = {j: swap(qkv_sent[j], 0, 1) for j in first_steps}
    sent = [swap(v, 1, 0) for v in sent]
    for j in last_steps[nz // 4 : -1]:
        o_far[j] = swap_z(o_mid[j], j)
    total_1, total_0 = gather(made, 1, 1), gather(made, 0, 1)
    held = [did(one_term(0, sent[1], F32)), did(one_term(2, sent[0], BF16))]
    tick()

    qkv_near.update({j: swap(qkv_sent[j], 0, 1) for j in other_steps})
    one_far = swap(held[1], 2, 0)
    qkv_mid = lambda j: (qkv_term(j, 0) + now(qkv_near[j]).astype(F32)).astype(BF16)
    qkv_far = {j: swap_z(qkv_mid(j), j) for j in last_steps[: nz // 4]}
    home(total_1, homes, 0)
    o_sum = o_term(0, 0) + o_near[0].astype(F32)
    for j in range(1, nz):
        o_sum = o_sum + now(o_far[j]).astype(F32)
    o_grad = did(o_sum[:o_own])
    router_sum = did(o_sum[o_own:].reshape(experts, nctx, own_width).transpose(1, 2, 0))
    input_grad, attn_gain_part = by_rows(
        first_back_kernel,
        [held[0], one_far, layer_input[0], scale_one, attn_gain[None], grad_resid],
        [shape((rows, width), F32), shape((1, width), F32)],
        "first_back",
    )
    did(input_grad)
    tick()

    qkv_far.update({j: swap_z(qkv_mid(j), j) for j in last_steps[nz // 4 : -1]})
    home(total_0, homes, 0)
    late = jnp.concatenate([now(attn_gain_part)[0], ffn_gain_part[0], q_gain_part[0], k_gain_part[0]])
    late = did(sum_over(late, [(1 << b, 0) for b in range(nctx.bit_length() - 1)] + [(0, 1)]))
    tick()

    qkv_sum = qkv_term(0, 0) + qkv_near[0].astype(F32)
    for j in range(1, nz):
        qkv_sum = qkv_sum + now(qkv_far[j]).astype(F32)
    last = jnp.concatenate([qkv_sum, router_sum], axis=2).astype(BF16)
    last_block = lambda m: lax.dynamic_index_in_dim(last, at_ctx ^ m, 0)
    last = place([swap(last_block(m), m, 0) for m in range(nctx)], lambda i: at_ctx ^ i).astype(F32)
    late = sum_over(now(late), [(0, 2 << b) for b in range(nz.bit_length() - 1)])
    qkv_grad = last
    router_grad = jnp.sum(last[:, :, q_cols + 2 * HEAD_DIM :], axis=0)
    mixed = resid
    for j in sorted(homes):
        mixed = mixed + jnp.concatenate(homes[j]).astype(F32)

    def columns(first, last):
        return jnp.concatenate([qkv_grad[c, :, first:last] for c in range(nctx)], axis=1)

    return (
        mixed.astype(BF16)[None],
        input_grad[None],
        late[:width],
        columns(0, q_cols),
        columns(q_cols, q_cols + HEAD_DIM),
        columns(q_cols + HEAD_DIM, q_cols + 2 * HEAD_DIM),
        o_grad,
        late[2 * width : 2 * width + HEAD_DIM],
        late[2 * width + HEAD_DIM :],
        late[width : 2 * width],
        router_grad,
        gate_part[None],
        up_part[None],
        down_part[None],
    )


def solution(mesh):
    nctx, nep = mesh.shape["ctx"], mesh.shape["ep"]
    tokens = P("ep", "ctx", None)
    own = P(("ctx", "ep"), None)
    expert = P(("ctx", "ep"), None, None)
    split_rows = P("ep", None)

    def on_device(*arrays):
        return layer(nctx, nep, *arrays)

    return jax.shard_map(
        on_device,
        mesh=mesh,
        in_specs=(
            tokens, P(), split_rows, split_rows, split_rows, split_rows, P(), P(), P(), split_rows,
            expert, expert, expert, tokens, tokens,
        ),
        out_specs=(
            tokens, tokens, P(), own, own, own, own, P(), P(), P(), own, expert, expert, expert,
        ),
        check_vma=False,
    )
```

```python
import math

import jax
import jax.numpy as jnp
from jax import lax
from jax.experimental import pallas as pl
from jax.experimental.pallas import tpu as pltpu
from jax.sharding import PartitionSpec as P

QUERY_HEADS = 32
KEY_VALUE_HEADS = 4
HEAD_DIM = 128
TOP = 8
BLOCK = 256

EPSILON = 1e-06
ROPE_BASE = 1000000.0
LOG2_E = 1.4426950408889634
F32 = jnp.float32
BF16 = jnp.bfloat16
AXES = ("ctx", "ep")
HIGHEST = lax.Precision.HIGHEST


def mm(a, b):
    return jnp.dot(a, b, preferred_element_type=F32)


def mm_t(a, b):
    return lax.dot_general(a, b, (((1,), (1,)), ((), ())), preferred_element_type=F32)


def t_mm(a, b):
    return lax.dot_general(a, b, (((0,), (0,)), ((), ())), preferred_element_type=F32)


LIGHT = pl.CostEstimate(flops=1, bytes_accessed=1, transcendentals=0)
VMEM_MOST = 56 * 1024 * 1024


def half_turn(v):
    return pltpu.roll(v, HEAD_DIM // 2, 1)


def head_norm(v, gain):
    scale = lax.rsqrt(jnp.mean(v * v, axis=-1, keepdims=True) + EPSILON)
    return v * scale * gain


def head_norm_back(v, gain, dy):
    scale = lax.rsqrt(jnp.mean(v * v, axis=-1, keepdims=True) + EPSILON)
    lifted = gain * dy
    inner = jnp.mean(v * lifted, axis=-1, keepdims=True)
    return (
        scale * lifted - v * (scale * scale * scale * inner),
        jnp.sum(v * scale * dy, axis=0, keepdims=True),
    )


def diagonal_mask():
    key_at = lax.broadcasted_iota(jnp.int32, (BLOCK, BLOCK), 0)
    query_at = lax.broadcasted_iota(jnp.int32, (BLOCK, BLOCK), 1)
    return key_at <= query_at


def attend_kernel(
    q_ref, k_ref, v_ref, cos_ref, sin_ref, qg_ref, kg_ref,
    out_ref, qr_ref, kr_ref, lse_ref, keys, values_t,
):
    blocks = q_ref.shape[0] // BLOCK
    coefficient = LOG2_E * HEAD_DIM ** (-0.5)

    @pl.when(pl.program_id(0) == 0)
    def _():
        normed = head_norm(k_ref[...], kg_ref[...])
        turned = (normed * cos_ref[...] + half_turn(normed) * sin_ref[...]).astype(BF16)
        keys[...] = turned
        kr_ref[...] = turned
        values_t[...] = v_ref[...].T.astype(BF16)

    normed = head_norm(q_ref[...], qg_ref[...])
    queries = (normed * cos_ref[...] + half_turn(normed) * sin_ref[...]).astype(BF16)
    qr_ref[...] = queries
    visible = diagonal_mask()
    for i in range(blocks):
        low, high = i * BLOCK, (i + 1) * BLOCK
        q_i = queries[low:high]
        s_in = jnp.where(visible, mm_t(keys[low:high, :], q_i) * coefficient, -1e30)
        top = jnp.max(s_in, axis=0, keepdims=True)
        if i:
            s_off = mm_t(keys[:low, :], q_i) * coefficient
            top = jnp.maximum(top, jnp.max(s_off, axis=0, keepdims=True))
        p_in = jnp.exp2(s_in - top)
        total = jnp.sum(p_in, axis=0, keepdims=True)
        mixed = mm(values_t[:, low:high], p_in.astype(BF16))
        if i:
            p_off = jnp.exp2(s_off - top)
            total = total + jnp.sum(p_off, axis=0, keepdims=True)
            mixed = mixed + mm(values_t[:, :low], p_off.astype(BF16))
        out_ref[low:high, :] = (mixed * (1.0 / total)).T.astype(BF16)
        lse_ref[0, :, low:high] = top + jnp.log2(total)


def attend_back_kernel(
    qr_ref, q_ref, do_ref, out_ref, lse_ref, kr_ref, k_ref, v_ref, cos_ref, sin_ref, qg_ref, kg_ref,
    grad_ref, qgain_ref, kgain_ref, keys_t, values, dk, dv, dq,
):
    step = pl.program_id(0)
    heads = pl.num_programs(0) - 2
    blocks = q_ref.shape[0] // BLOCK
    scale = HEAD_DIM ** (-0.5)
    coefficient = LOG2_E * scale

    @pl.when(step == 0)
    def _():
        keys_t[...] = kr_ref[...].astype(F32).T.astype(BF16)
        values[...] = v_ref[...].astype(BF16)
        dk[...] = jnp.zeros_like(dk)
        dv[...] = jnp.zeros_like(dv)
        qgain_ref[...] = jnp.zeros_like(qgain_ref)

    def turn_back(v):
        return v * cos_ref[...] - half_turn(v) * sin_ref[...]

    @pl.when(step < heads)
    def _():
        delta = jnp.sum((do_ref[...].astype(F32) * out_ref[...].astype(F32)).T, axis=0, keepdims=True)
        visible = diagonal_mask()
        for i in range(blocks):
            low, high = i * BLOCK, (i + 1) * BLOCK
            q_i = qr_ref[low:high, :]
            do_i = do_ref[low:high, :]
            lse_i = lse_ref[0, :, low:high]
            delta_i = delta[:, low:high]

            def part(first, last, masked):
                p = jnp.exp2(mm_t(kr_ref[first:last, :], q_i) * coefficient - lse_i)
                if masked:
                    p = jnp.where(visible, p, 0.0)
                dp = mm_t(values[first:last, :], do_i)
                dv[first:last, :] += mm(p.astype(BF16), do_i)
                ds = (p * (dp - delta_i)).astype(BF16)
                dk[first:last, :] += mm(ds, q_i)
                return mm(keys_t[:, first:last], ds)

            turned = part(low, high, True)
            if i:
                turned = turned + part(0, low, False)
            dq[low:high, :] = turned.T * scale
        back, gain_part = head_norm_back(q_ref[...], qg_ref[...], turn_back(dq[...]))
        grad_ref[...] = back.astype(BF16)
        qgain_ref[...] += gain_part

    @pl.when(step == heads)
    def _():
        back, gain_part = head_norm_back(k_ref[...], kg_ref[...], turn_back(dk[...] * scale))
        grad_ref[...] = back.astype(BF16)
        kgain_ref[...] = gain_part

    @pl.when(step == heads + 1)
    def _():
        grad_ref[...] = dv[...].astype(BF16)


def attend(qkv, cos, sin, q_gain, k_gain, heads):
    length = qkv.shape[0]
    column = lambda at: pl.BlockSpec((length, HEAD_DIM), lambda h: (0, at))
    moving = pl.BlockSpec((length, HEAD_DIM), lambda h: (0, h))
    fixed = pl.BlockSpec((length, HEAD_DIM), lambda h: (0, 0))
    row = pl.BlockSpec((1, HEAD_DIM), lambda h: (0, 0))
    return pl.pallas_call(
        attend_kernel,
        grid=(heads,),
        in_specs=[moving, column(heads), column(heads + 1), fixed, fixed, row, row],
        out_specs=[moving, moving, fixed, pl.BlockSpec((1, 1, length), lambda h: (h, 0, 0))],
        out_shape=[
            jax.ShapeDtypeStruct((length, heads * HEAD_DIM), BF16),
            jax.ShapeDtypeStruct((length, heads * HEAD_DIM), BF16),
            jax.ShapeDtypeStruct((length, HEAD_DIM), BF16),
            jax.ShapeDtypeStruct((heads, 1, length), F32),
        ],
        scratch_shapes=[pltpu.VMEM((length, HEAD_DIM), BF16), pltpu.VMEM((HEAD_DIM, length), BF16)],
        compiler_params=pltpu.CompilerParams(vmem_limit_bytes=40 * 1024 * 1024),
        cost_estimate=LIGHT,
        name="attend",
    )(qkv, qkv, qkv, cos, sin, q_gain, k_gain)


def attend_back(qkv, turned_q, turned_k, out, lse, grad_out, cos, sin, q_gain, k_gain, heads):
    length = qkv.shape[0]
    column = lambda at: pl.BlockSpec((length, HEAD_DIM), lambda h: (0, at))
    moving = pl.BlockSpec((length, HEAD_DIM), lambda h: (0, jnp.minimum(h, heads - 1)))
    fixed = pl.BlockSpec((length, HEAD_DIM), lambda h: (0, 0))
    row = pl.BlockSpec((1, HEAD_DIM), lambda h: (0, 0))
    return pl.pallas_call(
        attend_back_kernel,
        grid=(heads + 2,),
        in_specs=[
            moving, moving, moving, moving,
            pl.BlockSpec((1, 1, length), lambda h: (jnp.minimum(h, heads - 1), 0, 0)),
            fixed, column(heads), column(heads + 1), fixed, fixed, row, row,
        ],
        out_specs=[pl.BlockSpec((length, HEAD_DIM), lambda h: (0, h)), row, row],
        out_shape=[
            jax.ShapeDtypeStruct((length, (heads + 2) * HEAD_DIM), BF16),
            jax.ShapeDtypeStruct((1, HEAD_DIM), F32),
            jax.ShapeDtypeStruct((1, HEAD_DIM), F32),
        ],
        scratch_shapes=[
            pltpu.VMEM((HEAD_DIM, length), BF16),
            pltpu.VMEM((length, HEAD_DIM), BF16),
            pltpu.VMEM((length, HEAD_DIM), F32),
            pltpu.VMEM((length, HEAD_DIM), F32),
            pltpu.VMEM((length, HEAD_DIM), F32),
        ],
        compiler_params=pltpu.CompilerParams(vmem_limit_bytes=40 * 1024 * 1024),
        cost_estimate=LIGHT,
        name="attend_back",
    )(turned_q, qkv, grad_out, out, lse, turned_k, qkv, qkv, cos, sin, q_gain, k_gain)


def select_kernel(n_parts, table, *refs):
    parts, outs = refs[:n_parts], refs[n_parts:]
    deep = outs[0].shape[0]
    first = 0
    for part in parts:
        for at in range(0, part.shape[1], 1024):
            wide = min(1024, part.shape[1] - at)
            rows = mm(table[...], part[:, at : at + wide]).astype(BF16)
            for b, out in enumerate(outs):
                out[:, first : first + wide] = rows[b * deep : (b + 1) * deep]
            first += wide


def select(table, parts, chips):
    width, deep = sum(v.shape[1] for v in parts), table.shape[0] // chips
    return pl.pallas_call(
        lambda *refs: select_kernel(len(parts), *refs),
        out_shape=[jax.ShapeDtypeStruct((deep, width), BF16)] * chips,
        compiler_params=pltpu.CompilerParams(vmem_limit_bytes=VMEM_MOST),
        cost_estimate=LIGHT,
        name="select",
    )(table, *parts)


def combine_kernel(n_pieces, table, *refs):
    pieces, outs = refs[:n_pieces], refs[n_pieces:]
    deep, width = outs[0].shape
    for first in range(0, width, 512):
        at = slice(first, min(first + 512, width))
        rows = jnp.concatenate([p[:, at] for p in pieces], axis=0)
        total = t_mm(table[...], rows)
        for i, out in enumerate(outs):
            out[:, at] = total[i * deep : (i + 1) * deep].astype(out.dtype)


def combine(table, pieces, dtype, shares):
    shape = (table.shape[1] // shares, pieces[0].shape[1])
    return pl.pallas_call(
        lambda *refs: combine_kernel(len(pieces), *refs),
        out_shape=[jax.ShapeDtypeStruct(shape, dtype)] * shares,
        compiler_params=pltpu.CompilerParams(vmem_limit_bytes=VMEM_MOST),
        cost_estimate=LIGHT,
        name="combine",
    )(table, *pieces)


def pack_kernel(chips, near, other, *outs):
    deep = outs[0].shape[0] // 2
    first = 0
    for group in (outs[:chips], outs[chips:]):
        at = slice(first, first + group[0].shape[1])
        for b, out in enumerate(group):
            out[:deep, :] = near[b * deep : (b + 1) * deep, at]
            out[deep:, :] = other[b * deep : (b + 1) * deep, at]
        first = at.stop


def pack(near, other, chips, width):
    deep, first = 2 * near.shape[0] // chips, near.shape[1] - width
    got = pl.pallas_call(
        lambda *refs: pack_kernel(chips, *refs),
        out_shape=[jax.ShapeDtypeStruct((deep, n), BF16) for n in (first, width) for _ in range(chips)],
        compiler_params=pltpu.CompilerParams(vmem_limit_bytes=VMEM_MOST),
        cost_estimate=LIGHT,
        name="pack",
    )(near, other)
    return got[:chips], got[chips:]


def expert_kernel(chips, ff_tiles, n_in, *refs):
    h_in, g_in = refs[: chips + 1], refs[chips + 1 : 2 * chips + 2]
    gate_c, up_c, down_r, gate_r, up_r, down_c, router, picks, marks = refs[2 * chips + 2 : 2 * chips + 11]
    results = refs[n_in : n_in + 2]
    h_all, g_all, hid_all, gg_all, gu_all, scale, dots = refs[n_in + 2 :]
    step = pl.program_id(0)
    deep = h_in[0].shape[0] // 2
    half = chips * deep
    wide, out_wide = gate_c.shape[1], down_c.shape[1]
    width = h_in[0].shape[1]

    @pl.when(step == 0)
    def _():
        for arrived, joined in ((h_in, h_all), (g_in, g_all)):
            for b in range(chips):
                joined[b * deep : (b + 1) * deep, :] = arrived[b][:deep, :]
            joined[half:, :] = arrived[chips][...]
        dots[...] = jnp.zeros_like(dots)
        logits = mm(h_all[...], router[...])
        picked = picks[...] > 0
        top = jnp.max(jnp.where(picked, logits, -1e30), axis=-1, keepdims=True)
        weight = jnp.where(picked, jnp.exp(logits - top), 0.0)
        total = jnp.sum(weight, axis=-1, keepdims=True)
        own = jnp.sum(weight * marks[0:1, : logits.shape[1]], axis=-1, keepdims=True)
        scale[...] = own / jnp.where(total > 0, total, 1.0)

    @pl.when(step < ff_tiles)
    def _():
        gate_proj = mm(h_all[...], gate_c[...])
        up_proj = mm(h_all[...], up_c[...])
        grad_hidden = mm_t(g_all[...], down_r[...])
        at = pl.ds(pl.multiple_of(step * wide, wide), wide)
        sigmoid = jax.nn.sigmoid(gate_proj)
        turned = gate_proj * sigmoid
        hidden = turned * up_proj
        dots[...] += jnp.sum(hidden * grad_hidden, axis=-1, keepdims=True)
        weighted = grad_hidden * scale[...]
        hid_all[:, at] = (hidden * scale[...]).astype(BF16)
        gu_all[:, at] = (weighted * turned).astype(BF16)
        gg_all[:, at] = (weighted * up_proj * (sigmoid + turned * (1.0 - sigmoid))).astype(BF16)

    @pl.when(step >= ff_tiles)
    def _():
        back = (mm_t(gg_all[...], gate_r[...]) + mm_t(gu_all[...], up_r[...])).astype(BF16)
        made = mm(hid_all[...], down_c[...]).astype(BF16)
        at = pl.multiple_of((step - ff_tiles) * out_wide, out_wide)
        behind = pl.multiple_of(at + width + marks.shape[1], 128)
        for core in range(2):
            results[core][:, pl.ds(at, out_wide)] = back[core * half : (core + 1) * half]
            results[core][:, pl.ds(behind, out_wide)] = made[core * half : (core + 1) * half]

    @pl.when(step == ff_tiles)
    def _():
        high = dots[...].astype(BF16).astype(F32)
        tagged = (high * marks[1:2, :] + (dots[...] - high) * marks[2:3, :]).astype(BF16)
        for core in range(2):
            results[core][:, width : width + marks.shape[1]] = tagged[core * half : (core + 1) * half]


def expert_step(j, steps, h_in, g_in, gate, up, down, router, picks, marks, joined):
    chips, (deep, width), ff = len(h_in) - 1, h_in[0].shape, down.shape[0]
    rows, extra = chips * deep, marks.shape[1]
    half = rows // 2
    ff_tile, out_tile = min(256, ff), min(512, width)
    ff_tiles, out_tiles = ff // ff_tile, width // out_tile
    first = lambda i: jnp.minimum(i, ff_tiles - 1)
    second = lambda i: jnp.maximum(i - ff_tiles, 0)
    whole = lambda shape: pl.BlockSpec(shape, lambda i: (0, 0))
    here = lambda n: pl.BlockSpec((rows, n), lambda i: (j, 0))
    in_specs = ([whole((deep, width))] * chips + [whole((half, width))]) * 2 + [
        pl.BlockSpec((width, ff_tile), lambda i: (0, first(i))),
        pl.BlockSpec((width, ff_tile), lambda i: (0, first(i))),
        pl.BlockSpec((ff_tile, width), lambda i: (first(i), 0)),
        pl.BlockSpec((out_tile, ff), lambda i: (second(i), 0)),
        pl.BlockSpec((out_tile, ff), lambda i: (second(i), 0)),
        pl.BlockSpec((ff, out_tile), lambda i: (0, second(i))),
        whole(router.shape),
        pl.BlockSpec((rows, picks.shape[1]), lambda i: (j, 0)),
        whole(marks.shape),
    ]
    args = [*h_in, *g_in, gate, up, down, gate, up, down, router, picks, marks]
    aliases = {}
    if joined:
        aliases = {len(args) + i: 2 + i for i in range(len(joined))}
        args += joined
        in_specs += [pl.BlockSpec(memory_space=pl.ANY)] * len(joined)
    got = pl.pallas_call(
        lambda *refs: expert_kernel(chips, ff_tiles, len(args), *refs),
        grid=(ff_tiles + out_tiles,),
        in_specs=in_specs,
        out_specs=[whole((half, 2 * width + extra))] * 2
        + [here(width), here(width), here(ff), here(ff), here(ff)],
        out_shape=[jax.ShapeDtypeStruct((half, 2 * width + extra), BF16)] * 2
        + [jax.ShapeDtypeStruct((steps * rows, n), BF16) for n in (width, width, ff, ff, ff)],
        scratch_shapes=[pltpu.VMEM((rows, 1), F32), pltpu.VMEM((rows, 1), F32)],
        input_output_aliases=aliases,
        compiler_params=pltpu.CompilerParams(vmem_limit_bytes=VMEM_MOST),
        cost_estimate=LIGHT,
        name="expert",
    )(*args)
    return got[:2], list(got[2:])


def picks_kernel(capacity, own, routes, upto, out):
    top, sources, rows = routes.shape
    lanes = out.shape[1]
    hits = jnp.zeros((sources, rows), F32)
    for i in range(top):
        hits = hits + (routes[i] == own[0:1, 0:1]).astype(F32)
    rank = jnp.where(hits > 0, mm(hits.astype(BF16), upto[...]) - 1.0, -1.0)
    slot = lax.broadcasted_iota(jnp.int32, (capacity, rows), 0).astype(F32)
    lane = lax.broadcasted_iota(jnp.int32, (lanes, rows), 0)
    for source in range(sources):
        table = (rank[source : source + 1] == slot).astype(BF16)
        named = jnp.zeros((lanes, rows), F32)
        for i in range(top):
            named = named + (routes[i, source : source + 1, :] == lane).astype(F32)
        out[source * capacity : (source + 1) * capacity, :] = mm_t(table, named.astype(BF16)).astype(BF16)


def pick_rows(own, routes, upto, capacity, lanes):
    return pl.pallas_call(
        lambda *refs: picks_kernel(capacity, *refs),
        out_shape=jax.ShapeDtypeStruct((routes.shape[1] * capacity, lanes), BF16),
        compiler_params=pltpu.CompilerParams(vmem_limit_bytes=VMEM_MOST),
        cost_estimate=LIGHT,
        name="picks",
    )(own, routes, upto)


def join_kernel(at, *refs):
    pieces, out = refs[:-1], refs[-1]
    for i, piece in enumerate(pieces):

        @pl.when((at[0] ^ pl.program_id(0)) == i)
        def _(piece=piece):
            out[...] = piece[...]


def join(pieces, at):
    deep, width = pieces[0].shape
    return pl.pallas_call(
        join_kernel,
        grid=(len(pieces),),
        in_specs=[pl.BlockSpec(memory_space=pltpu.SMEM)]
        + [pl.BlockSpec((deep, width), lambda i: (0, 0))] * len(pieces),
        out_specs=pl.BlockSpec((deep, width), lambda i: (i, 0)),
        out_shape=jax.ShapeDtypeStruct((len(pieces) * deep, width), pieces[0].dtype),
        compiler_params=pltpu.CompilerParams(vmem_limit_bytes=VMEM_MOST),
        cost_estimate=LIGHT,
        name="join",
    )(at, *pieces)


def product_kernel(kind, dtype, a, b, *rest):
    out = rest[-1]
    dims = {"nn": ((1,), (0,)), "nt": ((1,), (1,)), "tn": ((0,), (0,))}[kind]
    made = lax.dot_general(a[...], b[...], (dims, ((), ())), preferred_element_type=F32)
    if len(rest) == 2:
        made = made + rest[0][...].astype(F32)
    out[...] = made.astype(dtype)


def product(a, b, kind, dtype, tile, plus=None):
    m, n = a.shape[1 if kind == "tn" else 0], b.shape[0 if kind == "nt" else 1]
    tile = min(tile, m if kind == "tn" else n)
    whole = lambda v: pl.BlockSpec(v.shape, lambda i: (0, 0))
    if kind == "tn":
        specs = [pl.BlockSpec((a.shape[0], tile), lambda i: (0, i)), whole(b)]
        out_spec = pl.BlockSpec((tile, n), lambda i: (i, 0))
    else:
        b_spec = pl.BlockSpec((b.shape[0], tile), lambda i: (0, i))
        if kind == "nt":
            b_spec = pl.BlockSpec((tile, b.shape[1]), lambda i: (i, 0))
        specs = [whole(a), b_spec]
        out_spec = pl.BlockSpec((m, tile), lambda i: (0, i))
    args = [a, b] if plus is None else [a, b, plus]
    return pl.pallas_call(
        lambda *refs: product_kernel(kind, dtype, *refs),
        grid=((m if kind == "tn" else n) // tile,),
        in_specs=specs if plus is None else [*specs, out_spec],
        out_specs=out_spec,
        out_shape=jax.ShapeDtypeStruct((m, n), dtype),
        compiler_params=pltpu.CompilerParams(vmem_limit_bytes=VMEM_MOST),
        cost_estimate=LIGHT,
        name="product",
    )(*args)


def second_norm_kernel(held, arrived, x, gain, resid, normed, scale):
    total = x[...].astype(F32) + held[...] + arrived[...].astype(F32)
    factor = lax.rsqrt(jnp.mean(total * total, axis=-1, keepdims=True) + EPSILON)
    resid[...] = total
    normed[...] = (total * factor * gain[...]).astype(BF16)
    scale[...] = factor


def route_kernel(experts, h, router_weight, picker, router, gates, total):
    logits = mm(h[...], router_weight[...])
    real = lax.broadcasted_iota(jnp.int32, logits.shape, 1) < experts
    logits = jnp.where(real, logits, -1e30)
    shifted = jnp.where(real, jnp.exp(logits - jnp.max(logits, axis=-1, keepdims=True)), 0.0)
    probs = shifted / jnp.sum(shifted, axis=-1, keepdims=True)
    picked = picker[...] * probs
    picked_total = jnp.sum(picked, axis=-1, keepdims=True)
    router[...] = probs
    gates[...] = picked / picked_total
    total[...] = picked_total


def norm_back(v, scale, gain, dy):
    lifted = gain * dy
    inner = jnp.mean(v * lifted, axis=-1, keepdims=True)
    return scale * lifted - v * (scale * scale * scale * inner), jnp.sum(v * scale * dy, axis=0, keepdims=True)


def second_back_kernel(experts, n_homes, n_whole, *refs):
    homes = refs[:n_homes]
    gates, router, picker, total, router_weight, resid, scale, gain, grad_out = refs[n_homes : n_homes + 9]
    grad_resid, low, logit_low, gain_part = refs[n_homes + 9 :]
    width, lanes = resid.shape[1], router.shape[1]
    arrived = homes[0][...]
    for home in homes[1 : 1 + n_whole]:
        arrived = arrived + home[...].astype(F32)
    for upper, lower in zip(homes[1 + n_whole :: 2], homes[2 + n_whole :: 2]):
        arrived = arrived + jnp.where(pl.program_id(0) == 0, upper[...].astype(F32), lower[...].astype(F32))
    tags = arrived[:, width:]
    if tags.shape[1] == lanes:
        dots = tags + pltpu.roll(tags, lanes - experts, 1)
    else:
        dots = tags[:, :lanes] + tags[:, lanes : 2 * lanes]
    probs, chosen = router[...], picker[...]
    dots = jnp.where(chosen > 0, dots, 0.0)
    grad_pick = chosen * (dots - jnp.sum(dots * gates[...], axis=-1, keepdims=True)) / total[...]
    grad_logits = probs * (grad_pick - jnp.sum(probs * grad_pick, axis=-1, keepdims=True))
    logit_low[...] = grad_logits.astype(BF16)
    grad_two = arrived[:, :width] + mm_t(grad_logits.astype(BF16), router_weight[...])
    back, part = norm_back(resid[...], scale[...], gain[...], grad_two)
    back = back + grad_out[...].astype(F32)
    grad_resid[...] = back
    low[...] = back.astype(BF16)
    gain_part[...] = jnp.where(pl.program_id(0) == 0, 0.0, gain_part[...]) + part


def first_back_kernel(held, arrived, x, scale, gain, grad_resid, input_grad, gain_part):
    dy = held[...] + arrived[...].astype(F32)
    back, part = norm_back(x[...].astype(F32), scale[...], gain[...], dy)
    input_grad[...] = grad_resid[...] + back
    gain_part[...] = jnp.where(pl.program_id(0) == 0, 0.0, gain_part[...]) + part


def by_rows(kernel, args, outs, name, step=128):
    rows = args[0].shape[0]

    def spec(shape):
        if shape[0] == rows:
            return pl.BlockSpec((step, shape[1]), lambda i: (i, 0))
        return pl.BlockSpec(shape, lambda i: (0, 0))

    return pl.pallas_call(
        kernel,
        grid=(rows // step,),
        in_specs=[spec(v.shape) for v in args],
        out_specs=[spec(v.shape) for v in outs],
        out_shape=outs,
        compiler_params=pltpu.CompilerParams(vmem_limit_bytes=VMEM_MOST),
        cost_estimate=LIGHT,
        name=name,
    )(*args)


def layer(
    nctx, nep,
    layer_input, attn_gain, q_weight, key_matrix, value_matrix, o_weight, q_gain, key_norm_gain,
    ffn_gain, router_weight, gate_weight, up_weight, down_weight, routes, out_grad,
):
    rows, width = layer_input.shape[1:]
    devices = nctx * nep
    nz = nep // 2
    np_ = nctx * 2
    nb = nctx
    experts = devices
    capacity = -(-rows * TOP * 5 // (4 * experts) // 16) * 16
    length = rows * nctx
    heads = QUERY_HEADS // nctx
    q_cols = heads * HEAD_DIM
    at_ctx = lax.axis_index("ctx")
    at_ep = lax.axis_index("ep")

    due = {}
    clock = 0

    def after(v, *done):
        return lax.optimization_barrier((v, *done))[0] if done else v

    def now(v):
        return after(v, *due.get(clock, []))

    def tick():
        nonlocal clock
        clock += 1

    def swap(v, by_ctx, by_ep, rounds=1):
        if by_ctx == 0 and by_ep == 0:
            return v
        pairs = [(i, ((i // nep) ^ by_ctx) * nep + ((i % nep) ^ by_ep)) for i in range(devices)]
        got = lax.ppermute(now(v) if rounds else v, AXES, pairs)
        if rounds:
            due.setdefault(clock + rounds, []).append(got)
        return got

    def did(v):
        due.setdefault(clock + 1, []).append(v)
        return v

    def swap_z(v, j, rounds=1):
        return swap(v, 0, 2 * j, rounds)

    def sum_over(v, bits):
        for by_ctx, by_ep in bits:
            v = v + swap(v, by_ctx, by_ep, 0)
        return v

    def place(pieces, at, axis=0):
        size = pieces[0].shape[axis]
        shape = list(pieces[0].shape)
        shape[axis] = size * len(pieces)
        whole = after(jnp.zeros(shape, pieces[0].dtype), pieces[-1])
        for i, piece in enumerate(pieces):
            whole = lax.dynamic_update_slice_in_dim(whole, piece, at(i) * size, axis)
        return whole

    def place_ep(far, near):
        return place([v for j in range(nz) for v in (far[j], near[j])], lambda i: at_ep ^ i)

    def own_rows(v, m):
        return lax.dynamic_slice_in_dim(v, (at_ctx ^ m) * rows, rows, 0)

    z_first, z_second = range(1, nz // 2 + 1), range(nz // 2 + 1, nz)
    groups = [list(range(q * nz // 4, (q + 1) * nz // 4)) for q in range(4)]

    x = layer_input[0].astype(F32)
    scale_one = lax.rsqrt(jnp.mean(x * x, axis=-1, keepdims=True) + EPSILON)
    h_one = (x * scale_one * attn_gain).astype(BF16)
    o_cols = width // nctx
    o_piece = lax.dynamic_slice_in_dim(o_weight, at_ctx * o_cols, o_cols, 1)
    qkv_piece = jnp.concatenate(
        [
            lax.dynamic_slice_in_dim(q_weight, at_ctx * q_cols, q_cols, 1),
            lax.dynamic_slice_in_dim(key_matrix, at_ctx * HEAD_DIM, HEAD_DIM, 1),
            lax.dynamic_slice_in_dim(value_matrix, at_ctx * HEAD_DIM, HEAD_DIM, 1),
        ],
        axis=1,
    )
    router_deep = router_weight.size // o_cols
    o_deep = o_piece.shape[0]
    o_piece = jnp.concatenate([o_piece, router_weight.reshape(router_deep, o_cols)])
    far_o, near_o, far_w, near_w = {0: o_piece}, {}, {0: qkv_piece}, {}
    for j in z_first:
        far_o[j] = swap_z(o_piece, j)
    near_o[0] = swap(o_piece, 0, 1)
    near_w[0] = swap(qkv_piece, 0, 1)
    h_pieces = [h_one, None, swap(h_one, 2, 0, 3), None]
    routes_t = routes[0].T
    there = [routes_t] + [None] * (nz - 1)
    for j in groups[1]:
        there[j] = swap_z(routes_t, j)
    tick()

    for j in z_second:
        far_o[j] = swap_z(o_piece, j)
    for j in z_first:
        near_o[j] = swap(far_o[j], 0, 1)
    h_pieces[1] = swap(h_one, 1, 0)
    for j in groups[2]:
        there[j] = swap_z(routes_t, j)
    tick()

    for j in z_first:
        far_w[j] = swap_z(qkv_piece, j)
    for j in z_second:
        near_o[j] = swap(far_o[j], 0, 1)
    for j in groups[0][1:] + groups[3]:
        there[j] = swap_z(routes_t, j)
    tick()

    h_pieces[3] = swap(h_pieces[2], 1, 0)
    for j in z_second:
        far_w[j] = swap_z(qkv_piece, j)
    for j in z_first:
        near_w[j] = swap(far_w[j], 0, 1)
    o_all = now(place_ep(far_o, near_o)).reshape(nep, o_deep + router_deep, o_cols)
    o_part_of = nep // nctx

    def o_block(m):
        block = lax.dynamic_slice(o_all, ((at_ctx ^ m) * o_part_of, 0, 0), (o_part_of, o_deep, o_cols))
        return block.reshape(q_cols, o_cols)

    o_pieces = {0: o_block(0), 2: swap(o_block(2), 2, 0)}
    router_full = o_all[:, o_deep:].reshape(width, experts)
    token = jnp.arange(rows, dtype=jnp.int32)
    upto = (token[:, None] <= token[None, :]).astype(BF16)
    slots = jnp.arange(capacity, dtype=jnp.int32).astype(F32)

    def slot_table(hits):
        rank = mm(hits.astype(BF16), upto) - 1.0
        return ((rank[:, None, :] == slots[None, :, None]) & (hits[:, None, :] > 0)).astype(BF16)

    places = jnp.arange(np_, dtype=jnp.int32)
    plane_experts = (at_ctx ^ (places >> 1 & ~1) ^ (places & 1)) * nep + (at_ep ^ (places >> 1 & 1))
    tables = []
    for j in range(nz):
        hits = jnp.sum((now(there[j])[None] == plane_experts[:, None, None]).astype(F32), axis=1)
        tables.append(slot_table(hits).reshape(np_ * capacity, rows))
    lane_ids = jnp.arange(-(-experts // 128) * 128, dtype=jnp.int32)
    picker = jnp.sum((routes[0][:, :, None] == lane_ids).astype(F32), axis=1)

    def pick(far, q):
        return {j: [did(v) for v in select(tables[j], [now(v) for v in far[j]], nb)] for j in groups[q]}

    def fetch(v, far, q, *parts, rounds=1):
        half = width // 2
        for j in groups[q]:
            if j and len(parts) == 2:
                far[j] = [swap_z(v, j, rounds)]
            elif j:
                far.setdefault(j, []).append(swap_z(v[:, parts[0] * half : (parts[0] + 1) * half], j, rounds))

    def post(pieces, got, q, *bs, rounds=1):
        for j in groups[q]:
            for b in bs:
                got.setdefault(j, [pieces[j][0]] + [None] * (nb - 1))[b] = swap(pieces[j][b], b & ~1, b & 1, rounds)

    def share(got, q):
        half = np_ * capacity // 2 // nb
        for j in groups[q]:
            got[j].append(swap(jnp.concatenate([v[half:] for v in got[j]], axis=0), 1, 0))

    def share_back(made, q):
        for j in groups[q]:
            made[j] = [made[j][0], swap(made[j][1], 1, 0)]

    def packed(made, q):
        for j in groups[q]:
            copies[j], outs[j] = pack(now(made[j][0]), made[j][1], nb, width)
            did(copies[j][0])

    def gather(pieces, q, shares=2):
        total = {}
        for j in groups[q]:
            ready = [now(pieces[j][0]), *pieces[j][1:]]
            total[j] = combine(tables[j], ready, BF16, shares) if j else combine(tables[j], ready, F32, 1)
            for v in total[j]:
                did(v)
        return total

    def home(total, kept, part, rounds=1):
        for j, v in total.items():
            if j:
                kept.setdefault(j, [None] * len(v))[part] = swap_z(v[part], j, rounds)
            else:
                kept[j] = v

    grad_out = out_grad[0]
    far_g, got_g = {0: [grad_out]}, {}
    tick()

    for j in z_second:
        near_w[j] = swap(far_w[j], 0, 1)
    fetch(grad_out, far_g, 2, 0)
    fetch(grad_out, far_g, 0, 0, 1)
    picked_g0 = pick(far_g, 0)
    frequency = ROPE_BASE ** (-jnp.arange(HEAD_DIM // 2).astype(F32) * 2.0 / HEAD_DIM)
    angles = jnp.arange(length).astype(F32)[:, None] * frequency[None, :]
    cosine, sine = jnp.cos(angles), jnp.sin(angles)
    cos_full = jnp.concatenate([cosine, cosine], axis=1)
    sin_full = jnp.concatenate([-sine, sine], axis=1)
    q_gain_row, k_gain_row = q_gain[None, :], key_norm_gain[None, :]
    h_full = join(h_pieces, at_ctx[None])
    flat_routes = now(jnp.concatenate(there))
    plane_routes = [flat_routes] + [swap(flat_routes, b & ~1, b & 1) for b in range(1, nb)]
    tick()

    o_pieces[3] = swap(o_block(3), 3, 0)
    o_pieces[1] = swap(o_block(1), 1, 0)
    post(picked_g0, got_g, 0, 1)
    fetch(grad_out, far_g, 2, 1)
    behind = after(grad_out, far_g[groups[2][-1]][-1])
    fetch(behind, far_g, 3, 0, rounds=2)
    qkv_weight = place_ep(far_w, near_w)
    qkv = mm(h_full, now(qkv_weight))
    attn, turned_q, turned_k, lse = attend(qkv, cos_full, sin_full, q_gain_row, k_gain_row, heads)
    did(attn)
    tick()

    router_wide = jnp.pad(router_full, ((0, 0), (0, lane_ids.shape[0] - experts)))
    fetch(grad_out, far_g, 3, 1, rounds=2)
    picked_g2 = pick(far_g, 2)
    o_rows = place([o_pieces[m] for m in range(nctx)], lambda i: at_ctx ^ i, 1)
    attn = now(attn)
    held = {}
    for hi in reversed(range(0, nctx, 2)):
        sent = swap(mm(own_rows(attn, hi + 1), o_rows).astype(BF16), 1, 0)
        held[hi] = did(mm(own_rows(attn, hi), o_rows) + sent.astype(F32))
    branch_far = swap(held[2].astype(BF16), 2, 0)
    tick()

    post(picked_g0, got_g, 0, 2, 3)
    post(picked_g2, got_g, 2, 1)
    shape = jax.ShapeDtypeStruct
    resid, h_two, scale_two = by_rows(
        second_norm_kernel,
        [held[0], now(branch_far), layer_input[0], ffn_gain[None]],
        [shape((rows, width), F32), shape((rows, width), BF16), shape((rows, 1), F32)],
        "second_norm",
    )
    far_h, got_h = {0: [h_two]}, {}
    fetch(h_two, far_h, 2, 0)
    fetch(h_two, far_h, 0, 0, 1)
    picked_h = pick(far_h, 0)
    tick()

    post(picked_h, got_h, 0, 1, 2, 3)
    share(got_g, 0)
    fetch(h_two, far_h, 2, 1)
    here_routes = now(jnp.stack(plane_routes))
    all_routes = jnp.stack([here_routes, swap(here_routes, 1, 0)])
    picked_g3 = pick(far_g, 3)
    gate, up, down = gate_weight[0], up_weight[0], down_weight[0]
    results, copies, outs, joined = {}, {}, {}, None

    def expert(q):
        nonlocal joined
        for j in groups[q]:
            h_in = [now(got_h[j][0]), *got_h[j][1:]]
            results[j], joined = expert_step(
                j, nz, h_in, got_g[j], gate, up, down, router_wide, picks, marks, joined
            )
            did(results[j][0])

    tick()

    post(picked_g2, got_g, 2, 2, 3)
    post(picked_g3, got_g, 3, 1)
    fetch(h_two, far_h, 3, 0)
    share(got_h, 0)
    picked_h2 = pick(far_h, 2)
    at_device = at_ctx * nep + at_ep
    all_routes = now(all_routes).reshape(2, nb, nz, TOP, rows).transpose(3, 2, 0, 1, 4)
    all_routes = all_routes.reshape(TOP, devices, rows)
    own_id = jnp.full((1, 128), at_device, jnp.int32)
    picks = did(pick_rows(own_id, all_routes, upto, capacity, lane_ids.shape[0]))
    extra = -(-2 * experts // 128) * 128
    extra_ids = jnp.arange(extra, dtype=jnp.int32)
    marks = jnp.stack([extra_ids == at_device, extra_ids == at_device, extra_ids == at_device + experts]).astype(F32)
    lanes = lane_ids.shape[0]
    router, gates, picked_total = by_rows(
        lambda *refs: route_kernel(experts, *refs),
        [now(h_two), router_wide, picker],
        [shape((rows, lanes), F32), shape((rows, lanes), F32), shape((rows, 1), F32)],
        "route",
    )
    did(gates)
    tick()
    post(picked_h2, got_h, 2, 1, 2, 3)
    share(got_g, 2)
    fetch(h_two, far_h, 3, 1)
    expert(0)
    tick()
    post(picked_g3, got_g, 3, 2, 3)
    fetch(grad_out, far_g, 1, 0, 1)
    picked_h3 = pick(far_h, 3)
    share(got_h, 2)
    share_back(results, 0)
    tick()
    post(picked_h3, got_h, 3, 1, 2, 3)
    share(got_g, 3)
    fetch(h_two, far_h, 1, 0, 1)
    picked_g1 = pick(far_g, 1)
    expert(2)
    tick()
    post(picked_g1, got_g, 1, 1, 2, 3)
    share(got_h, 3)
    share_back(results, 2)
    picked_h1 = pick(far_h, 1)
    packed(results, 0)
    tick()
    post(picked_h1, got_h, 1, 1, 2, 3)
    share(got_g, 1)
    expert(3)
    packed(results, 2)
    back, made = {}, {}
    tick()

    post(copies, back, 2, 1, 2, 3)
    share(got_h, 1)
    share_back(results, 3)
    packed(results, 3)
    tick()
    post(copies, back, 3, 1, 2, 3)
    total_2 = gather(back, 2)
    homes = {}
    home(total_2, homes, 0)
    for j in groups[1]:
        got_h[j][0] = after(got_h[j][0], *total_2[groups[2][-1]])
    expert(1)
    tick()
    post(copies, back, 0, 1, 2, 3)
    home(total_2, homes, 1)
    total_3 = gather(back, 3, 1)
    share_back(results, 1)
    packed(results, 1)
    joined_h, joined_g, hidden_all, grad_gate_all, grad_up_all = joined
    gate_part = did(product(joined_h, now(grad_gate_all), "tn", F32, 512))
    tick()
    post(copies, back, 1, 1, 2, 3)
    home(total_3, homes, 0, 2)
    total_0 = gather(back, 0, 1)
    up_part = did(product(joined_h, now(grad_up_all), "tn", F32, 512))
    tick()

    home(gather(back, 1, 1), homes, 0)
    home(total_0, homes, 0)
    post(outs, made, 3, 1, 2, 3)
    down_part = did(product(now(hidden_all), joined_g, "tn", F32, 256))
    tick()

    whole = [homes[j][0] for j in sorted(homes) if j and len(homes[j]) == 1]
    homes = [now(homes[0][0]), *whole, *[v for j in sorted(homes) if len(homes[j]) == 2 for v in homes[j]]]
    grad_resid, low, logit_low, ffn_gain_part = by_rows(
        lambda *refs: second_back_kernel(experts, len(homes), len(whole), *refs),
        [*homes, gates, router, picker, picked_total, router_wide, resid, scale_two, ffn_gain[None], grad_out],
        [shape((rows, width), F32), shape((rows, width), BF16), shape((rows, lanes), BF16), shape((1, width), F32)],
        "second_back",
    )
    did(low)
    homes = {}
    total_3 = gather(made, 3, 1)
    home(total_3, homes, 0, 2)
    tick()
    low_pieces = [low, swap(low, 1, 0), swap(low, 2, 0), None]
    post(outs, made, 2, 1)
    post(outs, made, 1, 1)
    tick()
    low_pieces[3] = swap(low_pieces[2], 1, 0)
    post(outs, made, 2, 2, 3, rounds=2)
    post(outs, made, 1, 3, rounds=2)
    post(outs, made, 0, 1, rounds=2)
    tick()

    branch_full = now(join(low_pieces, at_ctx[None]))
    o_own = q_cols // nep
    own_width = width // devices
    o_part = product(attn, branch_full, "tn", F32, 256)
    router_part = t_mm(logit_low, h_two)[:experts].reshape(experts, nctx, nep, own_width)
    router_rows = experts * nctx * own_width // width

    def o_term(j, ry):
        place_of = at_ep ^ (2 * j + ry)
        block = lax.dynamic_slice_in_dim(o_part, place_of * o_own, o_own, 0)
        router_block = lax.dynamic_slice_in_dim(router_part, place_of, 1, 2).reshape(router_rows, width)
        return jnp.concatenate([block, router_block], axis=0)

    last_steps = list(reversed(range(nz)))
    o_sent = {j: did(o_term(j, 1).astype(BF16)) for j in last_steps}
    grad_attn = did(product(branch_full, o_rows, "nt", BF16, 512))
    for j in groups[2]:
        made[j][0] = after(made[j][0], grad_attn)
    total_2 = gather(made, 2, 1)
    home(total_2, homes, 0, 2)
    tick()

    o_near = {j: swap(o_sent[j], 0, 1) for j in last_steps[:-1]}
    post(outs, made, 1, 2)
    grad_qkv, q_gain_part, k_gain_part = attend_back(
        qkv, turned_q, turned_k, attn, lse, now(grad_attn), cos_full, sin_full, q_gain_row, k_gain_row, heads
    )
    did(grad_qkv)
    tick()

    post(outs, made, 0, 2, 3)
    total_1 = gather(made, 1, 1)
    o_near[0] = swap(o_sent[0], 0, 1)
    o_far = {}
    o_mid = {j: (o_term(j, 0) + now(o_near[j]).astype(F32)).astype(BF16) for j in last_steps[:-1]}
    for j in last_steps[: nz // 4]:
        o_far[j] = swap_z(o_mid[j], j)
    qkv_part = product(h_full, now(grad_qkv), "tn", F32, 512).reshape(nctx, nep, own_width, -1)

    def qkv_term(j, ry):
        return lax.dynamic_slice_in_dim(qkv_part, at_ep ^ (2 * j + ry), 1, 1)[:, 0]

    qkv_sent = {j: did(qkv_term(j, 1).astype(BF16)) for j in last_steps}
    one_term = lambda m, plus, dtype: product(
        own_rows(grad_qkv, m), qkv_weight, "nt", dtype, 1024, plus
    )
    sent = [did(one_term(m, None, BF16)) for m in (3, 1)]
    tick()

    first_steps, other_steps = last_steps[::2], last_steps[1::2]
    qkv_near = {j: swap(qkv_sent[j], 0, 1) for j in first_steps}
    sent = [swap(v, 1, 0) for v in sent]
    for j in last_steps[nz // 4 : -2]:
        o_far[j] = swap_z(o_mid[j], j)
    home(total_1, homes, 0)
    total_0 = gather(made, 0, 1)
    held = [did(one_term(0, sent[1], F32)), did(one_term(2, sent[0], BF16))]
    tick()

    qkv_near.update({j: swap(qkv_sent[j], 0, 1) for j in other_steps})
    one_far = swap(held[1], 2, 0)
    qkv_mid = lambda j: (qkv_term(j, 0) + now(qkv_near[j]).astype(F32)).astype(BF16)
    qkv_far = {j: swap_z(qkv_mid(j), j) for j in last_steps[: nz // 4]}
    o_far[1] = swap_z(o_mid[1], 1)
    input_grad, attn_gain_part = by_rows(
        first_back_kernel,
        [held[0], one_far, layer_input[0], scale_one, attn_gain[None], grad_resid],
        [shape((rows, width), F32), shape((1, width), F32)],
        "first_back",
    )
    did(input_grad)
    tick()

    qkv_far.update({j: swap_z(qkv_mid(j), j) for j in last_steps[nz // 4 : -1]})
    home(total_0, homes, 0)
    o_sum = o_term(0, 0) + o_near[0].astype(F32)
    for j in range(1, nz):
        o_sum = o_sum + now(o_far[j]).astype(F32)
    o_grad = did(o_sum[:o_own])
    router_sum = did(o_sum[o_own:].reshape(experts, nctx, own_width).transpose(1, 2, 0))
    late = jnp.concatenate([now(attn_gain_part)[0], ffn_gain_part[0], q_gain_part[0], k_gain_part[0]])
    late = did(sum_over(late, [(1 << b, 0) for b in range(nctx.bit_length() - 1)] + [(0, 1)]))
    tick()

    qkv_sum = qkv_term(0, 0) + qkv_near[0].astype(F32)
    for j in range(1, nz):
        qkv_sum = qkv_sum + now(qkv_far[j]).astype(F32)
    last = jnp.concatenate([qkv_sum, router_sum], axis=2).astype(BF16)
    last_block = lambda m: lax.dynamic_index_in_dim(last, at_ctx ^ m, 0)
    last = place([swap(last_block(m), m, 0) for m in range(nctx)], lambda i: at_ctx ^ i).astype(F32)
    late = sum_over(now(late), [(0, 2 << b) for b in range(nz.bit_length() - 1)])
    qkv_grad = last
    router_grad = jnp.sum(last[:, :, q_cols + 2 * HEAD_DIM :], axis=0)
    mixed = resid
    for j in sorted(homes):
        mixed = mixed + jnp.concatenate(homes[j]).astype(F32)

    def columns(first, last):
        return jnp.concatenate([qkv_grad[c, :, first:last] for c in range(nctx)], axis=1)

    return (
        mixed.astype(BF16)[None],
        input_grad[None],
        late[:width],
        columns(0, q_cols),
        columns(q_cols, q_cols + HEAD_DIM),
        columns(q_cols + HEAD_DIM, q_cols + 2 * HEAD_DIM),
        o_grad,
        late[2 * width : 2 * width + HEAD_DIM],
        late[2 * width + HEAD_DIM :],
        late[width : 2 * width],
        router_grad,
        gate_part[None],
        up_part[None],
        down_part[None],
    )


def solution(mesh):
    nctx, nep = mesh.shape["ctx"], mesh.shape["ep"]
    tokens = P("ep", "ctx", None)
    own = P(("ctx", "ep"), None)
    expert = P(("ctx", "ep"), None, None)
    split_rows = P("ep", None)

    def on_device(*arrays):
        return layer(nctx, nep, *arrays)

    return jax.shard_map(
        on_device,
        mesh=mesh,
        in_specs=(
            tokens, P(), split_rows, split_rows, split_rows, split_rows, P(), P(), P(), split_rows,
            expert, expert, expert, tokens, tokens,
        ),
        out_specs=(
            tokens, tokens, P(), own, own, own, own, P(), P(), P(), own, expert, expert, expert,
        ),
        check_vma=False,
    )
```
